32 devices in a mesh: dp: 16 (over z, y, x), mp: 2 (over core).
Axes of the slice: x: 2, y: 2, z: 4, core: 2. Of those that a mesh axis runs over, the one named last changes fastest.
Arguments:
- tokens: bfloat16 [32768, 1472], P('dp', 'mp'), may hold values from -6 to 6
- cotangent: bfloat16 [32768, 1472], P('dp', 'mp'), may hold values from -6 to 6
- lengths: int32 [32], P('dp'), may hold values from 512 to 1024, as said below
- keep_mask: int32 [32768], P('dp'), may hold values from 0 to 1, as said below
- ln_attn: float32 [1472], replicated, may hold values from 0.1 to 1.9
- w_query: bfloat16 [1472, 384], P(None, 'mp'), may hold values from -0.15625 to 0.15625
- w_key: bfloat16 [1472, 384], P(None, 'mp'), may hold values from -0.15625 to 0.15625
- w_value: bfloat16 [1472, 384], P(None, 'mp'), may hold values from -0.15625 to 0.15625
- w_attn_out: bfloat16 [384, 1472], P('mp'), may hold values from -1.75 to 1.75
- rel_table: float32 [32, 6], P(None, 'mp'), may hold values from -4 to 4
- w_delete: bfloat16 [1472], replicated, may hold values from -0.15625 to 0.15625
- ln_ffn: float32 [1472], replicated, may hold values from 0.1 to 1.9
- w_gate: bfloat16 [1472, 3584], P(None, 'mp'), may hold values from -0.15625 to 0.15625
- w_up: bfloat16 [1472, 3584], P(None, 'mp'), may hold values from -0.15625 to 0.15625
- w_ffn_out: bfloat16 [3584, 1472], P('mp'), may hold values from -0.09375 to 0.09375
Outputs:
- mixed: bfloat16 [32768, 1472], P('dp', 'mp')
- grad_tokens: bfloat16 [32768, 1472], P('dp', 'mp')
- grad_ln_attn: float32 [1472], P('mp')
- grad_w_query: float32 [1472, 384], P(None, 'mp')
- grad_w_key: float32 [1472, 384], P(None, 'mp')
- grad_w_value: float32 [1472, 384], P(None, 'mp')
- grad_w_attn_out: float32 [384, 1472], P('mp')
- grad_rel_table: float32 [32, 6], P(None, 'mp')
- grad_w_delete: float32 [1472], replicated
- grad_ln_ffn: float32 [1472], P('mp')
- grad_w_gate: float32 [1472, 3584], P(None, ('mp', 'dp'))
- grad_w_up: float32 [1472, 3584], P(None, ('mp', 'dp'))
- grad_w_ffn_out: float32 [3584, 1472], P(('mp', 'dp'))
The draws below stay inside these ranges and needn't reach their ends.
Inputs may be any that keep to these rules, and one draw needn't show every extreme that they name: `lengths`: on one index of dp every item has length 1024. `keep_mask`: zero on every padding row; exactly 16384 ones in all; on one index of dp every one of its 2048 rows is kept.
All inputs are finite; a program needn't handle non-finite values.
Results may differ from the reference program's by a relative error of at most 0.015.
Values may be sent and summed in bfloat16 or wider, within the bound.
A program may use at most 448 MiB of HBM per device.

```python
import jax
import jax.numpy as jnp
import numpy as np
from jax import lax

D = 1472
HEADS = 6
HDIM = 64
FF = 3584
BUCKETS = 32
LMAX = 1024
ITEMS_DEV = 2
LMIN = 512
ROWS_DEV = 2048
TOKENS = 32768
TOTAL_KEPT = 16384
N_DP = 16


def packing(key):
    key_len, key_full, key_level, key_score = jax.random.split(key, 4)
    item_len = jax.random.randint(key_len, (N_DP, ITEMS_DEV), LMIN, LMAX + 1).astype(jnp.int32)
    chosen = jax.random.randint(key_full, (), 0, N_DP)
    device_ids = jnp.arange(N_DP, dtype=jnp.int32)
    item_len = jnp.where(device_ids[:, None] == chosen, LMAX, item_len)
    real_rows = jnp.sum(item_len, axis=1)
    row_ids = jnp.arange(ROWS_DEV, dtype=jnp.int32)
    real_row = row_ids[None, :] < real_rows[:, None]
    level = jax.random.randint(key_level, (N_DP, 1), 0, 4) * 75
    noise = jax.random.randint(key_score, (N_DP, ROWS_DEV), 0, 256)
    base = jnp.where(device_ids[:, None] == chosen, 511, noise + level)
    flat_index = jnp.arange(TOKENS, dtype=jnp.int32).reshape(N_DP, ROWS_DEV)
    priority = jnp.where(real_row, base * TOKENS + flat_index, -1).astype(jnp.int32)
    picked = lax.top_k(priority.reshape(-1), TOTAL_KEPT)[1]
    keep_flags = jnp.zeros((TOKENS,), jnp.int32).at[picked].set(1)
    return (item_len.reshape(-1), keep_flags)


def draw_lengths(key, part):
    return packing(key)[0]


def draw_keep_mask(key, part):
    return packing(key)[1]


def steps_of(rng, extent, pieces, smallest, top_value):
    def one(dim, shards_of):
        steps = jax.random.uniform(jax.random.fold_in(jax.random.fold_in(rng, 6), dim), (shards_of,), jnp.float32, smallest / len(pieces), top_value / len(pieces))
        return jnp.repeat(jnp.exp(steps), extent[dim] // shards_of).reshape((-1,) + (1,) * (len(extent) - dim - 1))

    gain = one(*pieces[0])
    for cut in pieces[1:]:
        gain = gain * one(*cut)
    return gain


def gaussian(own_key, dims, deviation, reach, pieces=(), kind=jnp.bfloat16):
    entries = jax.random.normal(own_key, dims, jnp.float32) * deviation
    if len(pieces) > 0:
        entries = steps_of(own_key, dims, pieces, -0.22, 0.18) * entries
    return jnp.clip(entries, min=-reach, max=reach).astype(kind)


def setup_inputs(seed: int = 0) -> dict:
    splits = jax.random.split(jax.random.key(seed), 16)
    tokens = gaussian(splits[0], (TOKENS, D), 1.0, 6.0, ((0, 16), (1, 2)))
    cotangent = gaussian(splits[1], (TOKENS, D), 1.0, 6.0, ((0, 16), (1, 2)))
    lengths = draw_lengths(jax.random.fold_in(splits[15], 71), 0)
    keep_mask = draw_keep_mask(jax.random.fold_in(splits[15], 71), 0)
    ln_attn = jnp.clip(1.0 + 0.18 * jax.random.normal(splits[4], (D,), jnp.float32), 0.1, 1.9)
    w_query = gaussian(splits[5], (D, HEADS * HDIM), D ** -0.5, 0.15625, ((1, 2),))
    w_key = gaussian(splits[6], (D, HEADS * HDIM), D ** -0.5, 0.15625, ((1, 2),))
    w_value = gaussian(splits[7], (D, HEADS * HDIM), D ** -0.5, 0.15625, ((1, 2),))
    w_attn_out = gaussian(splits[8], (HEADS * HDIM, D), (HEADS * HDIM // 32) ** -0.5, 1.75, ((0, 2),))
    rel_table = gaussian(splits[9], (BUCKETS, HEADS), 1.0, 4.0, ((1, 2),), jnp.float32)
    w_delete = gaussian(splits[10], (D,), D ** -0.5, 0.15625)
    ln_ffn = jnp.clip(1.0 + 0.18 * jax.random.normal(splits[11], (D,), jnp.float32), 0.1, 1.9)
    w_gate = gaussian(splits[12], (D, FF), D ** -0.5, 0.15625, ((1, 2),))
    w_up = gaussian(splits[13], (D, FF), D ** -0.5, 0.15625, ((1, 2),))
    w_ffn_out = gaussian(splits[14], (FF, D), FF ** -0.5, 0.09375, ((0, 2),))
    return dict(tokens=tokens, cotangent=cotangent, lengths=lengths, keep_mask=keep_mask, ln_attn=ln_attn, w_query=w_query, w_key=w_key, w_value=w_value, w_attn_out=w_attn_out, rel_table=rel_table, w_delete=w_delete, ln_ffn=ln_ffn, w_gate=w_gate, w_up=w_up, w_ffn_out=w_ffn_out)


EPSILON = 1e-06
DELETE_DEPTH = 4.0
NEG_LARGE = -1e+30
HIGHEST_PREC = lax.Precision.HIGHEST
THRESHOLDS = np.array([8, 12, 16, 23, 32, 46, 64, 91], np.int32)

@jax.custom_vjp
def low(v):
    return lax.optimization_barrier(v.astype(jnp.bfloat16)).astype(jnp.float32)

@jax.custom_vjp
def low_back(v):
    return v

def low_keep(v):
    return (low(v), None)

def low_pass(kept, grad):
    return (grad,)

def back_keep(v):
    return (v, None)

def back_low(kept, grad):
    return (low(grad),)
low.defvjp(low_keep, low_pass)
low_back.defvjp(back_keep, back_low)

def bucket_of(relative):
    distance = jnp.abs(relative)
    far_bucket = 7 + lax.optimization_barrier(jnp.sum((distance[..., None] >= THRESHOLDS).astype(jnp.int32), axis=-1))
    near_bucket = jnp.where(distance < 8, distance, far_bucket)
    return (near_bucket + 16 * (relative > 0).astype(jnp.int32)).astype(jnp.int32)

def rms_norm(values, gain_vec):
    factor = lax.rsqrt(lax.optimization_barrier(jnp.mean(values * values, axis=-1, keepdims=True)) + EPSILON)
    return values * factor * gain_vec

def forward(kept_state, ln_attn, w_query, w_key, w_value, w_attn_out, rel_table, w_delete, ln_ffn, w_gate, w_up, w_ffn_out, item_ids, rel_bucket):
    normed_one = low(rms_norm(kept_state, ln_attn))
    del_logit = jnp.dot(normed_one, w_delete, precision=HIGHEST_PREC)
    del_gate = low(-DELETE_DEPTH * jax.nn.sigmoid(-del_logit))
    queries = low_back(low(jnp.dot(normed_one, w_query, precision=HIGHEST_PREC)))
    key_rows = low_back(low(jnp.dot(normed_one, w_key, precision=HIGHEST_PREC)))
    val_rows = low_back(low(jnp.dot(normed_one, w_value, precision=HIGHEST_PREC)))
    head_count = w_query.shape[1] // HDIM
    margin = ((LMAX, LMAX), (0, 0))
    key_ext = jnp.pad(key_rows, margin)
    val_ext = jnp.pad(val_rows, margin)
    gate_ext = jnp.pad(del_gate, (LMAX, LMAX))
    item_ext = jnp.pad(item_ids, (LMAX, LMAX), constant_values=-1)
    rel_bias = jnp.transpose(jnp.take(rel_table, rel_bucket, axis=0), (2, 0, 1))
    score_scale = HDIM ** (-0.5)

    def attend_block(block_index):
        start = block_index * LMAX
        q_block = lax.dynamic_slice_in_dim(queries, start, LMAX, 0).reshape(LMAX, head_count, HDIM)
        k_block = lax.dynamic_slice_in_dim(key_ext, start, 3 * LMAX, 0).reshape(3 * LMAX, head_count, HDIM)
        v_block = lax.dynamic_slice_in_dim(val_ext, start, 3 * LMAX, 0).reshape(3 * LMAX, head_count, HDIM)
        g_block = lax.dynamic_slice_in_dim(gate_ext, start, 3 * LMAX, 0)
        own_items = lax.dynamic_slice_in_dim(item_ids, start, LMAX, 0)
        ext_items = lax.dynamic_slice_in_dim(item_ext, start, 3 * LMAX, 0)
        scores = jnp.einsum('qhd,khd->hqk', q_block, k_block, precision=HIGHEST_PREC) * score_scale + rel_bias + g_block[None, None, :]
        scores = low_back(scores)
        same_item = own_items[:, None] == ext_items[None, :]
        scores = jnp.where(same_item[None], scores, NEG_LARGE)
        row_max = lax.optimization_barrier(jnp.max(scores, axis=2, keepdims=True))
        exp_scores = jnp.exp(scores - row_max)
        attn_prob = low(exp_scores / lax.optimization_barrier(jnp.sum(exp_scores, axis=2, keepdims=True)))
        merged = jnp.einsum('hqk,khd->qhd', attn_prob, v_block, precision=HIGHEST_PREC)
        return merged.reshape(LMAX, head_count * HDIM)
    block_count = kept_state.shape[0] // LMAX
    attended = lax.map(jax.checkpoint(attend_block), jnp.arange(block_count, dtype=jnp.int32))
    attended = low_back(low(attended.reshape(kept_state.shape[0], head_count * HDIM)))
    attn_out = low_back(jnp.dot(attended, w_attn_out, precision=HIGHEST_PREC))
    mid_state = kept_state + attn_out
    normed_two = low(rms_norm(mid_state, ln_ffn))
    gate_pre = low_back(jnp.dot(normed_two, w_gate, precision=HIGHEST_PREC))
    up_pre = low_back(jnp.dot(normed_two, w_up, precision=HIGHEST_PREC))
    hidden = low(jax.nn.gelu(gate_pre, approximate=True) * up_pre)
    return mid_state + low_back(jnp.dot(hidden, w_ffn_out, precision=HIGHEST_PREC))

def reference(tokens, cotangent, lengths, keep_mask, ln_attn, w_query, w_key, w_value, w_attn_out, rel_table, w_delete, ln_ffn, w_gate, w_up, w_ffn_out):
    item_len = lengths.reshape(N_DP, ITEMS_DEV)
    item_end = jnp.cumsum(item_len, axis=1)
    row_ids = jnp.arange(ROWS_DEV, dtype=jnp.int32)
    local_item = lax.optimization_barrier(jnp.sum((row_ids[None, :, None] >= item_end[:, None, :]).astype(jnp.int32), axis=2))
    device_ids = jnp.arange(N_DP, dtype=jnp.int32)
    item_of_row = (device_ids[:, None] * ITEMS_DEV + local_item).reshape(TOKENS).astype(jnp.int32)
    kept_rows = jnp.nonzero(keep_mask > 0, size=TOTAL_KEPT)[0].astype(jnp.int32)
    item_ids = item_of_row[kept_rows]
    relative = jnp.arange(3 * LMAX, dtype=jnp.int32)[None, :] - LMAX - jnp.arange(LMAX, dtype=jnp.int32)[:, None]
    rel_bucket = bucket_of(relative)
    kept_state = tokens[kept_rows].astype(jnp.float32)
    kept_cot = cotangent[kept_rows].astype(jnp.float32)
    params = tuple((weight_in.astype(jnp.float32) for weight_in in (ln_attn, w_query, w_key, w_value, w_attn_out, rel_table, w_delete, ln_ffn, w_gate, w_up, w_ffn_out)))

    def layer(state_in, *weights):
        return forward(state_in, *weights, item_ids, rel_bucket)
    mixed_kept, pull_back = jax.vjp(layer, kept_state, *params)
    grads = pull_back(kept_cot)
    mixed = jnp.zeros((TOKENS, D), jnp.float32).at[kept_rows].set(mixed_kept).astype(jnp.bfloat16)
    grad_tokens = jnp.zeros((TOKENS, D), jnp.float32).at[kept_rows].set(grads[0]).astype(jnp.bfloat16)
    return (mixed, grad_tokens, grads[1], grads[2], grads[3], grads[4], grads[5], grads[6], grads[7], grads[8], grads[9], grads[10], grads[11])
```

```python
import functools

import jax
import jax.numpy as jnp
import numpy as np
from jax import lax
from jax.experimental import pallas as pl
from jax.experimental.pallas import tpu as pltpu
from jax.sharding import PartitionSpec as P

D = 1472
HDIM = 64
BUCKETS = 32
LMAX = 1024
ROWS_DEV = 2048

EPSILON = 1e-06
DELETE_DEPTH = 4.0
NEG_LARGE = -1e30
NEAR_STEPS = (1, 2, 3, 4, 5, 6, 7, 8, 12, 16, 23, 32, 46, 64, 91)
TILE = 128
QBLOCK = 256
AUG = 16
F32 = jnp.float32
BF16 = jnp.bfloat16
GELU_C = float(np.sqrt(2.0 / np.pi))

NN = (((1,), (0,)), ((), ()))
TN = (((0,), (0,)), ((), ()))
NT = (((1,), (1,)), ((), ()))


def dot(a, b, dims):
    return lax.dot_general(a, b, dims, preferred_element_type=F32)


def call(kernel, name, flops, nbytes, **kw):
    return pl.pallas_call(
        kernel,
        name=name,
        cost_estimate=pl.CostEstimate(
            flops=int(flops), bytes_accessed=int(nbytes), transcendentals=0
        ),
        compiler_params=pltpu.CompilerParams(vmem_limit_bytes=56 << 20),
        **kw,
    )


VMEM = pl.BlockSpec(memory_space=pltpu.VMEM)
SMEM = pl.BlockSpec(memory_space=pltpu.SMEM)


def compact_kernel(part_ref, slot_ref, x_ref, own_ref, peer_ref):
    part = part_ref[0]
    for which, out_ref in ((0, own_ref), (1, peer_ref)):
        item = part if which == 0 else 1 - part
        for block in range(LMAX // QBLOCK):
            width = ROWS_DEV - 512 - block * QBLOCK
            start = pl.multiple_of(item * 512 + block * QBLOCK, 128)
            ids = item * LMAX + block * QBLOCK + lax.broadcasted_iota(jnp.int32, (QBLOCK, 1), 0)
            hot = (slot_ref[:, pl.ds(start, width)] == ids).astype(F32).astype(BF16)
            rows = dot(x_ref[:, pl.ds(start, width)], hot, NT)
            out_ref[:, block * QBLOCK : (block + 1) * QBLOCK] = rows.astype(BF16)


def compact(part, slot, columns):
    width = columns.shape[0]
    shape = jax.ShapeDtypeStruct((width, LMAX), BF16)
    return call(
        compact_kernel,
        "compact",
        2 * width * 2 * 4608 * 256,
        width * 2048 * 4,
        in_specs=[SMEM, VMEM, VMEM],
        out_specs=[VMEM, VMEM],
        out_shape=[shape, shape],
    )(part, slot, columns)


def spread_kernel(part_ref, slot_ref, own_ref, peer_ref, out_ref):
    first = part_ref[0] == 0
    items = (
        jnp.where(first, own_ref[...], peer_ref[...]),
        jnp.where(first, peer_ref[...], own_ref[...]),
    )
    for block in range(ROWS_DEV // QBLOCK):
        end = (block + 1) * QBLOCK
        slots = slot_ref[:, end - QBLOCK : end]
        total = None
        for item in range(2):
            reach = min(end - 512 * item, LMAX)
            if reach <= 0 or (item == 0 and end > LMAX):
                continue
            ids = item * LMAX + lax.broadcasted_iota(jnp.int32, (reach, 1), 0)
            hot = (slots == ids).astype(F32).astype(BF16)
            part = dot(items[item][:, :reach], hot, NN)
            total = part if total is None else total + part
        out_ref[:, end - QBLOCK : end] = total.astype(BF16)


def spread(part, slot, own, peer):
    width = own.shape[0]
    return call(
        spread_kernel,
        "spread",
        2 * width * 7168 * 256,
        width * 2048 * 4,
        in_specs=[SMEM, VMEM, VMEM, VMEM],
        out_specs=VMEM,
        out_shape=jax.ShapeDtypeStruct((width, ROWS_DEV), BF16),
    )(part, slot, own, peer)


STRIP = LMAX + LMAX - TILE


def offsets(shift):
    keys = lax.broadcasted_iota(jnp.int32, (TILE, TILE), 0)
    queries = lax.broadcasted_iota(jnp.int32, (TILE, TILE), 1)
    return shift * TILE + keys - queries


def strip_kernel(table_ref, strip_ref):
    head = pl.program_id(0)
    middle = LMAX - TILE

    def value(bucket):
        return table_ref[bucket, head]

    def side(distance, base, start):
        tile = jnp.full((TILE, TILE), start, F32)
        for count, step in enumerate(NEAR_STEPS):
            tile = jnp.where(distance >= step, value(base + count + 1), tile)
        return tile

    strip_ref[0, : middle - TILE, :] = jnp.full((middle - TILE, TILE), value(15), F32)
    strip_ref[0, middle + 2 * TILE :, :] = jnp.full((STRIP - middle - 2 * TILE, TILE), value(31), F32)
    before = offsets(-1)
    strip_ref[0, middle - TILE : middle, :] = side(-before, 0, value(0))
    relative = offsets(0)
    strip_ref[0, middle : middle + TILE, :] = jnp.where(
        relative > 0, side(relative, 16, value(0)), side(-relative, 0, value(0))
    )
    after = offsets(1)
    strip_ref[0, middle + TILE : middle + 2 * TILE, :] = side(after, 16, value(0))


def bias_strip(table, heads):
    return call(
        strip_kernel,
        "bias_strip",
        heads * 3e6,
        heads * STRIP * TILE * 4,
        grid=(heads,),
        in_specs=[SMEM],
        out_specs=pl.BlockSpec((1, STRIP, TILE), lambda h: (h, 0, 0)),
        out_shape=jax.ShapeDtypeStruct((heads, STRIP, TILE), F32),
    )(table)


def attend_kernel(q_ref, k_ref, v_ref, gate_ref, strip_ref, prob_ref, out_ref):
    ones = (lax.broadcasted_iota(jnp.int32, (AUG, LMAX), 0) == 0).astype(F32).astype(BF16)
    scale = HDIM ** (-0.5)
    queries = jnp.concatenate([(q_ref[...].astype(F32) * scale).astype(BF16), ones], axis=0)
    keys = jnp.concatenate([k_ref[...], gate_ref[...]], axis=0)
    for block in range(LMAX // QBLOCK):
        low = block * QBLOCK
        scores = dot(keys, queries[:, low : low + QBLOCK], TN)
        bias = []
        for sub in range(QBLOCK // TILE):
            start = LMAX - TILE - (low + sub * TILE)
            bias.append(strip_ref[0, start : start + LMAX, :])
        scores = scores + jnp.concatenate(bias, axis=1)
        top = jnp.max(scores, axis=0, keepdims=True)
        weights = jnp.exp(scores - top)
        total = jnp.sum(weights, axis=0, keepdims=True)
        prob = (weights * (1.0 / total)).astype(BF16)
        prob_ref[0, :, low : low + QBLOCK] = prob
        out_ref[:, low : low + QBLOCK] = dot(v_ref[...], prob, NN).astype(BF16)


def attend(qkv, gate, strip, heads):
    return call(
        attend_kernel,
        "attend",
        heads * 4 * LMAX * LMAX * HDIM * 4,
        heads * LMAX * LMAX * 2,
        grid=(heads,),
        in_specs=[
            pl.BlockSpec((HDIM, LMAX), lambda h: (h, 0)),
            pl.BlockSpec((HDIM, LMAX), lambda h: (heads + h, 0)),
            pl.BlockSpec((HDIM, LMAX), lambda h: (2 * heads + h, 0)),
            pl.BlockSpec((AUG, LMAX), lambda h: (0, 0)),
            pl.BlockSpec((1, STRIP, TILE), lambda h: (h, 0, 0)),
        ],
        out_specs=[
            pl.BlockSpec((1, LMAX, LMAX), lambda h: (h, 0, 0)),
            pl.BlockSpec((HDIM, LMAX), lambda h: (h, 0)),
        ],
        out_shape=[
            jax.ShapeDtypeStruct((heads, LMAX, LMAX), BF16),
            jax.ShapeDtypeStruct((heads * HDIM, LMAX), BF16),
        ],
    )(qkv, qkv, qkv, gate, strip)


def attend_back_kernel(
    q_ref, k_ref, v_ref, prob_ref, go_ref, gq_ref, gk_ref, gv_ref, sums_ref, near_ref
):
    scale = HDIM ** (-0.5)
    blocks = LMAX // TILE
    member = (
        lax.broadcasted_iota(jnp.int32, (AUG, LMAX), 0)
        == lax.broadcasted_iota(jnp.int32, (AUG, LMAX), 1) // TILE
    )
    queries = jnp.concatenate([q_ref[...], member.astype(F32).astype(BF16)], axis=0)
    near = [jnp.zeros((TILE, TILE), F32) for _ in range(3)]
    key_total = jnp.zeros((HDIM + AUG, LMAX), F32)
    val_total = jnp.zeros((HDIM, LMAX), F32)
    for block in range(LMAX // QBLOCK):
        low = block * QBLOCK
        prob = prob_ref[0, :, low : low + QBLOCK]
        grad_out = go_ref[:, low : low + QBLOCK]
        soft = prob.astype(F32)
        grad_prob = dot(v_ref[...], grad_out, TN)
        inner = jnp.sum(soft * grad_prob, axis=0, keepdims=True)
        grad_scores = (soft * (grad_prob - inner)).astype(BF16)
        gq_ref[:, low : low + QBLOCK] = (dot(k_ref[...], grad_scores, NN) * scale).astype(BF16)
        key_total = key_total + dot(queries[:, low : low + QBLOCK], grad_scores, NT)
        val_total = val_total + dot(grad_out, prob, NT)
        for sub in range(QBLOCK // TILE):
            place = block * (QBLOCK // TILE) + sub
            for shift in (-1, 0, 1):
                at = place + shift
                if 0 <= at < blocks:
                    piece = grad_scores[at * TILE : (at + 1) * TILE, sub * TILE : (sub + 1) * TILE]
                    near[shift + 1] = near[shift + 1] + piece.astype(F32)
    gk_ref[...] = (key_total[:HDIM] * scale).astype(BF16)
    gv_ref[...] = val_total.astype(BF16)
    sums_ref[0] = key_total[HDIM : HDIM + blocks]

    def fold(tile):
        return jnp.sum(tile.reshape(TILE // 8, 8, TILE), axis=0)

    before, same, after = near
    for sign, base, other, shift in ((-1, 0, before, -1), (1, 16, after, 1)):
        near_offset = sign * offsets(0)
        far_offset = sign * offsets(shift)
        floor = 0 if sign < 0 else 1
        last = fold(jnp.where(near_offset >= floor, same, 0.0)) + fold(
            jnp.where(far_offset >= floor, other, 0.0)
        )
        for count, step in enumerate(NEAR_STEPS):
            following = fold(jnp.where(near_offset >= step, same, 0.0)) + fold(
                jnp.where(far_offset >= step, other, 0.0)
            )
            near_ref[0, base + count] = last - following
            last = following
        near_ref[0, base + 15] = last


def attend_back(qkv, prob, grad_attended, heads):
    blocks = LMAX // TILE
    rows = jax.ShapeDtypeStruct((heads * HDIM, LMAX), BF16)
    spec = pl.BlockSpec((HDIM, LMAX), lambda h: (h, 0))
    return call(
        attend_back_kernel,
        "attend_back",
        heads * 8 * LMAX * LMAX * HDIM * 4,
        heads * LMAX * LMAX * 2,
        grid=(heads,),
        in_specs=[
            spec,
            pl.BlockSpec((HDIM, LMAX), lambda h: (heads + h, 0)),
            pl.BlockSpec((HDIM, LMAX), lambda h: (2 * heads + h, 0)),
            pl.BlockSpec((1, LMAX, LMAX), lambda h: (h, 0, 0)),
            spec,
        ],
        out_specs=[
            spec,
            spec,
            spec,
            pl.BlockSpec((1, blocks, LMAX), lambda h: (h, 0, 0)),
            pl.BlockSpec((1, BUCKETS, 8, TILE), lambda h: (h, 0, 0, 0)),
        ],
        out_shape=[
            rows,
            rows,
            rows,
            jax.ShapeDtypeStruct((heads, blocks, LMAX), F32),
            jax.ShapeDtypeStruct((heads, BUCKETS, 8, TILE), F32),
        ],
    )(qkv, qkv, qkv, prob, grad_attended)


def ffn_kernel(gate_ref, up_ref, down_ref, x_ref, cot_ref, hid_ref, gg_ref, gu_ref):
    gate = dot(gate_ref[...], x_ref[...], TN)
    up = dot(up_ref[...], x_ref[...], TN)
    grad = dot(down_ref[...], cot_ref[...], TN)
    square = gate * gate
    bend = jnp.tanh(GELU_C * gate * (1.0 + 0.044715 * square))
    half = 0.5 * (1.0 + bend)
    gelu = gate * half
    slope = half + 0.5 * gate * (1.0 - bend * bend) * (GELU_C * (1.0 + 3 * 0.044715 * square))
    hid_ref[...] = (gelu * up).astype(BF16)
    gg_ref[...] = (grad * up * slope).astype(BF16)
    gu_ref[...] = (grad * gelu).astype(BF16)


def ffn(w_gate, w_up, w_down_t, normed, cot):
    units = w_gate.shape[1]
    width = 256
    weight = pl.BlockSpec((D, width), lambda i: (0, i))
    whole = pl.BlockSpec((D, LMAX), lambda i: (0, 0))
    out = pl.BlockSpec((width, LMAX), lambda i: (i, 0))
    shape = jax.ShapeDtypeStruct((units, LMAX), BF16)
    return call(
        ffn_kernel,
        "ffn",
        6 * D * units * LMAX,
        3 * D * units * 2 + 2 * D * LMAX * 2 + 3 * units * LMAX * 2,
        grid=(units // width,),
        in_specs=[weight, weight, weight, whole, whole],
        out_specs=[out, out, out],
        out_shape=[shape, shape, shape],
    )(w_gate, w_up, w_down_t, normed, cot)


def weight_grad_kernel(a_own, a_peer, b_own, b_peer, out_ref):
    total = dot(a_own[...], b_own[...], NT) + dot(a_peer[...], b_peer[...], NT)
    out_ref[...] = total.astype(BF16)


def weight_grad(a_own, a_peer, b_own, b_peer):
    units = a_own.shape[0]
    width = 256
    left = pl.BlockSpec((width, LMAX), lambda i: (i, 0))
    whole = pl.BlockSpec((D, LMAX), lambda i: (0, 0))
    return call(
        weight_grad_kernel,
        "weight_grad",
        4 * D * units * LMAX,
        4 * D * LMAX + 4 * units * LMAX + 2 * units * D,
        grid=(units // width,),
        in_specs=[left, left, whole, whole],
        out_specs=pl.BlockSpec((width, D), lambda i: (i, 0)),
        out_shape=jax.ShapeDtypeStruct((units, D), BF16),
    )(a_own, a_peer, b_own, b_peer)


def project_kernel(count, *refs):
    total = dot(refs[0][...], refs[count][...], NN)
    for i in range(1, count):
        total = total + dot(refs[i][...], refs[count + i][...], NN)
    refs[-1][...] = total.astype(refs[-1].dtype)


def project(weights, values, dtype):
    count = len(weights)
    units = weights[0].shape[1]
    width = D // 4
    weight = pl.BlockSpec((width, units), lambda i: (i, 0))
    whole = pl.BlockSpec((units, LMAX), lambda i: (0, 0))
    return call(
        functools.partial(project_kernel, count),
        "project",
        2 * count * D * units * LMAX,
        2 * count * (D * units + units * LMAX) + 4 * D * LMAX,
        grid=(D // width,),
        in_specs=[weight] * count + [whole] * count,
        out_specs=pl.BlockSpec((width, LMAX), lambda i: (i, 0)),
        out_shape=jax.ShapeDtypeStruct((D, LMAX), dtype),
    )(*weights, *values)


def halve(values, order):
    size = lax.axis_size("dp")
    bits = size.bit_length() - 1
    index = lax.axis_index("dp")
    rows = values.shape[0] // size
    values = values.reshape((2,) * bits + (rows, values.shape[1]))
    left = list(range(bits - 1, -1, -1))
    for step, bit in enumerate(order):
        axis = left.index(bit)
        left.pop(axis)
        mine = (index >> bit) & 1
        keep = lax.dynamic_index_in_dim(values, mine, axis, keepdims=False)
        give = lax.dynamic_index_in_dim(values, 1 - mine, axis, keepdims=False)
        came = lax.ppermute(give, "dp", [(i, i ^ (1 << bit)) for i in range(size)])
        total = keep.astype(F32) + came.astype(F32)
        values = total if step == bits - 1 else total.astype(BF16)
    return values


def regather(values, order):
    size = lax.axis_size("dp")
    bits = size.bit_length() - 1
    index = lax.axis_index("dp")
    rows, width = values.shape
    have = []
    for bit in order[::-1]:
        came = lax.ppermute(values, "dp", [(i, i ^ (1 << bit)) for i in range(size)])
        axis = sum(1 for b in have if b > bit)
        have.append(bit)
        mine = (index >> bit) & 1
        values = jnp.where(
            mine == 0, jnp.stack([values, came], axis), jnp.stack([came, values], axis)
        )
    return values.reshape(size * rows, width)


def swap(values):
    return lax.ppermute(values, "mp", [(0, 1), (1, 0)])


def body(
    tokens,
    cotangent,
    lengths,
    keep_mask,
    ln_attn,
    w_query,
    w_key,
    w_value,
    w_attn_out,
    rel_table,
    w_delete,
    ln_ffn,
    w_gate,
    w_up,
    w_ffn_out,
):
    dev_count = lax.axis_size("dp")
    bits = dev_count.bit_length() - 1
    part = lax.axis_index("mp")
    inner = 2 * w_query.shape[1]
    heads = inner // HDIM
    half = tokens.shape[1]
    first = part == 0
    part_ref = part.reshape(1).astype(jnp.int32)
    order_one = tuple(range(bits))
    order_two = (1, 0) + tuple(range(2, bits))

    def in_parts(own, peer, axis):
        return jnp.where(
            first, jnp.concatenate([own, peer], axis), jnp.concatenate([peer, own], axis)
        )

    row_ids = jnp.arange(ROWS_DEV, dtype=jnp.int32)
    kept_total = jnp.cumsum(keep_mask)
    in_first = row_ids < lengths[0]
    kept_first = jnp.sum(jnp.where(in_first, keep_mask, 0))
    kept_count = jnp.where(first, kept_first, kept_total[-1] - kept_first)
    rank = kept_total - 1 + jnp.where(in_first, 0, LMAX - kept_first)
    slot = jnp.where(keep_mask > 0, rank, -1).reshape(1, ROWS_DEV)

    own_tokens, peer_tokens = compact(part_ref, slot, tokens.T)
    state_t = in_parts(own_tokens, swap(peer_tokens), 0)
    own_cot, peer_cot = compact(part_ref, slot, cotangent.T)
    cot_own = in_parts(own_cot, swap(peer_cot), 0)
    cot_peer = in_parts(peer_cot, swap(own_cot), 0)

    own_weights = jnp.stack([w_query.T, w_key.T, w_value.T, w_attn_out])
    weights = in_parts(own_weights, swap(own_weights), 1)
    w_qkv = weights[:3].reshape(3 * inner, D)
    w_out = weights[3]
    table = in_parts(rel_table, swap(rel_table), 1)
    strip = bias_strip(table, heads)

    state = state_t.astype(F32)
    scale_one = lax.rsqrt(jnp.mean(state * state, axis=0, keepdims=True) + EPSILON)
    gain_one = ln_attn[:, None]
    normed_one = (state * scale_one * gain_one).astype(BF16)
    qkv = dot(w_qkv, normed_one, NN).astype(BF16)
    del_logit = dot(w_delete.reshape(1, D), normed_one, NN)
    del_gate = (-DELETE_DEPTH * jax.nn.sigmoid(-del_logit)).astype(BF16)
    valid = jnp.arange(LMAX, dtype=jnp.int32)[None, :] < kept_count
    gate_row = jnp.where(valid, del_gate, jnp.asarray(NEG_LARGE, BF16))
    gate_rows = jnp.concatenate([gate_row, jnp.zeros((AUG - 1, LMAX), BF16)], axis=0)
    prob, attended = attend(qkv, gate_rows, strip, heads)

    mid = state + dot(w_out, attended, TN)
    scale_two = lax.rsqrt(jnp.mean(mid * mid, axis=0, keepdims=True) + EPSILON)
    gain_two = ln_ffn[:, None]
    normed_two = (mid * scale_two * gain_two).astype(BF16)
    normed_two_peer = swap(normed_two)
    w_down_t = w_ffn_out.T
    hid_own, gg_own, gu_own = ffn(w_gate, w_up, w_down_t, normed_two, cot_own)
    hid_peer, gg_peer, gu_peer = ffn(w_gate, w_up, w_down_t, normed_two_peer, cot_peer)

    part_down = weight_grad(hid_own, hid_peer, cot_own, cot_peer)
    part_gate = weight_grad(gg_own, gg_peer, normed_two, normed_two_peer)
    part_up = weight_grad(gu_own, gu_peer, normed_two, normed_two_peer)
    grad_down = halve(part_down, order_one)
    grad_gate = halve(part_gate, order_two)
    share = part_up.shape[0] // dev_count
    cut = (share // 2 + 15) // 16 * 16 if share % 16 == 0 else share // 2
    pieces = part_up.reshape(dev_count, share, D)
    grad_up = jnp.concatenate(
        [
            halve(pieces[:, :cut].reshape(-1, D), order_one),
            halve(pieces[:, cut:].reshape(-1, D), order_two),
        ],
        axis=0,
    )

    back_peer = project((w_gate, w_up), (gg_peer, gu_peer), BF16)
    back_own = project((w_gate, w_up), (gg_own, gu_own), F32)
    grad_normed_two = back_own + swap(back_peer).astype(F32)
    weighted_two = grad_normed_two * gain_two
    inner_two = jnp.sum(weighted_two * mid, axis=0, keepdims=True)
    grad_mid = (
        cot_own.astype(F32) + scale_two * weighted_two - mid * (scale_two**3 * inner_two / D)
    )
    grad_ln_ffn = jnp.sum(grad_normed_two * (mid * scale_two), axis=1)
    grad_attn = grad_mid.astype(BF16)
    grad_attended = dot(w_out, grad_attn, NN).astype(BF16)
    grad_w_out = dot(attended, grad_attn, NT)

    grad_q, grad_k, grad_v, sums, near = attend_back(qkv, prob, grad_attended, heads)
    grad_gate_own = jnp.sum(sums, axis=(0, 1))[None, :]
    grad_logit = (
        grad_gate_own * DELETE_DEPTH * jax.nn.sigmoid(del_logit) * jax.nn.sigmoid(-del_logit)
    )
    grad_qkv = jnp.concatenate([grad_q, grad_k, grad_v], axis=0)
    grad_w_qkv = dot(grad_qkv, normed_one, NT)
    grad_w_delete = jnp.sum(normed_one.astype(F32) * grad_logit, axis=1)
    grad_normed_one = dot(w_qkv, grad_qkv, TN) + w_delete.astype(F32)[:, None] * grad_logit
    weighted_one = grad_normed_one * gain_one
    inner_one = jnp.sum(weighted_one * state, axis=0, keepdims=True)
    grad_state = (
        grad_mid + scale_one * weighted_one - state * (scale_one**3 * inner_one / D)
    ).astype(BF16)
    grad_ln_attn = jnp.sum(grad_normed_one * (state * scale_one), axis=1)

    blocks = LMAX // TILE
    tile_sums = jnp.sum(sums.reshape(heads, blocks, blocks, TILE), axis=3)
    block_ids = jnp.arange(blocks)
    shift = block_ids[None, :] - block_ids[:, None]
    far_before = jnp.sum(jnp.where(shift <= -2, tile_sums, 0.0), axis=(1, 2))
    far_after = jnp.sum(jnp.where(shift >= 2, tile_sums, 0.0), axis=(1, 2))
    grad_table = jnp.sum(near, axis=(2, 3)).T
    bucket_ids = jnp.arange(BUCKETS)[:, None]
    grad_table = (
        grad_table
        + jnp.where(bucket_ids == 15, far_before[None, :], 0.0)
        + jnp.where(bucket_ids == 31, far_after[None, :], 0.0)
    )

    small = jnp.concatenate([grad_table.reshape(-1), grad_ln_ffn, grad_ln_attn, grad_w_delete])
    small = lax.psum(small, ("dp", "mp"))
    table_size = BUCKETS * heads
    grad_table = small[:table_size].reshape(BUCKETS, heads)
    grad_ln_ffn = small[table_size : table_size + D]
    grad_ln_attn = small[table_size + D : table_size + 2 * D]
    grad_w_delete = small[table_size + 2 * D :]

    own_rows = inner // 2
    grads = jnp.concatenate([grad_w_qkv, grad_w_out], axis=0).reshape(4, 2, own_rows, D)
    keep = lax.dynamic_index_in_dim(grads, part, 1, keepdims=False)
    give = lax.dynamic_index_in_dim(grads, 1 - part, 1, keepdims=False).astype(BF16)
    both = (keep + swap(give).astype(F32)).astype(BF16).reshape(4 * own_rows, D)
    total = regather(halve(both, order_one).astype(BF16), order_one).astype(F32)
    total = total.reshape(4, own_rows, D)

    mixed_peer = project((w_down_t,), (hid_peer,), BF16)
    mixed_own = project((w_down_t,), (hid_own,), F32)
    mixed = (mid + mixed_own + swap(mixed_peer).astype(F32)).astype(BF16)

    def home(values):
        mine = lax.dynamic_slice_in_dim(values, part * half, half, 0)
        other = lax.dynamic_slice_in_dim(values, (1 - part) * half, half, 0)
        return spread(part_ref, slot, mine, swap(other)).T

    def own_half(values):
        return lax.dynamic_slice_in_dim(values, part * half, half, 0)

    return (
        home(mixed),
        home(grad_state),
        own_half(grad_ln_attn),
        total[0].T,
        total[1].T,
        total[2].T,
        total[3],
        lax.dynamic_slice_in_dim(grad_table, part * (heads // 2), heads // 2, 1),
        grad_w_delete,
        own_half(grad_ln_ffn),
        grad_gate.T,
        grad_up.T,
        grad_down,
    )


def solution(mesh):
    return jax.shard_map(
        body,
        mesh=mesh,
        in_specs=(
            P("dp", "mp"),
            P("dp", "mp"),
            P("dp"),
            P("dp"),
            P(),
            P(None, "mp"),
            P(None, "mp"),
            P(None, "mp"),
            P("mp", None),
            P(None, "mp"),
            P(),
            P(),
            P(None, "mp"),
            P(None, "mp"),
            P("mp", None),
        ),
        out_specs=(
            P("dp", "mp"),
            P("dp", "mp"),
            P("mp"),
            P(None, "mp"),
            P(None, "mp"),
            P(None, "mp"),
            P("mp", None),
            P(None, "mp"),
            P(),
            P("mp"),
            P(None, ("mp", "dp")),
            P(None, ("mp", "dp")),
            P(("mp", "dp"), None),
        ),
        check_vma=False,
    )
```

```python
import functools

import jax
import jax.numpy as jnp
import numpy as np
from jax import lax
from jax.experimental import pallas as pl
from jax.experimental.pallas import tpu as pltpu
from jax.sharding import PartitionSpec as P

D = 1472
HDIM = 64
BUCKETS = 32
LMAX = 1024
ROWS_DEV = 2048

EPSILON = 1e-06
DELETE_DEPTH = 4.0
NEG_LARGE = -1e30
NEAR_STEPS = (1, 2, 3, 4, 5, 6, 7, 8, 12, 16, 23, 32, 46, 64, 91)
TILE = 128
QBLOCK = 256
ABLOCK = 512
AUG = 16
F32 = jnp.float32
BF16 = jnp.bfloat16
GELU_C = float(np.sqrt(2.0 / np.pi))

NN = (((1,), (0,)), ((), ()))
TN = (((0,), (0,)), ((), ()))
NT = (((1,), (1,)), ((), ()))


def dot(a, b, dims):
    return lax.dot_general(a, b, dims, preferred_element_type=F32)


def with_side(kernel, inputs, outputs, pairs, bits_ref, *refs):
    first = inputs + 2 * pairs
    last = first + outputs + 2 * pairs
    kernel(*refs[:inputs], *refs[first : first + outputs], *refs[last:])
    for pair in range(pairs):
        keep_ref, came_ref = refs[inputs + 2 * pair : inputs + 2 * pair + 2]
        outs = refs[first + outputs + 2 * pair : first + outputs + 2 * pair + 2]
        mine = bits_ref[pair]
        for out, which in zip(outs, (mine, 1 - mine)):
            total = keep_ref[:, which].astype(F32) + came_ref[:, which].astype(F32)
            out[...] = total.astype(BF16)


def call(kernel, name, flops, nbytes, limit, side=(), **kw):
    for _, keep, came in side:
        nbytes += 6 * keep.size
    extra = ()
    outputs = 1
    if side:
        single = not isinstance(kw["out_shape"], list)
        out_specs = [kw["out_specs"]] if single else list(kw["out_specs"])
        out_shape = [kw["out_shape"]] if single else list(kw["out_shape"])
        outputs, inputs = len(out_shape), len(kw["in_specs"])
        in_specs = list(kw["in_specs"])
        for _, keep, came in side:
            outer, _, rows, width = keep.shape
            block = pl.BlockSpec(
                (1, 2, rows, width), lambda i, n=outer: (jnp.minimum(i, n - 1), 0, 0, 0)
            )
            out = pl.BlockSpec(
                (1, rows, width), lambda i, n=outer: (jnp.minimum(i, n - 1), 0, 0)
            )
            in_specs += [block, block]
            out_specs += [out, out]
            out_shape += [jax.ShapeDtypeStruct((outer, rows, width), BF16)] * 2
            extra += (keep, came)
        kernel = functools.partial(with_side, kernel, inputs, outputs, len(side))
        kw.update(in_specs=[SMEM] + in_specs, out_specs=out_specs, out_shape=out_shape)
    run = pl.pallas_call(
        kernel,
        name=name,
        cost_estimate=pl.CostEstimate(
            flops=int(flops), bytes_accessed=int(nbytes), transcendentals=0
        ),
        compiler_params=pltpu.CompilerParams(vmem_limit_bytes=56 << 20),
        **kw,
    )
    if not side:
        return run

    def launch(*args):
        out = run(jnp.stack([bit for bit, _, _ in side]), *args, *extra)
        main = out[0] if single else out[:outputs]
        return main, out[outputs:]

    return launch


VMEM = pl.BlockSpec(memory_space=pltpu.VMEM)
SMEM = pl.BlockSpec(memory_space=pltpu.SMEM)
ANY = pl.BlockSpec(memory_space=pl.ANY)


def place_kernel(
    part_ref, length_ref, mask_ref, q_ref, k_ref, v_ref, out_ref, slot_ref, count_ref, stack_ref
):
    for i, ref in enumerate((q_ref, k_ref, v_ref, out_ref)):
        stack_ref[i] = ref[...]
    mask = mask_ref[...]
    rows = lax.broadcasted_iota(jnp.int32, (1, ROWS_DEV), 1)
    first = (rows < length_ref[0]).astype(jnp.int32)
    pieces = []
    before = jnp.zeros((1, 1), F32)
    ahead = lax.broadcasted_iota(jnp.int32, (QBLOCK, QBLOCK), 0) <= lax.broadcasted_iota(
        jnp.int32, (QBLOCK, QBLOCK), 1
    )
    ahead = ahead.astype(F32).astype(BF16)
    flags = mask.astype(F32).astype(BF16)
    for block in range(ROWS_DEV // QBLOCK):
        part = flags[:, block * QBLOCK : (block + 1) * QBLOCK]
        ranks = dot(jnp.broadcast_to(part, (16, QBLOCK)), ahead, NN)[:1] + before
        before = ranks[:, QBLOCK - 1 :]
        pieces.append(ranks)
    ranks = jnp.concatenate(pieces, axis=1).astype(jnp.int32)
    kept_first = jnp.sum(mask * first, axis=1, keepdims=True)
    total = jnp.sum(mask, axis=1, keepdims=True)
    rank = ranks - 1 + jnp.where(first > 0, 0, LMAX - kept_first)
    slot_ref[...] = jnp.where(mask > 0, rank, -1)
    count = jnp.where(part_ref[0] == 0, kept_first, total - kept_first)
    count_ref[...] = jnp.broadcast_to(count, (1, 128))


def places(part, lengths, mask, weights):
    return call(
        place_kernel,
        "places",
        1e6,
        1e5,
        16,
        in_specs=[SMEM, SMEM, VMEM] + [VMEM] * 4,
        out_specs=[VMEM, VMEM, VMEM],
        out_shape=[
            jax.ShapeDtypeStruct((1, ROWS_DEV), jnp.int32),
            jax.ShapeDtypeStruct((1, 128), jnp.int32),
            jax.ShapeDtypeStruct((4, *weights[0].shape), BF16),
        ],
    )(part, lengths, mask, *weights)


def compact_half(item, slot_ref, x_ref, out_ref):
    for block in range(LMAX // QBLOCK):
        width = ROWS_DEV - 512 - block * QBLOCK
        start = pl.multiple_of(item * 512 + block * QBLOCK, 128)
        ids = item * LMAX + block * QBLOCK + lax.broadcasted_iota(jnp.int32, (QBLOCK, 1), 0)
        hot = (slot_ref[:, pl.ds(start, width)] == ids).astype(F32).astype(BF16)
        rows = dot(x_ref[:, pl.ds(start, width)], hot, NT)
        out_ref[:, block * QBLOCK : (block + 1) * QBLOCK] = rows.astype(BF16)


def compact_kernel(part_ref, slot_ref, x_ref, own_ref, peer_ref):
    compact_half(part_ref[0], slot_ref, x_ref, own_ref)
    compact_half(1 - part_ref[0], slot_ref, x_ref, peer_ref)


def halves(part, own, came, whole, hold, sems):
    size = own.shape[0]
    copies_in, copies_out = [], []
    for i, (ref, place) in enumerate(((own, part), (came, 1 - part))):
        copies_in.append(pltpu.make_async_copy(ref, hold.at[i], sems.at[0, i]))
        target = whole.at[pl.ds(pl.multiple_of(place * size, 16), size)]
        copies_out.append(pltpu.make_async_copy(hold.at[i], target, sems.at[1, i]))
    return copies_in, copies_out


def compact_join_kernel(
    part_ref, slot_ref, x_ref, stack_ref, came_ref, own_ref, peer_ref, qkv_ref, out_ref, hold, sems
):
    part = part_ref[0]
    inner = out_ref.shape[0]
    copies_in, copies_out = [], []
    for i in range(4):
        whole = qkv_ref.at[pl.ds(i * inner, inner)] if i < 3 else out_ref
        ins, outs = halves(part, stack_ref.at[i], came_ref.at[i], whole, hold.at[i], sems.at[i])
        copies_in += ins
        copies_out += outs
    for copy in copies_in:
        copy.start()
    compact_half(part, slot_ref, x_ref, own_ref)
    for copy, following in zip(copies_in, copies_out):
        copy.wait()
        following.start()
    compact_half(1 - part, slot_ref, x_ref, peer_ref)
    for copy in copies_out:
        copy.wait()


def compact_join(part, slot, columns, stack, came):
    width = columns.shape[0]
    inner = 2 * stack.shape[1]
    shape = jax.ShapeDtypeStruct((width, LMAX), BF16)
    return call(
        compact_join_kernel,
        "compact_join",
        2 * width * 2 * 4608 * 256,
        width * 2048 * 4,
        24,
        in_specs=[SMEM, VMEM, VMEM, ANY, ANY],
        out_specs=[VMEM, VMEM, ANY, ANY],
        out_shape=[
            shape,
            shape,
            jax.ShapeDtypeStruct((3 * inner, D), BF16),
            jax.ShapeDtypeStruct((inner, D), BF16),
        ],
        scratch_shapes=[
            pltpu.VMEM((4, 2, inner // 2, D), BF16), pltpu.SemaphoreType.DMA((4, 2, 2))
        ],
    )(part, slot, columns, stack, came)


def compact(part, slot, columns):
    width = columns.shape[0]
    shape = jax.ShapeDtypeStruct((width, LMAX), BF16)
    return call(
        compact_kernel,
        "compact",
        2 * width * 2 * 4608 * 256,
        width * 2048 * 4,
        16,
        in_specs=[SMEM, VMEM, VMEM],
        out_specs=[VMEM, VMEM],
        out_shape=[shape, shape],
    )(part, slot, columns)


def spread_kernel(part_ref, slot_ref, own_ref, peer_ref, out_ref):
    first = part_ref[0] == 0
    items = (
        jnp.where(first, own_ref[...], peer_ref[...]),
        jnp.where(first, peer_ref[...], own_ref[...]),
    )
    for block in range(ROWS_DEV // QBLOCK):
        end = (block + 1) * QBLOCK
        slots = slot_ref[:, end - QBLOCK : end]
        total = None
        for item in range(2):
            reach = min(end - 512 * item, LMAX)
            if reach <= 0 or (item == 0 and end > LMAX):
                continue
            ids = item * LMAX + lax.broadcasted_iota(jnp.int32, (reach, 1), 0)
            hot = (slots == ids).astype(F32).astype(BF16)
            part = dot(items[item][:, :reach], hot, NN)
            total = part if total is None else total + part
        out_ref[:, end - QBLOCK : end] = total.astype(BF16)


def spread(part, slot, own, peer):
    width = own.shape[0]
    return call(
        spread_kernel,
        "spread",
        2 * width * 7168 * 256,
        width * 2048 * 4,
        16,
        in_specs=[SMEM, VMEM, VMEM, VMEM],
        out_specs=VMEM,
        out_shape=jax.ShapeDtypeStruct((width, ROWS_DEV), BF16),
    )(part, slot, own, peer)


COLUMNS = 3
ROWS = pl.BlockSpec((D, QBLOCK), lambda i: (0, i))
LINE = pl.BlockSpec((1, QBLOCK), lambda i: (0, i))
COLUMN = pl.BlockSpec((D, COLUMNS), lambda i: (0, 0))
SUMS = pl.BlockSpec((D, 128), lambda i: (0, 0))


def fixed_spec(shape):
    return pl.BlockSpec(shape, lambda i: (0,) * len(shape), pipeline_mode=pl.Buffered(1))


def whole_spec(array):
    return fixed_spec(array.shape)


def line(rows=1, dtype=F32):
    return jax.ShapeDtypeStruct((rows, LMAX), dtype)


def folded(values):
    return sum(values[:, i * 128 : (i + 1) * 128] for i in range(values.shape[1] // 128))


def input_kernel(
    part_ref, own_ref, came_ref, gain_ref, weight_ref, count_ref,
    state_ref, normed_ref, qkv_ref, gate_ref, logit_ref, scale_ref,
):
    first = part_ref[0] == 0
    own, came = own_ref[...], came_ref[...]
    half = own.shape[0]
    state_ref[:half] = jnp.where(first, own, came)
    state_ref[half:] = jnp.where(first, came, own)
    state = state_ref[...].astype(F32)
    scale = lax.rsqrt(jnp.sum(state * state, axis=0, keepdims=True) / D + EPSILON)
    normed = (state * scale * gain_ref[:, 0:1]).astype(BF16)
    normed_ref[...] = normed
    scale_ref[...] = scale
    qkv_ref[...] = dot(weight_ref[...], normed, NN).astype(BF16)
    logit = jnp.sum(normed.astype(F32) * gain_ref[:, 2:3], axis=0, keepdims=True)
    logit_ref[...] = logit
    gate = -DELETE_DEPTH * jax.nn.sigmoid(-logit)
    rows = pl.program_id(0) * QBLOCK + lax.broadcasted_iota(jnp.int32, (1, QBLOCK), 1)
    gate = jnp.where(rows < count_ref[:, :1], gate, NEG_LARGE)
    place = lax.broadcasted_iota(jnp.int32, (AUG, QBLOCK), 0)
    gate_ref[...] = jnp.where(place == 0, gate, 0.0).astype(BF16)


def input_part(part, own, came, gain, weights, count):
    inner = weights.shape[0]
    half = pl.BlockSpec((own.shape[0], QBLOCK), lambda i: (0, i))
    return call(
        input_kernel,
        "norm_project",
        2 * D * LMAX * weights.shape[0],
        D * LMAX * 10,
        24,
        grid=(LMAX // QBLOCK,),
        in_specs=[SMEM, half, half, COLUMN, whole_spec(weights), whole_spec(count)],
        out_specs=[
            ROWS,
            ROWS,
            pl.BlockSpec((inner, QBLOCK), lambda i: (0, i)),
            pl.BlockSpec((AUG, QBLOCK), lambda i: (0, i)),
            LINE,
            LINE,
        ],
        out_shape=[line(D, BF16), line(D, BF16), line(inner, BF16), line(AUG, BF16), line(), line()],
    )(part, own, came, gain, weights, count)


def middle_kernel(weight_ref, attended_ref, state_ref, gain_ref, mid_ref, normed_ref, scale_ref):
    mid = state_ref[...].astype(F32) + dot(weight_ref[...], attended_ref[...], TN)
    scale = lax.rsqrt(jnp.sum(mid * mid, axis=0, keepdims=True) / D + EPSILON)
    mid_ref[...] = mid
    scale_ref[...] = scale
    normed_ref[...] = (mid * scale * gain_ref[:, 1:2]).astype(BF16)


def middle_part(weights, attended, state, gain):
    inner = attended.shape[0]
    return call(
        middle_kernel,
        "attention_out_norm",
        2 * D * LMAX * inner,
        D * LMAX * 8,
        24,
        grid=(LMAX // QBLOCK,),
        in_specs=[
            whole_spec(weights),
            pl.BlockSpec((inner, QBLOCK), lambda i: (0, i)),
            ROWS,
            COLUMN,
        ],
        out_specs=[ROWS, ROWS, LINE],
        out_shape=[line(D), line(D, BF16), line()],
    )(weights, attended, state, gain)


def middle_back_kernel(
    gate_ref, up_ref, gg_ref, gu_ref, came_ref, mid_ref, cot_ref, gain_ref, scale_ref, weight_ref,
    grad_mid_ref, grad_attn_ref, attended_ref, sums_ref,
):
    grad = dot(gate_ref[...], gg_ref[...], NN) + dot(up_ref[...], gu_ref[...], NN)
    grad = grad + came_ref[...].astype(F32)
    mid, scale = mid_ref[...], scale_ref[...]
    weighted = grad * gain_ref[:, 1:2]
    inner = jnp.sum(weighted * mid, axis=0, keepdims=True)
    grad_mid = (
        cot_ref[...].astype(F32) + scale * weighted - mid * (scale * scale * scale * inner / D)
    )
    grad_mid_ref[...] = grad_mid
    grad_attn = grad_mid.astype(BF16)
    grad_attn_ref[...] = grad_attn
    attended_ref[...] = dot(weight_ref[...], grad_attn, NN).astype(BF16)

    @pl.when(pl.program_id(0) == 0)
    def _():
        sums_ref[...] = jnp.zeros_like(sums_ref)

    sums_ref[...] += folded(grad * (mid * scale))


def middle_back(w_gate, w_up, gg, gu, came, mid, cot, gain, scale, w_out):
    inner, units = w_out.shape[0], w_gate.shape[1]
    unit_rows = pl.BlockSpec((units, QBLOCK), lambda i: (0, i))
    return call(
        middle_back_kernel,
        "norm_back",
        4 * D * LMAX * units,
        D * LMAX * 20 + 4 * D * units,
        44,
        grid=(LMAX // QBLOCK,),
        in_specs=[
            whole_spec(w_gate), whole_spec(w_up), unit_rows, unit_rows, ROWS, ROWS, ROWS, COLUMN,
            LINE, whole_spec(w_out),
        ],
        out_specs=[ROWS, ROWS, pl.BlockSpec((inner, QBLOCK), lambda i: (0, i)), SUMS],
        out_shape=[
            line(D), line(D, BF16), line(inner, BF16), jax.ShapeDtypeStruct((D, 128), F32),
        ],
    )(w_gate, w_up, gg, gu, came, mid, cot, gain, scale, w_out)


def input_back_block(q, k, v, weight_ref, normed, state, grad_mid, scale, logit, sums, columns):
    heads = sums.shape[0]
    gate = sums[0]
    for head in range(1, heads):
        gate = gate + sums[head]
    gate = jnp.sum(gate, axis=0, keepdims=True)
    grad_logit = gate * DELETE_DEPTH * jax.nn.sigmoid(logit) * jax.nn.sigmoid(-logit)
    inner = q.shape[0]
    grad = dot(weight_ref[:inner], q, TN)
    grad = grad + dot(weight_ref[inner : 2 * inner], k, TN)
    grad = grad + dot(weight_ref[2 * inner : 3 * inner], v, TN)
    grad = grad + columns[:, 2:3] * grad_logit
    state = state.astype(F32)
    weighted = grad * columns[:, 0:1]
    total = jnp.sum(weighted * state, axis=0, keepdims=True)
    grad_state = grad_mid + scale * weighted - state * (scale * scale * scale * total / D)
    gain_part = folded(grad * (state * scale))
    delete_part = folded(normed.astype(F32) * grad_logit)
    return grad_state.astype(BF16), gain_part, delete_part


def input_back_kernel(
    q_ref, k_ref, v_ref, weight_ref, normed_ref, state_ref, grad_mid_ref, scale_ref, logit_ref,
    sums_ref, columns_ref, grad_ref, gain_sum_ref, delete_sum_ref,
):
    grad_ref[...], gain_part, delete_part = input_back_block(
        q_ref[...], k_ref[...], v_ref[...], weight_ref, normed_ref[...], state_ref[...],
        grad_mid_ref[...], scale_ref[...], logit_ref[...], sums_ref[...], columns_ref[...],
    )

    @pl.when(pl.program_id(0) == 0)
    def _():
        gain_sum_ref[...] = jnp.zeros_like(gain_sum_ref)
        delete_sum_ref[...] = jnp.zeros_like(delete_sum_ref)

    gain_sum_ref[...] += gain_part
    delete_sum_ref[...] += delete_part


def input_back(side, q, k, v, weights, normed, state, grad_mid, scale, logit, sums, gain):
    inner = q.shape[0]
    head_rows = pl.BlockSpec((inner, QBLOCK), lambda i: (0, i))
    return call(
        input_back_kernel,
        "project_norm_back",
        6 * D * LMAX * inner,
        D * LMAX * 12,
        28,
        side=side,
        grid=(LMAX // QBLOCK,),
        in_specs=[
            head_rows, head_rows, head_rows, whole_spec(weights), ROWS, ROWS, ROWS, LINE, LINE,
            pl.BlockSpec((sums.shape[0], sums.shape[1], QBLOCK), lambda i: (0, 0, i)),
            COLUMN,
        ],
        out_specs=[ROWS, SUMS, SUMS],
        out_shape=[
            line(D, BF16),
            jax.ShapeDtypeStruct((D, 128), F32),
            jax.ShapeDtypeStruct((D, 128), F32),
        ],
    )(q, k, v, weights, normed, state, grad_mid, scale, logit, sums, gain)


def mixed_kernel(down_ref, hid_ref, came_ref, mid_ref, out_ref):
    mixed = mid_ref[...] + dot(down_ref[...], hid_ref[...], NN)
    out_ref[...] = (mixed + came_ref[...].astype(F32)).astype(BF16)


def mixed_part(down, hid, came, mid):
    width = D // 4
    units = down.shape[1]
    rows = pl.BlockSpec((width, LMAX), lambda i: (i, 0))
    return call(
        mixed_kernel,
        "mixed",
        2 * D * LMAX * units,
        D * LMAX * 8 + D * units * 2,
        24,
        grid=(D // width,),
        in_specs=[pl.BlockSpec((width, units), lambda i: (i, 0)), whole_spec(hid), rows, rows],
        out_specs=rows,
        out_shape=line(D, BF16),
    )(down, hid, came, mid)


def head_grad_kernel(part_ref, q_ref, v_ref, k_ref, attended_ref, normed_ref, back_ref, *outs):
    keep_ref, give_ref, hold = outs
    part = part_ref[0]
    rows = hold.shape[0] // 2
    pieces = (
        (q_ref, normed_ref), (v_ref, normed_ref), (k_ref, normed_ref), (attended_ref, back_ref),
    )
    for place, (left, right) in enumerate(pieces):
        hold[...] = dot(left[...], right[...], NT).astype(BF16)
        keep_ref[place] = hold[pl.ds(pl.multiple_of(part * rows, 16), rows)]
        give_ref[place] = hold[pl.ds(pl.multiple_of((1 - part) * rows, 16), rows)]


def head_grads(part, q, k, v, normed, attended, back):
    inner = q.shape[0]
    shape = jax.ShapeDtypeStruct((4, inner // 2, D), BF16)
    return call(
        head_grad_kernel,
        "head_grads",
        8 * D * LMAX * inner,
        D * LMAX * 4 + 4 * LMAX * inner * 2 + 16 * inner * D,
        36,
        in_specs=[SMEM] + [VMEM] * 6,
        out_specs=[VMEM, VMEM],
        out_shape=[shape, shape],
        scratch_shapes=[pltpu.VMEM((inner, D), BF16)],
    )(part, q, v, k, attended, normed, back)


MESH = pl.DeviceIdType.MESH


class Sender:
    def __init__(self, send_sems, recv_sems):
        self.send_sems, self.recv_sems, self.made = send_sems, recv_sems, []

    def start(self, source, target, device):
        place = len(self.made)
        copy = pltpu.make_async_remote_copy(
            src_ref=source,
            dst_ref=target,
            send_sem=self.send_sems.at[place],
            recv_sem=self.recv_sems.at[place],
            device_id=device,
            device_id_type=MESH,
        )
        copy.start()
        self.made.append(copy)
        return copy

    def finish(self):
        for copy in self.made:
            copy.wait_send()


def arrived(copies):
    for copy in copies:
        copy.wait_recv()


def plus(first, *others):
    total = first.astype(F32)
    for other in others:
        total = total + other.astype(F32)
    return total


def neighbours():
    me, part = lax.axis_index("dp"), lax.axis_index("mp")
    x, y, z = me % 2, (me // 2) % 2, me // 4
    across_x, across_y = 1 - 2 * x, 2 - 4 * y
    planes = [(z + k) % 4 for k in range(1, 4)]
    return dict(
        x=x,
        y=y,
        z=z,
        part=part,
        planes=planes,
        to_core=(me, 1 - part),
        to_x=(me + across_x, part),
        to_y=(me + across_y, part),
        to_corner=(me + across_x + across_y, part),
        to_plane=[(p * 4 + me % 4, part) for p in planes],
    )


def meet(devices):
    barrier = pltpu.get_barrier_semaphore()
    for device in devices:
        pl.semaphore_signal(barrier, inc=1, device_id=device, device_id_type=MESH)
    pl.semaphore_wait(barrier, len(devices))


CHUNK = 16


def tail_kernel(
    keep_ref, give_ref, keep_x, came_x, keep_y, came_y, ffn_sum_ref, near_ref,
    q_ref, k_ref, v_ref, weight_ref, normed_ref, state_ref, grad_mid_ref, scale_ref, logit_ref,
    sums_ref, columns_ref,
    out_ref, share_ref, vector_ref, own_ref, came_grad_ref,
    came_ref, total, from_x, from_y, sum_x, sum_y, last_x, last_y, plane_sum, from_planes,
    give_x, give_y, second_x, second_y, whole, from_whole,
    vector, vector_core, vector_near, vector_far, grad_state, send_sems, recv_sems,
):
    at = neighbours()
    x, y, z = at["x"], at["y"], at["z"]
    to_x, to_y = at["to_x"], at["to_y"]
    rows = keep_ref.shape[3]
    chunks = [slice(c * CHUNK, (c + 1) * CHUNK) for c in range(rows // CHUNK)]
    sender = Sender(send_sems, recv_sems)
    meet([at["to_core"], to_x, to_y, at["to_corner"], *at["to_plane"]])

    cores = [
        sender.start(give_ref.at[:, :, :, c], came_ref.at[:, :, :, c], at["to_core"])
        for c in chunks
    ]
    give_x[...] = plus(keep_x[:, 1 - y], came_x[:, 1 - y]).astype(BF16)
    give_y[...] = plus(keep_y[:, 1 - x], came_y[:, 1 - x]).astype(BF16)

    def first(c):
        arrived([cores[c]])
        c = chunks[c]
        total[:, :, :, c] = plus(keep_ref[:, :, :, c], came_ref[:, :, :, c]).astype(BF16)
        return [
            sender.start(total.at[0:2, :, 1 - x, c], from_x.at[:, :, c], to_x),
            sender.start(total.at[2:4, 1 - y, :, c], from_y.at[:, :, c], to_y),
        ]

    def second(c, copies):
        arrived(copies)
        c = chunks[c]
        sum_x[:, :, c] = plus(total[0:2, :, x, c], from_x[:, :, c]).astype(BF16)
        sum_y[:, :, c] = plus(total[2:4, y, :, c], from_y[:, :, c]).astype(BF16)
        return [
            sender.start(sum_x.at[:, 1 - y, c], last_x.at[:, c], to_y),
            sender.start(sum_y.at[:, 1 - x, c], last_y.at[:, c], to_x),
        ]

    def third(c, copies):
        arrived(copies)
        c = chunks[c]
        plane_sum[0:2, c] = plus(sum_x[:, y, c], last_x[:, c]).astype(BF16)
        plane_sum[2:4, c] = plus(sum_y[:, x, c], last_y[:, c]).astype(BF16)
        return [
            sender.start(plane_sum.at[p, c], from_planes.at[k, c], device)
            for k, (p, device) in enumerate(zip(at["planes"], at["to_plane"]))
        ]

    def fourth(c, copies):
        arrived(copies)
        c = chunks[c]
        got = [from_planes[k, c] for k in range(3)]
        out_ref[z, y, x, c] = plus(plane_sum[z, c], *got).astype(BF16)
        here = out_ref.at[z, y, x, c]
        return [sender.start(here, here, device) for device in at["to_plane"]]

    def fifth(c, copies):
        arrived(copies)
        c = chunks[c]
        here_x, here_y = out_ref.at[0:2, y, x, c], out_ref.at[2:4, y, x, c]
        return [sender.start(here_x, here_x, to_y), sender.start(here_y, here_y, to_x)]

    def sixth(c, copies):
        arrived(copies)
        c = chunks[c]
        here_x, here_y = out_ref.at[0:2, :, x, c], out_ref.at[2:4, y, :, c]
        return [sender.start(here_x, here_x, to_x), sender.start(here_y, here_y, to_y)]

    stages = [first, second, third, fourth, fifth, sixth]
    flying = [None] * len(chunks)

    def advance(c, stage):
        flying[c] = stages[stage](c, flying[c]) if stage else first(c)

    half = own_ref.shape[0]
    mine = pl.ds(pl.multiple_of(at["part"] * half, 16), half)
    other = pl.ds(pl.multiple_of((1 - at["part"]) * half, 16), half)
    parts = []
    came_grads = []

    def compute(block):
        cols = slice(block * QBLOCK, (block + 1) * QBLOCK)
        grad, gain_part, delete_part = input_back_block(
            q_ref[:, cols], k_ref[:, cols], v_ref[:, cols], weight_ref, normed_ref[:, cols],
            state_ref[:, cols], grad_mid_ref[:, cols], scale_ref[:, cols], logit_ref[:, cols],
            sums_ref[:, :, cols], columns_ref[...],
        )
        grad_state[:, cols] = grad
        own_ref[:, cols] = grad_state[mine, cols]
        came_grads.append(
            sender.start(grad_state.at[other, cols], came_grad_ref.at[:, cols], at["to_core"])
        )
        parts.append((gain_part, delete_part))

    advance(0, 0)
    seconds = [
        sender.start(give_x, second_x, to_y),
        sender.start(give_y, second_y, to_x),
    ]
    advance(1, 0)
    advance(2, 0)
    compute(0)
    advance(0, 1)
    compute(1)
    advance(1, 1)
    advance(0, 2)
    arrived(seconds)
    cut = keep_x.shape[2]
    whole[:, :cut] = plus(keep_x[:, y], came_x[:, y], second_x[...]).astype(BF16)
    whole[:, cut:] = plus(keep_y[:, x], came_y[:, x], second_y[...]).astype(BF16)
    wholes = [
        sender.start(whole.at[p], from_whole.at[k], device)
        for k, (p, device) in enumerate(zip(at["planes"], at["to_plane"]))
    ]
    compute(2)
    advance(2, 1)
    advance(1, 2)
    advance(0, 3)
    compute(3)
    advance(2, 2)
    advance(1, 3)
    advance(0, 4)

    ones = jnp.ones((8, 128), F32)

    def line_of(values):
        return lax.dot_general(
            ones, values, NT, preferred_element_type=F32, precision=lax.Precision.HIGHEST
        )[:1]

    vector[...] = jnp.zeros_like(vector)
    vector[0:1] = line_of(ffn_sum_ref[...])
    vector[1:2] = line_of(sum(p[0] for p in parts))
    vector[2:3] = line_of(sum(p[1] for p in parts))
    vector[3:4, : near_ref.shape[0]] = line_of(near_ref[...])
    vectors = [sender.start(vector, vector_core, at["to_core"])]
    advance(2, 3)
    advance(1, 4)
    advance(0, 5)
    arrived(vectors)
    vector_core[...] = vector_core[...] + vector[...]
    vectors = [
        sender.start(vector_core, vector_near.at[k], device)
        for k, device in enumerate((to_x, to_y, at["to_corner"]))
    ]
    advance(2, 4)
    advance(1, 5)
    arrived(vectors)
    vector_ref[...] = vector_core[...] + vector_near[0] + vector_near[1] + vector_near[2]
    vectors = [
        sender.start(vector_ref, vector_far.at[k], device)
        for k, device in enumerate(at["to_plane"])
    ]
    advance(2, 5)
    arrived(wholes)
    share_ref[...] = plus(whole[z], from_whole[0], from_whole[1], from_whole[2])
    for copies in flying:
        arrived(copies)
    arrived(came_grads)
    arrived(vectors)
    sender.finish()
    vector_ref[...] = vector_ref[...] + vector_far[0] + vector_far[1] + vector_far[2]


def tail(keep, give, up_x, up_y, ffn_sum, near, *values):
    rows = keep.shape[1] // 4
    (keep_x, came_x), (keep_y, came_y) = up_x, up_y
    cut, rest = keep_x.shape[2], keep_y.shape[2]
    share = cut + rest
    shape = (4, 2, 2, rows, D)
    copies = 80

    def hold(*dims, dtype=BF16):
        return pltpu.VMEM(dims, dtype)

    return pl.pallas_call(
        tail_kernel,
        name="tail",
        in_specs=[VMEM] * (8 + len(values)),
        out_specs=[VMEM] * 5,
        out_shape=[
            jax.ShapeDtypeStruct(shape, BF16),
            jax.ShapeDtypeStruct((share, D), F32),
            jax.ShapeDtypeStruct((8, D), F32),
            jax.ShapeDtypeStruct((D // 2, LMAX), BF16),
            jax.ShapeDtypeStruct((D // 2, LMAX), BF16),
        ],
        scratch_shapes=[
            hold(*shape), hold(*shape), hold(2, 2, rows, D), hold(2, 2, rows, D),
            hold(2, 2, rows, D), hold(2, 2, rows, D), hold(2, rows, D), hold(2, rows, D),
            hold(4, rows, D), hold(3, rows, D),
            hold(4, cut, D), hold(4, rest, D), hold(4, cut, D), hold(4, rest, D),
            hold(4, share, D), hold(3, share, D),
            hold(8, D, dtype=F32), hold(8, D, dtype=F32), hold(3, 8, D, dtype=F32),
            hold(3, 8, D, dtype=F32), hold(D, LMAX),
            pltpu.SemaphoreType.DMA((copies,)),
            pltpu.SemaphoreType.DMA((copies,)),
        ],
        cost_estimate=pl.CostEstimate(
            flops=6 * D * LMAX * 384, bytes_accessed=60 << 20, transcendentals=0
        ),
        compiler_params=pltpu.CompilerParams(
            vmem_limit_bytes=63 << 20, collective_id=1, has_side_effects=True
        ),
    )(keep.reshape(shape), give.reshape(shape), keep_x, came_x, keep_y, came_y, ffn_sum, near, *values)


STRIP = LMAX + LMAX - TILE


def offsets(shift):
    keys = lax.broadcasted_iota(jnp.int32, (TILE, TILE), 0)
    queries = lax.broadcasted_iota(jnp.int32, (TILE, TILE), 1)
    return shift * TILE + keys - queries


def strip_kernel(table_ref, strip_ref):
    head = pl.program_id(0)
    middle = LMAX - TILE

    def value(bucket):
        return table_ref[bucket, head]

    def side(distance, base, start):
        tile = jnp.full((TILE, TILE), start, F32)
        for count, step in enumerate(NEAR_STEPS):
            tile = jnp.where(distance >= step, value(base + count + 1), tile)
        return tile

    strip_ref[0, : middle - TILE, :] = jnp.full((middle - TILE, TILE), value(15), F32)
    strip_ref[0, middle + 2 * TILE :, :] = jnp.full((STRIP - middle - 2 * TILE, TILE), value(31), F32)
    before = offsets(-1)
    strip_ref[0, middle - TILE : middle, :] = side(-before, 0, value(0))
    relative = offsets(0)
    strip_ref[0, middle : middle + TILE, :] = jnp.where(
        relative > 0, side(relative, 16, value(0)), side(-relative, 0, value(0))
    )
    after = offsets(1)
    strip_ref[0, middle + TILE : middle + 2 * TILE, :] = side(after, 16, value(0))


def bias_strip(table, heads):
    return call(
        strip_kernel,
        "bias_strip",
        heads * 3e6,
        heads * STRIP * TILE * 4,
        8,
        grid=(heads,),
        in_specs=[SMEM],
        out_specs=pl.BlockSpec((1, STRIP, TILE), lambda h: (h, 0, 0)),
        out_shape=jax.ShapeDtypeStruct((heads, STRIP, TILE), F32),
    )(table)


def attend_kernel(
    part_ref, q_ref, k_ref, v_ref, gate_ref, strip_ref, own_ref, peer_ref, came_own_ref, came_peer_ref,
    prob_ref, out_ref, wide_ref, cot_own_ref, cot_peer_ref, hold, sems,
):
    head = pl.program_id(0)
    part = part_ref[0]
    copies_in, copies_out = halves(part, own_ref, came_own_ref, cot_own_ref, hold.at[0], sems.at[0])
    ins, outs = halves(part, peer_ref, came_peer_ref, cot_peer_ref, hold.at[1], sems.at[1])
    copies_in, copies_out = copies_in + ins, copies_out + outs

    @pl.when(head == 0)
    def _():
        for copy in copies_in:
            copy.start()

    @pl.when(head == 2)
    def _():
        for copy, following in zip(copies_in, copies_out):
            copy.wait()
            following.start()

    ones = (lax.broadcasted_iota(jnp.int32, (AUG, LMAX), 0) == 0).astype(F32).astype(BF16)
    scale = HDIM ** (-0.5)
    queries = jnp.concatenate([(q_ref[...].astype(F32) * scale).astype(BF16), ones], axis=0)
    keys = jnp.concatenate([k_ref[...], gate_ref[...]], axis=0)
    for block in range(LMAX // ABLOCK):
        low = block * ABLOCK
        scores = dot(keys, queries[:, low : low + ABLOCK], TN)
        bias = []
        for sub in range(ABLOCK // TILE):
            start = LMAX - TILE - (low + sub * TILE)
            bias.append(strip_ref[0, start : start + LMAX, :])
        scores = scores + jnp.concatenate(bias, axis=1)
        top = jnp.max(scores, axis=0, keepdims=True)
        weights = jnp.exp(scores - top)
        total = jnp.sum(weights, axis=0, keepdims=True)
        prob = (weights * (1.0 / total)).astype(BF16)
        prob_ref[0, :, low : low + ABLOCK] = prob
        out = dot(v_ref[...], prob, NN)
        wide_ref[:, low : low + ABLOCK] = out
        out_ref[:, low : low + ABLOCK] = out.astype(BF16)

    @pl.when(head == pl.num_programs(0) - 1)
    def _():
        for copy in copies_out:
            copy.wait()


def attend(part, qkv, gate, strip, own, peer, came_own, came_peer, heads):
    return call(
        attend_kernel,
        "attend",
        heads * 4 * LMAX * LMAX * HDIM * 4,
        heads * LMAX * LMAX * 2,
        36,
        grid=(heads,),
        in_specs=[
            SMEM,
            pl.BlockSpec((HDIM, LMAX), lambda h: (h, 0)),
            pl.BlockSpec((HDIM, LMAX), lambda h: (heads + h, 0)),
            pl.BlockSpec((HDIM, LMAX), lambda h: (2 * heads + h, 0)),
            pl.BlockSpec((AUG, LMAX), lambda h: (0, 0)),
            pl.BlockSpec((1, STRIP, TILE), lambda h: (h, 0, 0)),
            ANY, ANY, ANY, ANY,
        ],
        out_specs=[
            pl.BlockSpec((1, LMAX, LMAX), lambda h: (h, 0, 0)),
            pl.BlockSpec((HDIM, LMAX), lambda h: (h, 0)),
            pl.BlockSpec((HDIM, LMAX), lambda h: (h, 0)),
            ANY, ANY,
        ],
        out_shape=[
            jax.ShapeDtypeStruct((heads, LMAX, LMAX), BF16),
            jax.ShapeDtypeStruct((heads * HDIM, LMAX), BF16),
            jax.ShapeDtypeStruct((heads * HDIM, LMAX), F32),
            line(D, BF16), line(D, BF16),
        ],
        scratch_shapes=[
            pltpu.VMEM((2, 2, D // 2, LMAX), BF16), pltpu.SemaphoreType.DMA((2, 2, 2))
        ],
    )(part, qkv, qkv, qkv, gate, strip, own, peer, came_own, came_peer)


def attend_back_kernel(
    q_ref, k_ref, v_ref, prob_ref, go_ref, wide_ref, gq_ref, gk_ref, gv_ref, sums_ref, near_ref
):
    scale = HDIM ** (-0.5)
    blocks = LMAX // TILE
    member = (
        lax.broadcasted_iota(jnp.int32, (AUG, LMAX), 0)
        == lax.broadcasted_iota(jnp.int32, (AUG, LMAX), 1) // TILE
    )
    queries = jnp.concatenate([q_ref[...], member.astype(F32).astype(BF16)], axis=0)
    near = [jnp.zeros((TILE, TILE), F32) for _ in range(3)]
    key_total = jnp.zeros((HDIM + AUG, LMAX), F32)
    val_total = jnp.zeros((HDIM, LMAX), F32)
    for block in range(LMAX // ABLOCK):
        low = block * ABLOCK
        prob = prob_ref[0, :, low : low + ABLOCK]
        grad_out = go_ref[:, low : low + ABLOCK]
        soft = prob.astype(F32)
        grad_prob = dot(v_ref[...], grad_out, TN)
        wide = wide_ref[:, low : low + ABLOCK]
        inner = jnp.sum(grad_out.astype(F32) * wide, axis=0, keepdims=True)
        grad_scores = (soft * (grad_prob - inner)).astype(BF16)
        gq_ref[:, low : low + ABLOCK] = (dot(k_ref[...], grad_scores, NN) * scale).astype(BF16)
        key_total = key_total + dot(queries[:, low : low + ABLOCK], grad_scores, NT)
        val_total = val_total + dot(grad_out, prob, NT)
        for sub in range(ABLOCK // TILE):
            place = block * (ABLOCK // TILE) + sub
            for shift in (-1, 0, 1):
                at = place + shift
                if 0 <= at < blocks:
                    piece = grad_scores[at * TILE : (at + 1) * TILE, sub * TILE : (sub + 1) * TILE]
                    near[shift + 1] = near[shift + 1] + piece.astype(F32)
    gk_ref[...] = (key_total[:HDIM] * scale).astype(BF16)
    gv_ref[...] = val_total.astype(BF16)
    sums = key_total[HDIM : HDIM + blocks]
    sums_ref[0] = sums
    shifts = (
        lax.broadcasted_iota(jnp.int32, (blocks, LMAX), 1) // TILE
        - lax.broadcasted_iota(jnp.int32, (blocks, LMAX), 0)
    )

    def fold(tile):
        return jnp.sum(tile, axis=0, keepdims=True)

    def far(chosen):
        return folded(fold(jnp.where(chosen, sums, 0.0)))

    before, same, after = near
    for sign, base, other, shift in ((-1, 0, before, -1), (1, 16, after, 1)):
        near_offset = sign * offsets(0)
        far_offset = sign * offsets(shift)
        floor = 0 if sign < 0 else 1
        last = fold(jnp.where(near_offset >= floor, same, 0.0)) + fold(
            jnp.where(far_offset >= floor, other, 0.0)
        )
        for count, step in enumerate(NEAR_STEPS):
            following = fold(jnp.where(near_offset >= step, same, 0.0)) + fold(
                jnp.where(far_offset >= step, other, 0.0)
            )
            near_ref[0, base + count : base + count + 1] = last - following
            last = following
        near_ref[0, base + 15 : base + 16] = last + far(sign * shifts >= 2)


def attend_back(side, qkv, prob, grad_attended, wide, heads):
    blocks = LMAX // TILE
    rows = jax.ShapeDtypeStruct((heads * HDIM, LMAX), BF16)
    spec = pl.BlockSpec((HDIM, LMAX), lambda h: (h, 0))
    return call(
        attend_back_kernel,
        "attend_back",
        heads * 8 * LMAX * LMAX * HDIM * 4,
        heads * LMAX * LMAX * 2,
        28,
        side=side,
        grid=(heads,),
        in_specs=[
            spec,
            pl.BlockSpec((HDIM, LMAX), lambda h: (heads + h, 0)),
            pl.BlockSpec((HDIM, LMAX), lambda h: (2 * heads + h, 0)),
            pl.BlockSpec((1, LMAX, LMAX), lambda h: (h, 0, 0)),
            spec,
            spec,
        ],
        out_specs=[
            spec,
            spec,
            spec,
            pl.BlockSpec((1, blocks, LMAX), lambda h: (h, 0, 0)),
            pl.BlockSpec((1, BUCKETS, TILE), lambda h: (h, 0, 0)),
        ],
        out_shape=[
            rows,
            rows,
            rows,
            jax.ShapeDtypeStruct((heads, blocks, LMAX), F32),
            jax.ShapeDtypeStruct((heads, BUCKETS, TILE), F32),
        ],
    )(qkv, qkv, qkv, prob, grad_attended, wide)


def ffn_kernel(gate_ref, up_ref, down_ref, x_ref, cot_ref, hid_ref, gg_ref, gu_ref):
    gate = dot(gate_ref[...], x_ref[...], TN)
    up = dot(up_ref[...], x_ref[...], TN)
    grad = dot(down_ref[...], cot_ref[...], TN)
    square = gate * gate
    bend = jnp.tanh(GELU_C * gate * (1.0 + 0.044715 * square))
    half = 0.5 * (1.0 + bend)
    gelu = gate * half
    slope = half + 0.5 * gate * (1.0 - bend * bend) * (GELU_C * (1.0 + 3 * 0.044715 * square))
    hid_ref[...] = (gelu * up).astype(BF16)
    gg_ref[...] = (grad * up * slope).astype(BF16)
    gu_ref[...] = (grad * gelu).astype(BF16)


def ffn(w_gate, w_up, w_down_t, normed, cot):
    units = w_gate.shape[1]
    width = 256
    weight = pl.BlockSpec((D, width), lambda i: (0, i))
    whole = fixed_spec((D, LMAX))
    out = pl.BlockSpec((width, LMAX), lambda i: (i, 0))
    shape = jax.ShapeDtypeStruct((units, LMAX), BF16)
    return call(
        ffn_kernel,
        "ffn",
        6 * D * units * LMAX,
        3 * D * units * 2 + 2 * D * LMAX * 2 + 3 * units * LMAX * 2,
        28,
        grid=(units // width,),
        in_specs=[weight, weight, weight, whole, whole],
        out_specs=[out, out, out],
        out_shape=[shape, shape, shape],
    )(w_gate, w_up, w_down_t, normed, cot)


def weight_grad_kernel(a_own, a_peer, b_own, b_peer, out_ref):
    total = dot(a_own[...], b_own[...], NT) + dot(a_peer[...], b_peer[...], NT)
    out_ref[...] = total.astype(BF16)


def weight_grad(a_own, a_peer, b_own, b_peer):
    units = a_own.shape[0]
    width = 256
    left = pl.BlockSpec((width, LMAX), lambda i: (i, 0))
    whole = fixed_spec((D, LMAX))
    return call(
        weight_grad_kernel,
        "weight_grad",
        4 * D * units * LMAX,
        4 * D * LMAX + 4 * units * LMAX + 2 * units * D,
        28,
        grid=(units // width,),
        in_specs=[left, left, whole, whole],
        out_specs=pl.BlockSpec((width, D), lambda i: (i, 0)),
        out_shape=jax.ShapeDtypeStruct((units, D), BF16),
    )(a_own, a_peer, b_own, b_peer)


def project_kernel(count, *refs):
    total = dot(refs[0][...], refs[count][...], NN)
    for i in range(1, count):
        total = total + dot(refs[i][...], refs[count + i][...], NN)
    refs[-1][...] = total.astype(refs[-1].dtype)


def project(side, weights, values, dtype):
    count = len(weights)
    units = weights[0].shape[1]
    width = D // 4
    weight = pl.BlockSpec((width, units), lambda i: (i, 0))
    whole = fixed_spec((units, LMAX))
    return call(
        functools.partial(project_kernel, count),
        "project",
        2 * count * D * units * LMAX,
        2 * count * (D * units + units * LMAX) + 4 * D * LMAX,
        28,
        side=side,
        grid=(D // width,),
        in_specs=[weight] * count + [whole] * count,
        out_specs=pl.BlockSpec((width, LMAX), lambda i: (i, 0)),
        out_shape=jax.ShapeDtypeStruct((D, LMAX), dtype),
    )(*weights, *values)


def split_grad_kernel(cut, bits_ref, a_own, a_peer, b_own, b_peer, *refs):
    keep_x, give_x, keep_y, give_y, hold = refs
    total = dot(a_own[...], b_own[...], NT) + dot(a_peer[...], b_peer[...], NT)
    hold[...] = total.reshape(hold.shape).astype(BF16)
    x, y = bits_ref[0], bits_ref[1]
    for other in range(2):
        keep_x[0, other] = hold[other, x, :cut]
        give_x[0, other] = hold[other, 1 - x, :cut]
        keep_y[0, other] = hold[y, other, cut:]
        give_y[0, other] = hold[1 - y, other, cut:]


def split_grad(cut, bits, a_own, a_peer, b_own, b_peer):
    units = a_own.shape[0]
    width = units // 4
    share = width // 4
    left = pl.BlockSpec((width, LMAX), lambda i: (i, 0))

    def out(rows):
        return pl.BlockSpec((1, 2, rows, D), lambda i: (i, 0, 0, 0))

    def shape(rows):
        return jax.ShapeDtypeStruct((4, 2, rows, D), BF16)

    return call(
        functools.partial(split_grad_kernel, cut),
        "weight_grad",
        4 * D * units * LMAX,
        4 * D * LMAX + 4 * units * LMAX + 2 * units * D,
        28,
        grid=(4,),
        in_specs=[SMEM, left, left, whole_spec(b_own), whole_spec(b_peer)],
        out_specs=[out(cut), out(cut), out(share - cut), out(share - cut)],
        out_shape=[shape(cut), shape(cut), shape(share - cut), shape(share - cut)],
        scratch_shapes=[pltpu.VMEM((2, 2, share, D), BF16)],
    )(bits, a_own, a_peer, b_own, b_peer)


def fold_kernel(bit_ref, keep_ref, came_ref, keep_out, give_out):
    mine = bit_ref[0]
    for out, which in ((keep_out, mine), (give_out, 1 - mine)):
        total = keep_ref[:, which].astype(F32) + came_ref[:, which].astype(F32)
        out[...] = total.astype(BF16)


def fold(bit, keep, came):
    outer, _, rows, width = keep.shape
    steps = 2 if outer % 2 == 0 else 1
    block = pl.BlockSpec((outer // steps, 2, rows, width), lambda i: (i, 0, 0, 0))
    out = pl.BlockSpec((outer // steps, rows, width), lambda i: (i, 0, 0))
    shape = jax.ShapeDtypeStruct((outer, rows, width), BF16)
    return call(
        fold_kernel,
        "fold",
        4 * keep.size,
        6 * keep.size,
        16,
        grid=(steps,),
        in_specs=[SMEM, block, block],
        out_specs=[out, out],
        out_shape=[shape, shape],
    )(bit.reshape(1), keep, came)


def across(values, bit):
    size = lax.axis_size("dp")
    return lax.ppermute(values, "dp", [(i, i ^ (1 << bit)) for i in range(size)])


def bit_of(bit):
    return (lax.axis_index("dp") >> bit) & 1


def join_kernel(count, bit_ref, *refs):
    keep_out, give_out = refs[4 * count :]
    mine = bit_ref[0]
    for i in range(count):
        keep_x, keep_y, came_x, came_y = refs[4 * i : 4 * i + 4]
        cut = keep_x.shape[2]
        for out, which in ((keep_out, mine), (give_out, 1 - mine)):
            total = keep_x[0, which].astype(F32) + came_x[0, which].astype(F32)
            out[0, i, :cut] = total.astype(BF16)
            total = keep_y[0, which].astype(F32) + came_y[0, which].astype(F32)
            out[0, i, cut:] = total.astype(BF16)


def join(bit, groups):
    count = len(groups)
    specs, args = [], []
    for group in groups:
        for array in group:
            rows = array.shape[1]
            specs.append(pl.BlockSpec((1, 2, rows, D), lambda i: (i, 0, 0, 0)))
            args.append(array.reshape(2, 2, rows, D))
    share = groups[0][0].shape[1] + groups[0][1].shape[1]
    out = pl.BlockSpec((1, count, share, D), lambda i: (i, 0, 0, 0))
    shape = jax.ShapeDtypeStruct((2, count, share, D), BF16)
    return call(
        functools.partial(join_kernel, count),
        "join",
        8 * count * share * D,
        24 * count * share * D,
        24,
        grid=(2,),
        in_specs=[SMEM] + specs,
        out_specs=[out, out],
        out_shape=[shape, shape],
    )(bit.reshape(1), *args)


def finish_groups(groups):
    count = len(groups)
    keep, give = join(bit_of(2), groups)
    share = keep.shape[2]
    came = across(give, 2)
    keep, give = fold(
        bit_of(3), keep.reshape(1, 2, count * share, D), came.reshape(1, 2, count * share, D)
    )
    came = across(give, 3)
    keep, came = keep.reshape(count, share, D), came.reshape(count, share, D)
    return [keep[i].astype(F32) + came[i].astype(F32) for i in range(count)]


def stacked(values, came, mine, axis):
    return jnp.where(mine == 0, jnp.stack([values, came], axis), jnp.stack([came, values], axis))


def sum_everywhere(keep, came):
    bits = lax.axis_size("dp").bit_length() - 1
    rows = keep.shape[1] // 4
    keep, came = (v.reshape(4, 2, 2, rows, D) for v in (keep, came))
    keep_x, give_x = fold(
        bit_of(0), keep[:2].reshape(4, 2, rows, D), came[:2].reshape(4, 2, rows, D)
    )
    keep_y, give_y = fold(
        bit_of(1), keep[2:].reshape(2, 2, 2 * rows, D), came[2:].reshape(2, 2, 2 * rows, D)
    )
    came_x, came_y = across(give_x, 0), across(give_y, 1)
    keep_x, give_x = fold(
        bit_of(1), keep_x.reshape(2, 2, rows, D), came_x.reshape(2, 2, rows, D)
    )
    keep_y, give_y = fold(
        bit_of(0), keep_y.reshape(2, 2, rows, D), came_y.reshape(2, 2, rows, D)
    )
    came_x, came_y = across(give_x, 1), across(give_y, 0)
    keep = jnp.concatenate([keep_x, keep_y], axis=0).reshape(2, 2, rows, D)
    came = jnp.concatenate([came_x, came_y], axis=0).reshape(2, 2, rows, D)
    keep, give = fold(bit_of(2), keep, came)
    came = across(give, 2)
    keep, give = fold(bit_of(3), keep.reshape(1, 2, rows, D), came.reshape(1, 2, rows, D))
    came = across(give, 3)
    total = (keep.astype(F32) + came.astype(F32)).astype(BF16)
    for bit in range(4, bits):
        total = (total.astype(F32) + across(total, bit).astype(F32)).astype(BF16)
    total = stacked(total, across(total, 3), bit_of(3), 1)
    total = stacked(total, across(total, 2), bit_of(2), 2).reshape(4, rows, D)
    total_x, total_y = total[:2], total[2:]
    total_x = stacked(total_x, across(total_x, 1), bit_of(1), 1)
    total_y = stacked(total_y, across(total_y, 0), bit_of(0), 1)
    total_x = stacked(total_x, across(total_x, 0), bit_of(0), 2)
    total_y = stacked(total_y, across(total_y, 1), bit_of(1), 1)
    return [v.reshape(4 * rows, D).astype(F32) for v in (*total_x, *total_y)]


def sum_small(values):
    bits = lax.axis_size("dp").bit_length() - 1
    values = values + swap(values)
    for bit in range(bits):
        values = values + across(values, bit)
    return values


def halve(values, order):
    size = lax.axis_size("dp")
    bits = size.bit_length() - 1
    index = lax.axis_index("dp")
    rows = values.shape[0] // size
    values = values.reshape((2,) * bits + (rows, values.shape[1]))
    left = list(range(bits - 1, -1, -1))
    for step, bit in enumerate(order):
        axis = left.index(bit)
        left.pop(axis)
        mine = (index >> bit) & 1
        keep = lax.dynamic_index_in_dim(values, mine, axis, keepdims=False)
        give = lax.dynamic_index_in_dim(values, 1 - mine, axis, keepdims=False)
        came = lax.ppermute(give, "dp", [(i, i ^ (1 << bit)) for i in range(size)])
        total = keep.astype(F32) + came.astype(F32)
        values = total if step == bits - 1 else total.astype(BF16)
    return values


def swap(values):
    return lax.ppermute(values, "mp", [(0, 1), (1, 0)])


def body(
    tokens,
    cotangent,
    lengths,
    keep_mask,
    ln_attn,
    w_query,
    w_key,
    w_value,
    w_attn_out,
    rel_table,
    w_delete,
    ln_ffn,
    w_gate,
    w_up,
    w_ffn_out,
):
    dev_count = lax.axis_size("dp")
    bits = dev_count.bit_length() - 1
    part = lax.axis_index("mp")
    inner = 2 * w_query.shape[1]
    heads = inner // HDIM
    half = tokens.shape[1]
    first = part == 0
    part_ref = part.reshape(1).astype(jnp.int32)

    def in_parts(own, peer, axis):
        return jnp.where(
            first, jnp.concatenate([own, peer], axis), jnp.concatenate([peer, own], axis)
        )

    def home(values):
        mine = lax.dynamic_slice_in_dim(values, part * half, half, 0)
        other = lax.dynamic_slice_in_dim(values, (1 - part) * half, half, 0)
        return spread(part_ref, slot, mine, swap(other)).T

    own_weights = (w_query.T, w_key.T, w_value.T, w_attn_out)
    slot, count, stack = places(part_ref, lengths, keep_mask.reshape(1, ROWS_DEV), own_weights)
    came_stack = swap(stack)
    own_tokens, peer_tokens = compact(part_ref, slot, tokens.T)
    came_tokens = swap(peer_tokens)
    own_cot, peer_cot, w_qkv, w_out = compact_join(
        part_ref, slot, cotangent.T, stack, came_stack
    )
    came_cot_own, came_cot_peer = swap(peer_cot), swap(own_cot)
    table = in_parts(rel_table, swap(rel_table), 1)
    strip = bias_strip(table, heads)
    columns = jnp.stack([ln_attn, ln_ffn, w_delete.astype(F32)], axis=1)

    state, normed_one, qkv, gate_rows, del_logit, scale_one = input_part(
        part_ref, own_tokens, came_tokens, columns, w_qkv, count
    )
    prob, attended, wide, cot_own, cot_peer = attend(
        part_ref, qkv, gate_rows, strip, own_cot, peer_cot, came_cot_own, came_cot_peer, heads
    )
    mid, normed_two, scale_two = middle_part(w_out, attended, state, columns)
    normed_two_peer = swap(normed_two)
    w_down_t = w_ffn_out.T
    hid_own, gg_own, gu_own = ffn(w_gate, w_up, w_down_t, normed_two, cot_own)
    hid_peer, gg_peer, gu_peer = ffn(w_gate, w_up, w_down_t, normed_two_peer, cot_peer)

    share = w_gate.shape[1] // dev_count
    split = bits == 4 and share % 16 == 0
    if split:
        cut = (share // 2 + 15) // 16 * 16
        my_bits = jnp.stack([bit_of(0), bit_of(1)])
        make = functools.partial(split_grad, cut, my_bits)
    else:
        make = weight_grad

    def first_step(pieces):
        if not split:
            return ()
        keep_x, give_x, keep_y, give_y = pieces
        return (
            (bit_of(1), keep_x, across(give_x, 0)),
            (bit_of(0), keep_y, across(give_y, 1)),
        )

    def second_step(folded_pieces):
        keep_x, give_x, keep_y, give_y = folded_pieces
        return keep_x, keep_y, across(give_x, 1), across(give_y, 0)

    def run(kernel, side, *args):
        out = kernel(side, *args)
        return out if side else (out, ())

    part_down = make(hid_own, hid_peer, cot_own, cot_peer)
    side_down = first_step(part_down)
    part_gate = make(gg_own, gg_peer, normed_two, normed_two_peer)
    side_gate = first_step(part_gate)
    part_up = make(gu_own, gu_peer, normed_two, normed_two_peer)
    side_up = first_step(part_up)
    gg_peer, gu_peer, gg_own, gu_own, _ = lax.optimization_barrier(
        (gg_peer, gu_peer, gg_own, gu_own, part_up)
    )
    back_peer, fold_down = run(project, side_down, (w_gate, w_up), (gg_peer, gu_peer), BF16)
    grad_mid, grad_attn, grad_attended, sum_ffn = middle_back(
        w_gate, w_up, gg_own, gu_own, swap(back_peer), mid, cot_own, columns, scale_two, w_out
    )
    (grad_q, grad_k, grad_v, sums, near), fold_gate = run(
        attend_back, side_gate, qkv, prob, grad_attended, wide, heads
    )
    keep, give = head_grads(part_ref, grad_q, grad_k, grad_v, normed_one, attended, grad_attn)
    back_args = (
        grad_q, grad_k, grad_v, w_qkv, normed_one, state, grad_mid, scale_one, del_logit, sums, columns
    )
    if split:
        grad_down, grad_gate = finish_groups([second_step(fold_down), second_step(fold_gate)])
        (_, keep_x, came_x), (_, keep_y, came_y) = side_up
        totals, grad_up, small, state_own, state_came = tail(
            keep, give, (keep_x, came_x), (keep_y, came_y), sum_ffn,
            near.reshape(heads * BUCKETS, TILE), *back_args,
        )
        total_q, total_v, total_k, total_out = totals.reshape(4, inner // 2, D).astype(F32)
        grad_tokens = spread(part_ref, slot, state_own, state_came).T
        grad_ln_ffn, grad_ln_attn, grad_w_delete = small[0], small[1], small[2]
        grad_table = small[3, : heads * BUCKETS].reshape(heads, BUCKETS).T
    else:
        total_q, total_v, total_k, total_out = sum_everywhere(keep, swap(give))
        order = tuple(range(bits))
        grad_down, grad_gate, grad_up = (halve(v, order) for v in (part_down, part_gate, part_up))
        grad_state, sum_attn, sum_delete = input_back((), *back_args)
        grad_tokens = home(grad_state)
        grad_table = jnp.sum(near, axis=2).T
        small = jnp.concatenate(
            [jnp.sum(v, axis=1) for v in (sum_ffn, sum_attn, sum_delete)]
            + [grad_table.reshape(-1)]
        )
        small = sum_small(small)
        grad_ln_ffn, grad_ln_attn = small[:D], small[D : 2 * D]
        grad_w_delete = small[2 * D : 3 * D]
        grad_table = small[3 * D :].reshape(BUCKETS, heads)

    mixed_peer = project((), (w_down_t,), (hid_peer,), BF16)
    mixed = mixed_part(w_down_t, hid_own, swap(mixed_peer), mid)

    def own_half(values):
        return lax.dynamic_slice_in_dim(values, part * half, half, 0)

    return (
        home(mixed),
        grad_tokens,
        own_half(grad_ln_attn),
        total_q.T,
        total_k.T,
        total_v.T,
        total_out,
        lax.dynamic_slice_in_dim(grad_table, part * (heads // 2), heads // 2, 1),
        grad_w_delete,
        own_half(grad_ln_ffn),
        grad_gate.T,
        grad_up.T,
        grad_down,
    )


def solution(mesh):
    return jax.shard_map(
        body,
        mesh=mesh,
        in_specs=(
            P("dp", "mp"),
            P("dp", "mp"),
            P("dp"),
            P("dp"),
            P(),
            P(None, "mp"),
            P(None, "mp"),
            P(None, "mp"),
            P("mp", None),
            P(None, "mp"),
            P(),
            P(),
            P(None, "mp"),
            P(None, "mp"),
            P("mp", None),
        ),
        out_specs=(
            P("dp", "mp"),
            P("dp", "mp"),
            P("mp"),
            P(None, "mp"),
            P(None, "mp"),
            P(None, "mp"),
            P("mp", None),
            P(None, "mp"),
            P(),
            P("mp"),
            P(None, ("mp", "dp")),
            P(None, ("mp", "dp")),
            P(("mp", "dp"), None),
        ),
        check_vma=False,
    )
```

```python
import functools

import jax
import jax.numpy as jnp
import numpy as np
from jax import lax
from jax.experimental import pallas as pl
from jax.experimental.pallas import tpu as pltpu
from jax.sharding import PartitionSpec as P

D = 1472
HDIM = 64
BUCKETS = 32
LMAX = 1024
ROWS_DEV = 2048

EPSILON = 1e-06
DELETE_DEPTH = 4.0
NEG_LARGE = -1e30
NEAR_STEPS = (1, 2, 3, 4, 5, 6, 7, 8, 12, 16, 23, 32, 46, 64, 91)
TILE = 128
QBLOCK = 256
ABLOCK = 512
AUG = 16
F32 = jnp.float32
BF16 = jnp.bfloat16
GELU_C = float(np.sqrt(2.0 / np.pi))

NN = (((1,), (0,)), ((), ()))
TN = (((0,), (0,)), ((), ()))
NT = (((1,), (1,)), ((), ()))


def dot(a, b, dims):
    return lax.dot_general(a, b, dims, preferred_element_type=F32)


def with_side(kernel, inputs, outputs, pairs, bits_ref, *refs):
    first = inputs + 2 * pairs
    last = first + outputs + 2 * pairs
    kernel(*refs[:inputs], *refs[first : first + outputs], *refs[last:])
    for pair in range(pairs):
        keep_ref, came_ref = refs[inputs + 2 * pair : inputs + 2 * pair + 2]
        outs = refs[first + outputs + 2 * pair : first + outputs + 2 * pair + 2]
        mine = bits_ref[pair]
        for out, which in zip(outs, (mine, 1 - mine)):
            total = keep_ref[:, which].astype(F32) + came_ref[:, which].astype(F32)
            out[...] = total.astype(BF16)


def call(kernel, name, flops, nbytes, limit, side=(), **kw):
    for _, keep, came in side:
        nbytes += 6 * keep.size
    extra = ()
    outputs = 1
    if side:
        single = not isinstance(kw["out_shape"], list)
        out_specs = [kw["out_specs"]] if single else list(kw["out_specs"])
        out_shape = [kw["out_shape"]] if single else list(kw["out_shape"])
        outputs, inputs = len(out_shape), len(kw["in_specs"])
        in_specs = list(kw["in_specs"])
        for _, keep, came in side:
            outer, _, rows, width = keep.shape
            block = pl.BlockSpec(
                (1, 2, rows, width), lambda i, n=outer: (jnp.minimum(i, n - 1), 0, 0, 0)
            )
            out = pl.BlockSpec(
                (1, rows, width), lambda i, n=outer: (jnp.minimum(i, n - 1), 0, 0)
            )
            in_specs += [block, block]
            out_specs += [out, out]
            out_shape += [jax.ShapeDtypeStruct((outer, rows, width), BF16)] * 2
            extra += (keep, came)
        kernel = functools.partial(with_side, kernel, inputs, outputs, len(side))
        kw.update(in_specs=[SMEM] + in_specs, out_specs=out_specs, out_shape=out_shape)
    run = pl.pallas_call(
        kernel,
        name=name,
        cost_estimate=pl.CostEstimate(
            flops=int(flops), bytes_accessed=int(nbytes), transcendentals=0
        ),
        compiler_params=pltpu.CompilerParams(vmem_limit_bytes=56 << 20),
        **kw,
    )
    if not side:
        return run

    def launch(*args):
        out = run(jnp.stack([bit for bit, _, _ in side]), *args, *extra)
        main = out[0] if single else out[:outputs]
        return main, out[outputs:]

    return launch


VMEM = pl.BlockSpec(memory_space=pltpu.VMEM)
SMEM = pl.BlockSpec(memory_space=pltpu.SMEM)
ANY = pl.BlockSpec(memory_space=pl.ANY)


def place_kernel(
    part_ref, length_ref, mask_ref, q_ref, k_ref, v_ref, out_ref, slot_ref, count_ref, stack_ref
):
    for i, ref in enumerate((q_ref, k_ref, v_ref, out_ref)):
        stack_ref[i] = ref[...]
    mask = mask_ref[...]
    rows = lax.broadcasted_iota(jnp.int32, (1, ROWS_DEV), 1)
    first = (rows < length_ref[0]).astype(jnp.int32)
    pieces = []
    before = jnp.zeros((1, 1), F32)
    ahead = lax.broadcasted_iota(jnp.int32, (QBLOCK, QBLOCK), 0) <= lax.broadcasted_iota(
        jnp.int32, (QBLOCK, QBLOCK), 1
    )
    ahead = ahead.astype(F32).astype(BF16)
    flags = mask.astype(F32).astype(BF16)
    for block in range(ROWS_DEV // QBLOCK):
        part = flags[:, block * QBLOCK : (block + 1) * QBLOCK]
        ranks = dot(jnp.broadcast_to(part, (16, QBLOCK)), ahead, NN)[:1] + before
        before = ranks[:, QBLOCK - 1 :]
        pieces.append(ranks)
    ranks = jnp.concatenate(pieces, axis=1).astype(jnp.int32)
    kept_first = jnp.sum(mask * first, axis=1, keepdims=True)
    total = jnp.sum(mask, axis=1, keepdims=True)
    rank = ranks - 1 + jnp.where(first > 0, 0, LMAX - kept_first)
    slot_ref[...] = jnp.where(mask > 0, rank, -1)
    count = jnp.where(part_ref[0] == 0, kept_first, total - kept_first)
    count_ref[...] = jnp.broadcast_to(count, (1, 128))


def places(part, lengths, mask, weights):
    return call(
        place_kernel,
        "places",
        1e6,
        1e5,
        16,
        in_specs=[SMEM, SMEM, VMEM] + [VMEM] * 4,
        out_specs=[VMEM, VMEM, VMEM],
        out_shape=[
            jax.ShapeDtypeStruct((1, ROWS_DEV), jnp.int32),
            jax.ShapeDtypeStruct((1, 128), jnp.int32),
            jax.ShapeDtypeStruct((4, *weights[0].shape), BF16),
        ],
    )(part, lengths, mask, *weights)


def compact_half(item, slot_ref, x_ref, out_ref):
    for block in range(LMAX // QBLOCK):
        width = ROWS_DEV - 512 - block * QBLOCK
        start = pl.multiple_of(item * 512 + block * QBLOCK, 128)
        ids = item * LMAX + block * QBLOCK + lax.broadcasted_iota(jnp.int32, (QBLOCK, 1), 0)
        hot = (slot_ref[:, pl.ds(start, width)] == ids).astype(F32).astype(BF16)
        rows = dot(x_ref[:, pl.ds(start, width)], hot, NT)
        out_ref[:, block * QBLOCK : (block + 1) * QBLOCK] = rows.astype(BF16)


def compact_kernel(part_ref, slot_ref, x_ref, own_ref, peer_ref):
    compact_half(part_ref[0], slot_ref, x_ref, own_ref)
    compact_half(1 - part_ref[0], slot_ref, x_ref, peer_ref)


def halves(part, own, came, whole, hold, sems):
    size = own.shape[0]
    copies_in, copies_out = [], []
    for i, (ref, place) in enumerate(((own, part), (came, 1 - part))):
        copies_in.append(pltpu.make_async_copy(ref, hold.at[i], sems.at[0, i]))
        target = whole.at[pl.ds(pl.multiple_of(place * size, 16), size)]
        copies_out.append(pltpu.make_async_copy(hold.at[i], target, sems.at[1, i]))
    return copies_in, copies_out


def compact_join_kernel(
    part_ref, slot_ref, x_ref, stack_ref, came_ref, own_ref, peer_ref, qkv_ref, out_ref, hold, sems
):
    part = part_ref[0]
    inner = out_ref.shape[0]
    copies_in, copies_out = [], []
    for i in range(4):
        whole = qkv_ref.at[pl.ds(i * inner, inner)] if i < 3 else out_ref
        ins, outs = halves(part, stack_ref.at[i], came_ref.at[i], whole, hold.at[i], sems.at[i])
        copies_in += ins
        copies_out += outs
    for copy in copies_in:
        copy.start()
    compact_half(part, slot_ref, x_ref, own_ref)
    for copy, following in zip(copies_in, copies_out):
        copy.wait()
        following.start()
    compact_half(1 - part, slot_ref, x_ref, peer_ref)
    for copy in copies_out:
        copy.wait()


def compact_join(part, slot, columns, stack, came):
    width = columns.shape[0]
    inner = 2 * stack.shape[1]
    shape = jax.ShapeDtypeStruct((width, LMAX), BF16)
    return call(
        compact_join_kernel,
        "compact_join",
        2 * width * 2 * 4608 * 256,
        width * 2048 * 4,
        24,
        in_specs=[SMEM, VMEM, VMEM, ANY, ANY],
        out_specs=[VMEM, VMEM, ANY, ANY],
        out_shape=[
            shape,
            shape,
            jax.ShapeDtypeStruct((3 * inner, D), BF16),
            jax.ShapeDtypeStruct((inner, D), BF16),
        ],
        scratch_shapes=[
            pltpu.VMEM((4, 2, inner // 2, D), BF16), pltpu.SemaphoreType.DMA((4, 2, 2))
        ],
    )(part, slot, columns, stack, came)


def compact(part, slot, columns):
    width = columns.shape[0]
    shape = jax.ShapeDtypeStruct((width, LMAX), BF16)
    return call(
        compact_kernel,
        "compact",
        2 * width * 2 * 4608 * 256,
        width * 2048 * 4,
        16,
        in_specs=[SMEM, VMEM, VMEM],
        out_specs=[VMEM, VMEM],
        out_shape=[shape, shape],
    )(part, slot, columns)


def spread_kernel(part_ref, slot_ref, own_ref, peer_ref, out_ref):
    first = part_ref[0] == 0
    items = (
        jnp.where(first, own_ref[...], peer_ref[...]),
        jnp.where(first, peer_ref[...], own_ref[...]),
    )
    for block in range(ROWS_DEV // QBLOCK):
        end = (block + 1) * QBLOCK
        slots = slot_ref[:, end - QBLOCK : end]
        total = None
        for item in range(2):
            reach = min(end - 512 * item, LMAX)
            if reach <= 0 or (item == 0 and end > LMAX):
                continue
            ids = item * LMAX + lax.broadcasted_iota(jnp.int32, (reach, 1), 0)
            hot = (slots == ids).astype(F32).astype(BF16)
            part = dot(items[item][:, :reach], hot, NN)
            total = part if total is None else total + part
        out_ref[:, end - QBLOCK : end] = total.astype(BF16)


def spread(part, slot, own, peer):
    width = own.shape[0]
    return call(
        spread_kernel,
        "spread",
        2 * width * 7168 * 256,
        width * 2048 * 4,
        16,
        in_specs=[SMEM, VMEM, VMEM, VMEM],
        out_specs=VMEM,
        out_shape=jax.ShapeDtypeStruct((width, ROWS_DEV), BF16),
    )(part, slot, own, peer)


COLUMNS = 3
ROWS = pl.BlockSpec((D, QBLOCK), lambda i: (0, i))
LINE = pl.BlockSpec((1, QBLOCK), lambda i: (0, i))
COLUMN = pl.BlockSpec((D, COLUMNS), lambda i: (0, 0))
SUMS = pl.BlockSpec((D, 128), lambda i: (0, 0))


def fixed_spec(shape):
    return pl.BlockSpec(shape, lambda i: (0,) * len(shape), pipeline_mode=pl.Buffered(1))


def whole_spec(array):
    return fixed_spec(array.shape)


def line(rows=1, dtype=F32):
    return jax.ShapeDtypeStruct((rows, LMAX), dtype)


def folded(values):
    return sum(values[:, i * 128 : (i + 1) * 128] for i in range(values.shape[1] // 128))


def input_kernel(
    part_ref, own_ref, came_ref, gain_ref, weight_ref, count_ref,
    state_ref, normed_ref, qkv_ref, gate_ref, logit_ref, scale_ref,
):
    first = part_ref[0] == 0
    own, came = own_ref[...], came_ref[...]
    half = own.shape[0]
    state_ref[:half] = jnp.where(first, own, came)
    state_ref[half:] = jnp.where(first, came, own)
    state = state_ref[...].astype(F32)
    scale = lax.rsqrt(jnp.sum(state * state, axis=0, keepdims=True) / D + EPSILON)
    normed = (state * scale * gain_ref[:, 0:1]).astype(BF16)
    normed_ref[...] = normed
    scale_ref[...] = scale
    qkv_ref[...] = dot(weight_ref[...], normed, NN).astype(BF16)
    logit = jnp.sum(normed.astype(F32) * gain_ref[:, 2:3], axis=0, keepdims=True)
    logit_ref[...] = logit
    gate = -DELETE_DEPTH * jax.nn.sigmoid(-logit)
    rows = pl.program_id(0) * QBLOCK + lax.broadcasted_iota(jnp.int32, (1, QBLOCK), 1)
    gate = jnp.where(rows < count_ref[:, :1], gate, NEG_LARGE)
    place = lax.broadcasted_iota(jnp.int32, (AUG, QBLOCK), 0)
    gate_ref[...] = jnp.where(place == 0, gate, 0.0).astype(BF16)


def input_part(part, own, came, gain, weights, count):
    inner = weights.shape[0]
    half = pl.BlockSpec((own.shape[0], QBLOCK), lambda i: (0, i))
    return call(
        input_kernel,
        "norm_project",
        2 * D * LMAX * weights.shape[0],
        D * LMAX * 10,
        24,
        grid=(LMAX // QBLOCK,),
        in_specs=[SMEM, half, half, COLUMN, whole_spec(weights), whole_spec(count)],
        out_specs=[
            ROWS,
            ROWS,
            pl.BlockSpec((inner, QBLOCK), lambda i: (0, i)),
            pl.BlockSpec((AUG, QBLOCK), lambda i: (0, i)),
            LINE,
            LINE,
        ],
        out_shape=[line(D, BF16), line(D, BF16), line(inner, BF16), line(AUG, BF16), line(), line()],
    )(part, own, came, gain, weights, count)


def middle_kernel(weight_ref, attended_ref, state_ref, gain_ref, mid_ref, normed_ref, scale_ref):
    mid = state_ref[...].astype(F32) + dot(weight_ref[...], attended_ref[...], TN)
    scale = lax.rsqrt(jnp.sum(mid * mid, axis=0, keepdims=True) / D + EPSILON)
    mid_ref[...] = mid
    scale_ref[...] = scale
    normed_ref[...] = (mid * scale * gain_ref[:, 1:2]).astype(BF16)


def middle_part(weights, attended, state, gain):
    inner = attended.shape[0]
    return call(
        middle_kernel,
        "attention_out_norm",
        2 * D * LMAX * inner,
        D * LMAX * 8,
        24,
        grid=(LMAX // QBLOCK,),
        in_specs=[
            whole_spec(weights),
            pl.BlockSpec((inner, QBLOCK), lambda i: (0, i)),
            ROWS,
            COLUMN,
        ],
        out_specs=[ROWS, ROWS, LINE],
        out_shape=[line(D), line(D, BF16), line()],
    )(weights, attended, state, gain)


def middle_back_kernel(
    gate_ref, up_ref, gg_ref, gu_ref, came_ref, mid_ref, cot_ref, gain_ref, scale_ref, weight_ref,
    grad_mid_ref, grad_attn_ref, attended_ref, sums_ref,
):
    grad = dot(gate_ref[...], gg_ref[...], NN) + dot(up_ref[...], gu_ref[...], NN)
    grad = grad + came_ref[...].astype(F32)
    mid, scale = mid_ref[...], scale_ref[...]
    weighted = grad * gain_ref[:, 1:2]
    inner = jnp.sum(weighted * mid, axis=0, keepdims=True)
    grad_mid = (
        cot_ref[...].astype(F32) + scale * weighted - mid * (scale * scale * scale * inner / D)
    )
    grad_mid_ref[...] = grad_mid
    grad_attn = grad_mid.astype(BF16)
    grad_attn_ref[...] = grad_attn
    attended_ref[...] = dot(weight_ref[...], grad_attn, NN).astype(BF16)

    @pl.when(pl.program_id(0) == 0)
    def _():
        sums_ref[...] = jnp.zeros_like(sums_ref)

    sums_ref[...] += folded(grad * (mid * scale))


def middle_back(w_gate, w_up, gg, gu, came, mid, cot, gain, scale, w_out):
    inner, units = w_out.shape[0], w_gate.shape[1]
    unit_rows = pl.BlockSpec((units, QBLOCK), lambda i: (0, i))
    return call(
        middle_back_kernel,
        "norm_back",
        4 * D * LMAX * units,
        D * LMAX * 20 + 4 * D * units,
        44,
        grid=(LMAX // QBLOCK,),
        in_specs=[
            whole_spec(w_gate), whole_spec(w_up), unit_rows, unit_rows, ROWS, ROWS, ROWS, COLUMN,
            LINE, whole_spec(w_out),
        ],
        out_specs=[ROWS, ROWS, pl.BlockSpec((inner, QBLOCK), lambda i: (0, i)), SUMS],
        out_shape=[
            line(D), line(D, BF16), line(inner, BF16), jax.ShapeDtypeStruct((D, 128), F32),
        ],
    )(w_gate, w_up, gg, gu, came, mid, cot, gain, scale, w_out)


def input_back_block(q, k, v, weight_ref, normed, state, grad_mid, scale, logit, sums, columns):
    heads = sums.shape[0]
    gate = sums[0]
    for head in range(1, heads):
        gate = gate + sums[head]
    gate = jnp.sum(gate, axis=0, keepdims=True)
    grad_logit = gate * DELETE_DEPTH * jax.nn.sigmoid(logit) * jax.nn.sigmoid(-logit)
    inner = q.shape[0]
    grad = dot(weight_ref[:inner], q, TN)
    grad = grad + dot(weight_ref[inner : 2 * inner], k, TN)
    grad = grad + dot(weight_ref[2 * inner : 3 * inner], v, TN)
    grad = grad + columns[:, 2:3] * grad_logit
    state = state.astype(F32)
    weighted = grad * columns[:, 0:1]
    total = jnp.sum(weighted * state, axis=0, keepdims=True)
    grad_state = grad_mid + scale * weighted - state * (scale * scale * scale * total / D)
    gain_part = folded(grad * (state * scale))
    delete_part = folded(normed.astype(F32) * grad_logit)
    return grad_state.astype(BF16), gain_part, delete_part


def input_back_kernel(
    q_ref, k_ref, v_ref, weight_ref, normed_ref, state_ref, grad_mid_ref, scale_ref, logit_ref,
    sums_ref, columns_ref, grad_ref, gain_sum_ref, delete_sum_ref,
):
    grad_ref[...], gain_part, delete_part = input_back_block(
        q_ref[...], k_ref[...], v_ref[...], weight_ref, normed_ref[...], state_ref[...],
        grad_mid_ref[...], scale_ref[...], logit_ref[...], sums_ref[...], columns_ref[...],
    )

    @pl.when(pl.program_id(0) == 0)
    def _():
        gain_sum_ref[...] = jnp.zeros_like(gain_sum_ref)
        delete_sum_ref[...] = jnp.zeros_like(delete_sum_ref)

    gain_sum_ref[...] += gain_part
    delete_sum_ref[...] += delete_part


def input_back(side, q, k, v, weights, normed, state, grad_mid, scale, logit, sums, gain):
    inner = q.shape[0]
    head_rows = pl.BlockSpec((inner, QBLOCK), lambda i: (0, i))
    return call(
        input_back_kernel,
        "project_norm_back",
        6 * D * LMAX * inner,
        D * LMAX * 12,
        28,
        side=side,
        grid=(LMAX // QBLOCK,),
        in_specs=[
            head_rows, head_rows, head_rows, whole_spec(weights), ROWS, ROWS, ROWS, LINE, LINE,
            pl.BlockSpec((sums.shape[0], sums.shape[1], QBLOCK), lambda i: (0, 0, i)),
            COLUMN,
        ],
        out_specs=[ROWS, SUMS, SUMS],
        out_shape=[
            line(D, BF16),
            jax.ShapeDtypeStruct((D, 128), F32),
            jax.ShapeDtypeStruct((D, 128), F32),
        ],
    )(q, k, v, weights, normed, state, grad_mid, scale, logit, sums, gain)


def mixed_kernel(down_ref, hid_ref, came_ref, mid_ref, out_ref):
    mixed = mid_ref[...] + dot(down_ref[...], hid_ref[...], NN)
    out_ref[...] = (mixed + came_ref[...].astype(F32)).astype(BF16)


def mixed_part(down, hid, came, mid):
    width = D // 4
    units = down.shape[1]
    rows = pl.BlockSpec((width, LMAX), lambda i: (i, 0))
    return call(
        mixed_kernel,
        "mixed",
        2 * D * LMAX * units,
        D * LMAX * 8 + D * units * 2,
        24,
        grid=(D // width,),
        in_specs=[pl.BlockSpec((width, units), lambda i: (i, 0)), whole_spec(hid), rows, rows],
        out_specs=rows,
        out_shape=line(D, BF16),
    )(down, hid, came, mid)


def head_grad_kernel(part_ref, q_ref, v_ref, k_ref, attended_ref, normed_ref, back_ref, *outs):
    keep_ref, give_ref, hold = outs
    part = part_ref[0]
    rows = hold.shape[0] // 2
    pieces = (
        (q_ref, normed_ref), (v_ref, normed_ref), (k_ref, normed_ref), (attended_ref, back_ref),
    )
    for place, (left, right) in enumerate(pieces):
        hold[...] = dot(left[...], right[...], NT).astype(BF16)
        keep_ref[place] = hold[pl.ds(pl.multiple_of(part * rows, 16), rows)]
        give_ref[place] = hold[pl.ds(pl.multiple_of((1 - part) * rows, 16), rows)]


def head_grads(part, q, k, v, normed, attended, back):
    inner = q.shape[0]
    shape = jax.ShapeDtypeStruct((4, inner // 2, D), BF16)
    return call(
        head_grad_kernel,
        "head_grads",
        8 * D * LMAX * inner,
        D * LMAX * 4 + 4 * LMAX * inner * 2 + 16 * inner * D,
        36,
        in_specs=[SMEM] + [VMEM] * 6,
        out_specs=[VMEM, VMEM],
        out_shape=[shape, shape],
        scratch_shapes=[pltpu.VMEM((inner, D), BF16)],
    )(part, q, v, k, attended, normed, back)


MESH = pl.DeviceIdType.MESH


class Sender:
    def __init__(self, send_sems, recv_sems):
        self.send_sems, self.recv_sems, self.made = send_sems, recv_sems, []

    def start(self, source, target, device):
        place = len(self.made)
        copy = pltpu.make_async_remote_copy(
            src_ref=source,
            dst_ref=target,
            send_sem=self.send_sems.at[place],
            recv_sem=self.recv_sems.at[place],
            device_id=device,
            device_id_type=MESH,
        )
        copy.start()
        self.made.append(copy)
        return copy

    def finish(self):
        for copy in self.made:
            copy.wait_send()


def arrived(copies):
    for copy in copies:
        copy.wait_recv()


def plus(first, *others):
    total = first.astype(F32)
    for other in others:
        total = total + other.astype(F32)
    return total


def neighbours():
    me, part = lax.axis_index("dp"), lax.axis_index("mp")
    x, y, z = me % 2, (me // 2) % 2, me // 4
    across_x, across_y = 1 - 2 * x, 2 - 4 * y
    planes = [(z + k) % 4 for k in range(1, 4)]
    return dict(
        x=x,
        y=y,
        z=z,
        part=part,
        planes=planes,
        to_core=(me, 1 - part),
        to_x=(me + across_x, part),
        to_y=(me + across_y, part),
        to_corner=(me + across_x + across_y, part),
        to_plane=[(p * 4 + me % 4, part) for p in planes],
    )


def meet(devices):
    barrier = pltpu.get_barrier_semaphore()
    for device in devices:
        pl.semaphore_signal(barrier, inc=1, device_id=device, device_id_type=MESH)
    pl.semaphore_wait(barrier, len(devices))


CHUNK = 16


def tail_kernel(
    keep_ref, give_ref, keep_x, came_x, keep_y, came_y, ffn_sum_ref, near_ref,
    q_ref, k_ref, v_ref, weight_ref, normed_ref, state_ref, grad_mid_ref, scale_ref, logit_ref,
    sums_ref, columns_ref,
    out_ref, share_ref, vector_ref, own_ref, came_grad_ref,
    came_ref, total, from_x, from_y, sum_x, sum_y, last_x, last_y, plane_sum, from_planes,
    give_x, give_y, second_x, second_y, whole, from_whole,
    vector, vector_core, vector_near, vector_far, grad_state, send_sems, recv_sems,
):
    at = neighbours()
    x, y, z = at["x"], at["y"], at["z"]
    to_x, to_y = at["to_x"], at["to_y"]
    rows = keep_ref.shape[3]
    chunks = [slice(c * CHUNK, (c + 1) * CHUNK) for c in range(rows // CHUNK)]
    sender = Sender(send_sems, recv_sems)
    meet([at["to_core"], to_x, to_y, at["to_corner"], *at["to_plane"]])

    cores = [
        sender.start(give_ref.at[:, :, :, c], came_ref.at[:, :, :, c], at["to_core"])
        for c in chunks
    ]
    give_x[...] = plus(keep_x[:, 1 - y], came_x[:, 1 - y]).astype(BF16)
    give_y[...] = plus(keep_y[:, 1 - x], came_y[:, 1 - x]).astype(BF16)

    def first(c):
        arrived([cores[c]])
        c = chunks[c]
        total[:, :, :, c] = plus(keep_ref[:, :, :, c], came_ref[:, :, :, c]).astype(BF16)
        return [
            sender.start(total.at[0:2, :, 1 - x, c], from_x.at[:, :, c], to_x),
            sender.start(total.at[2:4, 1 - y, :, c], from_y.at[:, :, c], to_y),
        ]

    def second(c, copies):
        arrived(copies)
        c = chunks[c]
        sum_x[:, :, c] = plus(total[0:2, :, x, c], from_x[:, :, c]).astype(BF16)
        sum_y[:, :, c] = plus(total[2:4, y, :, c], from_y[:, :, c]).astype(BF16)
        return [
            sender.start(sum_x.at[:, 1 - y, c], last_x.at[:, c], to_y),
            sender.start(sum_y.at[:, 1 - x, c], last_y.at[:, c], to_x),
        ]

    def third(c, copies):
        arrived(copies)
        c = chunks[c]
        plane_sum[0:2, c] = plus(sum_x[:, y, c], last_x[:, c]).astype(BF16)
        plane_sum[2:4, c] = plus(sum_y[:, x, c], last_y[:, c]).astype(BF16)
        return [
            sender.start(plane_sum.at[p, c], from_planes.at[k, c], device)
            for k, (p, device) in enumerate(zip(at["planes"], at["to_plane"]))
        ]

    def fourth(c, copies):
        arrived(copies)
        c = chunks[c]
        got = [from_planes[k, c] for k in range(3)]
        out_ref[z, y, x, c] = plus(plane_sum[z, c], *got).astype(BF16)
        here = out_ref.at[z, y, x, c]
        return [sender.start(here, here, device) for device in at["to_plane"]]

    def fifth(c, copies):
        arrived(copies)
        c = chunks[c]
        here_x, here_y = out_ref.at[0:2, y, x, c], out_ref.at[2:4, y, x, c]
        return [sender.start(here_x, here_x, to_y), sender.start(here_y, here_y, to_x)]

    def sixth(c, copies):
        arrived(copies)
        c = chunks[c]
        here_x, here_y = out_ref.at[0:2, :, x, c], out_ref.at[2:4, y, :, c]
        return [sender.start(here_x, here_x, to_x), sender.start(here_y, here_y, to_y)]

    stages = [first, second, third, fourth, fifth, sixth]
    flying = [None] * len(chunks)

    def advance(c, stage):
        flying[c] = stages[stage](c, flying[c]) if stage else first(c)

    half = own_ref.shape[0]
    mine = pl.ds(pl.multiple_of(at["part"] * half, 16), half)
    other = pl.ds(pl.multiple_of((1 - at["part"]) * half, 16), half)
    parts = []
    came_grads = []

    def compute(block):
        cols = slice(block * QBLOCK, (block + 1) * QBLOCK)
        grad, gain_part, delete_part = input_back_block(
            q_ref[:, cols], k_ref[:, cols], v_ref[:, cols], weight_ref, normed_ref[:, cols],
            state_ref[:, cols], grad_mid_ref[:, cols], scale_ref[:, cols], logit_ref[:, cols],
            sums_ref[:, :, cols], columns_ref[...],
        )
        grad_state[:, cols] = grad
        own_ref[:, cols] = grad_state[mine, cols]
        came_grads.append(
            sender.start(grad_state.at[other, cols], came_grad_ref.at[:, cols], at["to_core"])
        )
        parts.append((gain_part, delete_part))

    ones = jnp.ones((8, 128), F32)

    def line_of(values):
        return lax.dot_general(
            ones, values, NT, preferred_element_type=F32, precision=lax.Precision.HIGHEST
        )[:1]

    advance(0, 0)
    compute(0)
    advance(0, 1)
    advance(1, 0)
    compute(1)
    advance(0, 2)
    advance(1, 1)
    advance(2, 0)
    compute(2)
    advance(0, 3)
    advance(1, 2)
    advance(2, 1)
    seconds = [
        sender.start(give_x, second_x, to_y),
        sender.start(give_y, second_y, to_x),
    ]
    compute(3)
    advance(0, 4)
    advance(1, 3)
    advance(2, 2)
    vector[...] = jnp.zeros_like(vector)
    vector[0:1] = line_of(ffn_sum_ref[...])
    vector[1:2] = line_of(sum(p[0] for p in parts))
    vector[2:3] = line_of(sum(p[1] for p in parts))
    vector[3:4, : near_ref.shape[0]] = line_of(near_ref[...])
    vectors = [sender.start(vector, vector_core, at["to_core"])]
    advance(0, 5)
    advance(1, 4)
    advance(2, 3)
    arrived(seconds)
    cut = keep_x.shape[2]
    whole[:, :cut] = plus(keep_x[:, y], came_x[:, y], second_x[...]).astype(BF16)
    whole[:, cut:] = plus(keep_y[:, x], came_y[:, x], second_y[...]).astype(BF16)
    wholes = [
        sender.start(whole.at[p], from_whole.at[k], device)
        for k, (p, device) in enumerate(zip(at["planes"], at["to_plane"]))
    ]
    arrived(vectors)
    vector_core[...] = vector_core[...] + vector[...]
    vectors = [
        sender.start(vector_core, vector_near.at[k], device)
        for k, device in enumerate((to_x, to_y, at["to_corner"]))
    ]
    advance(1, 5)
    advance(2, 4)
    arrived(vectors)
    vector_ref[...] = vector_core[...] + vector_near[0] + vector_near[1] + vector_near[2]
    vectors = [
        sender.start(vector_ref, vector_far.at[k], device)
        for k, device in enumerate(at["to_plane"])
    ]
    advance(2, 5)
    arrived(wholes)
    share_ref[...] = plus(whole[z], from_whole[0], from_whole[1], from_whole[2])
    for copies in flying:
        arrived(copies)
    arrived(came_grads)
    arrived(vectors)
    sender.finish()
    vector_ref[...] = vector_ref[...] + vector_far[0] + vector_far[1] + vector_far[2]


def tail(keep, give, up_x, up_y, ffn_sum, near, *values):
    rows = keep.shape[1] // 4
    (keep_x, came_x), (keep_y, came_y) = up_x, up_y
    cut, rest = keep_x.shape[2], keep_y.shape[2]
    share = cut + rest
    shape = (4, 2, 2, rows, D)
    copies = 80

    def hold(*dims, dtype=BF16):
        return pltpu.VMEM(dims, dtype)

    return pl.pallas_call(
        tail_kernel,
        name="tail",
        in_specs=[VMEM] * (8 + len(values)),
        out_specs=[VMEM] * 5,
        out_shape=[
            jax.ShapeDtypeStruct(shape, BF16),
            jax.ShapeDtypeStruct((share, D), F32),
            jax.ShapeDtypeStruct((8, D), F32),
            jax.ShapeDtypeStruct((D // 2, LMAX), BF16),
            jax.ShapeDtypeStruct((D // 2, LMAX), BF16),
        ],
        scratch_shapes=[
            hold(*shape), hold(*shape), hold(2, 2, rows, D), hold(2, 2, rows, D),
            hold(2, 2, rows, D), hold(2, 2, rows, D), hold(2, rows, D), hold(2, rows, D),
            hold(4, rows, D), hold(3, rows, D),
            hold(4, cut, D), hold(4, rest, D), hold(4, cut, D), hold(4, rest, D),
            hold(4, share, D), hold(3, share, D),
            hold(8, D, dtype=F32), hold(8, D, dtype=F32), hold(3, 8, D, dtype=F32),
            hold(3, 8, D, dtype=F32), hold(D, LMAX),
            pltpu.SemaphoreType.DMA((copies,)),
            pltpu.SemaphoreType.DMA((copies,)),
        ],
        cost_estimate=pl.CostEstimate(
            flops=6 * D * LMAX * 384, bytes_accessed=60 << 20, transcendentals=0
        ),
        compiler_params=pltpu.CompilerParams(
            vmem_limit_bytes=63 << 20, collective_id=1, has_side_effects=True
        ),
    )(keep.reshape(shape), give.reshape(shape), keep_x, came_x, keep_y, came_y, ffn_sum, near, *values)


PLANES = 2


def feed_kernel(half, cut, *refs):
    (
        gate_hbm, up_hbm, down_hbm, normed_hbm, cot_own_hbm, cot_peer_hbm, *rest
    ) = refs
    if half:
        rest = rest[4:]
    (
        grad_own_hbm, grad_came_hbm, mixed_own_hbm, mixed_came_hbm,
        keep_x_hbm, give_x_hbm, keep_y_hbm, give_y_hbm, share_ref,
        weight, normed, cot, hidden, staged, blocks, up_blocks,
        came_x, came_y, last_x, last_y, from_planes,
        load_sems, store_sems, up_sems, send_sems, recv_sems, plane_send, plane_recv,
    ) = rest
    at = neighbours()
    x, y, z = at["x"], at["y"], at["z"]
    to_core, to_x, to_y = at["to_core"], at["to_x"], at["to_y"]
    units = weight.shape[2]
    rows = units // PLANES
    share = rows // 4
    sender = Sender(send_sems, recv_sems)
    order = (0, 1) if half == 0 else (1, 0)

    def load(place, source, target):
        copy = pltpu.make_async_copy(source, target, load_sems.at[place])
        copy.start()
        return copy

    columns = pl.ds(half * units, units)
    loads = [
        load(0, gate_hbm.at[:, columns], weight.at[0]),
        load(1, normed_hbm, normed.at[0]),
        load(2, up_hbm.at[:, columns], weight.at[1]),
        load(3, down_hbm.at[:, columns], weight.at[2]),
        load(4, cot_own_hbm, cot.at[0]),
        load(5, cot_peer_hbm, cot.at[1]),
    ]
    meet([to_core, to_x, to_y, *at["to_plane"]])
    exchange = sender.start(normed_hbm, normed.at[1], to_core)

    def activate(side, low, size):
        def step(block, carry):
            cols = pl.ds(pl.multiple_of(block * 512, 512), 512)
            span = slice(low, low + size)
            value = normed[side, :, cols]
            gate = dot(weight[0, :, span], value, TN)
            up = dot(weight[1, :, span], value, TN)
            grad = dot(weight[2, :, span], cot[side, :, cols], TN)
            square = gate * gate
            bend = jnp.tanh(GELU_C * gate * (1.0 + 0.044715 * square))
            whole = 0.5 * (1.0 + bend)
            gelu = gate * whole
            slope = whole + 0.5 * gate * (1.0 - bend * bend) * (
                GELU_C * (1.0 + 3 * 0.044715 * square)
            )
            hidden[0, side, span, cols] = (gelu * up).astype(BF16)
            hidden[1, side, span, cols] = (grad * up * slope).astype(BF16)
            hidden[2, side, span, cols] = (grad * gelu).astype(BF16)
            return carry

        lax.fori_loop(0, LMAX // 512, step, 0)

    def weight_block(matrix, plane, target):
        other = cot if matrix == 0 else normed
        span = slice(plane * rows, (plane + 1) * rows)
        for low, high in ((0, 768), (768, D)):
            total = dot(hidden[matrix, 0, span], other[0, low:high], NT)
            total = total + dot(hidden[matrix, 1, span], other[1, low:high], NT)
            target[:, :, :, low:high] = total.astype(BF16).reshape(2, 2, share, high - low)

    def first(b):
        block = blocks.at[b]
        return [
            sender.start(block.at[:, 1 - x, :cut], came_x.at[b], to_x),
            sender.start(block.at[1 - y, :, cut:], came_y.at[b], to_y),
        ]

    def second(b, copies):
        arrived(copies)
        block = blocks.at[b]
        block[:, x, :cut] = plus(block[:, x, :cut], came_x[b]).astype(BF16)
        block[y, :, cut:] = plus(block[y, :, cut:], came_y[b]).astype(BF16)
        return [
            sender.start(block.at[1 - y, x, :cut], last_x.at[b], to_y),
            sender.start(block.at[y, 1 - x, cut:], last_y.at[b], to_x),
        ]

    def plane_of(b):
        return half * PLANES + order[b // 2]

    def inward(b, source_plane):
        step = -1 if source_plane > plane_of(b) else 1
        me = lax.axis_index("dp")
        side = 0 if step < 0 else 1
        return pltpu.make_async_remote_copy(
            src_ref=blocks.at[b, y, x],
            dst_ref=from_planes.at[b, side],
            send_sem=plane_send.at[b],
            recv_sem=plane_recv.at[b, side],
            device_id=((source_plane + step) * 4 + me % 4, at["part"]),
            device_id_type=MESH,
        )

    def third(b, copies):
        arrived(copies)
        block = blocks.at[b]
        block[y, x, :cut] = plus(block[y, x, :cut], last_x[b]).astype(BF16)
        block[y, x, cut:] = plus(block[y, x, cut:], last_y[b]).astype(BF16)
        for end in (0, 3):
            if end != plane_of(b):

                @pl.when(z == end)
                def _(end=end):
                    inward(b, end).start()

    def hop(b, distance):
        for plane, side in ((3 - distance, 0), (distance, 1)):
            outside = plane > plane_of(b) if side == 0 else plane < plane_of(b)
            if outside:

                @pl.when(z == plane)
                def _(plane=plane, side=side):
                    inward(b, plane + 1 if side == 0 else plane - 1).wait_recv()
                    blocks[b, y, x] = plus(blocks[b, y, x], from_planes[b, side]).astype(BF16)
                    inward(b, plane).start()

    def final(b):
        plane = plane_of(b)

        @pl.when(z == plane)
        def _():
            got = []
            for side, exists in ((0, plane < 3), (1, plane > 0)):
                if exists:
                    inward(b, plane + 1 if side == 0 else plane - 1).wait_recv()
                    got.append(from_planes[b, side])
            share_ref[b % 2] = plus(blocks[b, y, x], *got)

    def finish_send(b):
        for plane in range(4):
            if plane != plane_of(b):

                @pl.when(z == plane)
                def _(plane=plane):
                    inward(b, plane).wait_send()

    up_copies = []

    def up_block(plane):
        weight_block(2, plane, up_blocks.at[plane])
        block = up_blocks.at[plane]
        to = half * PLANES + plane
        for i, (source, target) in enumerate(
            (
                (block.at[:, x, :cut], keep_x_hbm),
                (block.at[:, 1 - x, :cut], give_x_hbm),
                (block.at[y, :, cut:], keep_y_hbm),
                (block.at[1 - y, :, cut:], give_y_hbm),
            )
        ):
            copy = pltpu.make_async_copy(source, target.at[to], up_sems.at[plane, i])
            copy.start()
            up_copies.append(copy)

    def project_into(slot, side, pairs):
        width = D // 4

        def step(block, carry):
            span = pl.ds(pl.multiple_of(block * width, 16), width)
            total = dot(weight[pairs[0][0], span], hidden[pairs[0][1], side], NN)
            for which, matrix in pairs[1:]:
                total = total + dot(weight[which, span], hidden[matrix, side], NN)
            staged[slot, span] = total.astype(BF16)
            return carry

        lax.fori_loop(0, 4, step, 0)

    ahead_size = 512
    tiles = ((0, ahead_size), (ahead_size, units - ahead_size))
    if half:
        tiles = ((units - ahead_size, ahead_size), (0, units - ahead_size))
    for copy in loads[:5]:
        copy.wait()
    activate(0, *tiles[0])
    loads[5].wait()
    exchange.wait_recv()
    activate(1, *tiles[0])
    flying = {}
    weight_block(0, order[0], blocks.at[0])
    flying[0] = first(0)
    weight_block(1, order[0], blocks.at[1])
    flying[1] = first(1)
    activate(0, *tiles[1])
    flying[0] = second(0, flying[0])
    activate(1, *tiles[1])
    weight_block(0, order[1], blocks.at[2])
    flying[1] = second(1, flying[1])
    flying[2] = first(2)
    third(0, flying[0])
    weight_block(1, order[1], blocks.at[3])
    flying[3] = first(3)
    third(1, flying[1])
    up_block(0)
    hop(0, 1)
    flying[2] = second(2, flying[2])
    up_block(1)
    hop(1, 1)
    hop(0, 2)
    back = ((0, 1), (1, 2))
    ahead = ((2, 0),)
    project_into(0, 1, back)
    sent = [sender.start(staged.at[0], grad_came_hbm, to_core)]
    flying[3] = second(3, flying[3])
    hop(1, 2)
    third(2, flying[2])
    project_into(1, 1, ahead)
    sent.append(sender.start(staged.at[1], mixed_came_hbm, to_core))
    hop(2, 1)
    final(0)
    sent[0].wait_send()
    project_into(0, 0, back)
    store_one = pltpu.make_async_copy(staged.at[0], grad_own_hbm, store_sems.at[0])
    store_one.start()
    third(3, flying[3])
    hop(2, 2)
    final(1)
    sent[1].wait_send()
    project_into(1, 0, ahead)
    store_two = pltpu.make_async_copy(staged.at[1], mixed_own_hbm, store_sems.at[1])
    store_two.start()
    hop(3, 1)
    final(2)
    hop(3, 2)
    final(3)
    for b in range(4):
        finish_send(b)
    for copy in sent:
        copy.wait_recv()
    for copy in sender.made:
        if all(copy is not other for other in sent):
            copy.wait_send()
    for copy in up_copies + [store_one, store_two]:
        copy.wait()


def feed(half, cut, w_gate, w_up, w_down, normed, cot_own, cot_peer, pieces):
    units = w_gate.shape[1] // 2
    share = units // PLANES // 4
    rest = share - cut
    hbm = line(D, BF16)

    def hold(*dims, dtype=BF16):
        return pltpu.VMEM(dims, dtype)

    def piece(rows):
        return jax.ShapeDtypeStruct((4, 2, rows, D), BF16)

    inputs = 6 + len(pieces)
    copies = 24
    return pl.pallas_call(
        functools.partial(feed_kernel, half, cut),
        name="feed_forward",
        in_specs=[ANY] * inputs,
        out_specs=[ANY] * 8 + [VMEM],
        out_shape=[
            hbm, hbm, hbm, hbm, piece(cut), piece(cut), piece(rest), piece(rest),
            jax.ShapeDtypeStruct((2, share, D), F32),
        ],
        input_output_aliases={6 + i: 4 + i for i in range(len(pieces))},
        scratch_shapes=[
            hold(3, D, units), hold(2, D, LMAX), hold(2, D, LMAX), hold(3, 2, units, LMAX),
            hold(2, D, LMAX), hold(4, 2, 2, share, D), hold(2, 2, 2, share, D),
            hold(4, 2, cut, D), hold(4, 2, rest, D), hold(4, cut, D), hold(4, rest, D),
            hold(4, 2, share, D),
            pltpu.SemaphoreType.DMA((6,)),
            pltpu.SemaphoreType.DMA((2,)),
            pltpu.SemaphoreType.DMA((2, 4)),
            pltpu.SemaphoreType.DMA((copies,)),
            pltpu.SemaphoreType.DMA((copies,)),
            pltpu.SemaphoreType.DMA((4,)),
            pltpu.SemaphoreType.DMA((4, 2)),
        ],
        cost_estimate=pl.CostEstimate(
            flops=18 * 2 * D * LMAX * units, bytes_accessed=60 << 20, transcendentals=0
        ),
        compiler_params=pltpu.CompilerParams(
            vmem_limit_bytes=63 << 20, collective_id=2 + half, has_side_effects=True
        ),
    )(w_gate, w_up, w_down, normed, cot_own, cot_peer, *pieces)


def after_feed_kernel(
    own_one, own_two, came_one, came_two, mid_ref, cot_ref, columns_ref, scale_ref, weight_ref,
    grad_mid_ref, grad_attn_ref, attended_ref, sums_ref,
):
    grad = plus(own_one[...], own_two[...], came_one[...], came_two[...])
    mid, scale = mid_ref[...], scale_ref[...]
    weighted = grad * columns_ref[:, 1:2]
    inner = jnp.sum(weighted * mid, axis=0, keepdims=True)
    grad_mid = (
        cot_ref[...].astype(F32) + scale * weighted - mid * (scale * scale * scale * inner / D)
    )
    grad_mid_ref[...] = grad_mid
    grad_attn = grad_mid.astype(BF16)
    grad_attn_ref[...] = grad_attn
    attended_ref[...] = dot(weight_ref[...], grad_attn, NN).astype(BF16)

    @pl.when(pl.program_id(0) == 0)
    def _():
        sums_ref[...] = jnp.zeros_like(sums_ref)

    sums_ref[...] += folded(grad * (mid * scale))


def after_feed(parts, mid, cot, columns, scale, w_out):
    inner = w_out.shape[0]
    return call(
        after_feed_kernel,
        "norm_back",
        2 * D * LMAX * inner,
        D * LMAX * 26,
        44,
        grid=(LMAX // QBLOCK,),
        in_specs=[ROWS] * 6 + [COLUMN, LINE, whole_spec(w_out)],
        out_specs=[ROWS, ROWS, pl.BlockSpec((inner, QBLOCK), lambda i: (0, i)), SUMS],
        out_shape=[
            line(D), line(D, BF16), line(inner, BF16), jax.ShapeDtypeStruct((D, 128), F32),
        ],
    )(*parts, mid, cot, columns, scale, w_out)


def add_mixed_kernel(one, two, three, four, mid_ref, out_ref):
    out_ref[...] = plus(mid_ref[...], one[...], two[...], three[...], four[...]).astype(BF16)


def add_mixed(parts, mid):
    return call(
        add_mixed_kernel,
        "mixed_sum",
        D * LMAX * 5,
        D * LMAX * 14,
        44,
        grid=(LMAX // QBLOCK,),
        in_specs=[ROWS] * 5,
        out_specs=ROWS,
        out_shape=line(D, BF16),
    )(*parts, mid)


STRIP = LMAX + LMAX - TILE


def offsets(shift):
    keys = lax.broadcasted_iota(jnp.int32, (TILE, TILE), 0)
    queries = lax.broadcasted_iota(jnp.int32, (TILE, TILE), 1)
    return shift * TILE + keys - queries


def strip_kernel(table_ref, strip_ref):
    head = pl.program_id(0)
    middle = LMAX - TILE

    def value(bucket):
        return table_ref[bucket, head]

    def side(distance, base, start):
        tile = jnp.full((TILE, TILE), start, F32)
        for count, step in enumerate(NEAR_STEPS):
            tile = jnp.where(distance >= step, value(base + count + 1), tile)
        return tile

    strip_ref[0, : middle - TILE, :] = jnp.full((middle - TILE, TILE), value(15), F32)
    strip_ref[0, middle + 2 * TILE :, :] = jnp.full((STRIP - middle - 2 * TILE, TILE), value(31), F32)
    before = offsets(-1)
    strip_ref[0, middle - TILE : middle, :] = side(-before, 0, value(0))
    relative = offsets(0)
    strip_ref[0, middle : middle + TILE, :] = jnp.where(
        relative > 0, side(relative, 16, value(0)), side(-relative, 0, value(0))
    )
    after = offsets(1)
    strip_ref[0, middle + TILE : middle + 2 * TILE, :] = side(after, 16, value(0))


def bias_strip(table, heads):
    return call(
        strip_kernel,
        "bias_strip",
        heads * 3e6,
        heads * STRIP * TILE * 4,
        8,
        grid=(heads,),
        in_specs=[SMEM],
        out_specs=pl.BlockSpec((1, STRIP, TILE), lambda h: (h, 0, 0)),
        out_shape=jax.ShapeDtypeStruct((heads, STRIP, TILE), F32),
    )(table)


def attend_kernel(
    part_ref, q_ref, k_ref, v_ref, gate_ref, strip_ref, own_ref, peer_ref, came_own_ref, came_peer_ref,
    prob_ref, out_ref, wide_ref, cot_own_ref, cot_peer_ref, hold, sems,
):
    head = pl.program_id(0)
    part = part_ref[0]
    copies_in, copies_out = halves(part, own_ref, came_own_ref, cot_own_ref, hold.at[0], sems.at[0])
    ins, outs = halves(part, peer_ref, came_peer_ref, cot_peer_ref, hold.at[1], sems.at[1])
    copies_in, copies_out = copies_in + ins, copies_out + outs

    @pl.when(head == 0)
    def _():
        for copy in copies_in:
            copy.start()

    @pl.when(head == 2)
    def _():
        for copy, following in zip(copies_in, copies_out):
            copy.wait()
            following.start()

    ones = (lax.broadcasted_iota(jnp.int32, (AUG, LMAX), 0) == 0).astype(F32).astype(BF16)
    scale = HDIM ** (-0.5)
    queries = jnp.concatenate([(q_ref[...].astype(F32) * scale).astype(BF16), ones], axis=0)
    keys = jnp.concatenate([k_ref[...], gate_ref[...]], axis=0)
    for block in range(LMAX // ABLOCK):
        low = block * ABLOCK
        scores = dot(keys, queries[:, low : low + ABLOCK], TN)
        bias = []
        for sub in range(ABLOCK // TILE):
            start = LMAX - TILE - (low + sub * TILE)
            bias.append(strip_ref[0, start : start + LMAX, :])
        scores = scores + jnp.concatenate(bias, axis=1)
        top = jnp.max(scores, axis=0, keepdims=True)
        weights = jnp.exp(scores - top)
        total = jnp.sum(weights, axis=0, keepdims=True)
        prob = (weights * (1.0 / total)).astype(BF16)
        prob_ref[0, :, low : low + ABLOCK] = prob
        out = dot(v_ref[...], prob, NN)
        wide_ref[:, low : low + ABLOCK] = out
        out_ref[:, low : low + ABLOCK] = out.astype(BF16)

    @pl.when(head == pl.num_programs(0) - 1)
    def _():
        for copy in copies_out:
            copy.wait()


def attend(part, qkv, gate, strip, own, peer, came_own, came_peer, heads):
    return call(
        attend_kernel,
        "attend",
        heads * 4 * LMAX * LMAX * HDIM * 4,
        heads * LMAX * LMAX * 2,
        36,
        grid=(heads,),
        in_specs=[
            SMEM,
            pl.BlockSpec((HDIM, LMAX), lambda h: (h, 0)),
            pl.BlockSpec((HDIM, LMAX), lambda h: (heads + h, 0)),
            pl.BlockSpec((HDIM, LMAX), lambda h: (2 * heads + h, 0)),
            pl.BlockSpec((AUG, LMAX), lambda h: (0, 0)),
            pl.BlockSpec((1, STRIP, TILE), lambda h: (h, 0, 0)),
            ANY, ANY, ANY, ANY,
        ],
        out_specs=[
            pl.BlockSpec((1, LMAX, LMAX), lambda h: (h, 0, 0)),
            pl.BlockSpec((HDIM, LMAX), lambda h: (h, 0)),
            pl.BlockSpec((HDIM, LMAX), lambda h: (h, 0)),
            ANY, ANY,
        ],
        out_shape=[
            jax.ShapeDtypeStruct((heads, LMAX, LMAX), BF16),
            jax.ShapeDtypeStruct((heads * HDIM, LMAX), BF16),
            jax.ShapeDtypeStruct((heads * HDIM, LMAX), F32),
            line(D, BF16), line(D, BF16),
        ],
        scratch_shapes=[
            pltpu.VMEM((2, 2, D // 2, LMAX), BF16), pltpu.SemaphoreType.DMA((2, 2, 2))
        ],
    )(part, qkv, qkv, qkv, gate, strip, own, peer, came_own, came_peer)


def attend_back_kernel(
    q_ref, k_ref, v_ref, prob_ref, go_ref, wide_ref, gq_ref, gk_ref, gv_ref, sums_ref, near_ref
):
    scale = HDIM ** (-0.5)
    blocks = LMAX // TILE
    member = (
        lax.broadcasted_iota(jnp.int32, (AUG, LMAX), 0)
        == lax.broadcasted_iota(jnp.int32, (AUG, LMAX), 1) // TILE
    )
    queries = jnp.concatenate([q_ref[...], member.astype(F32).astype(BF16)], axis=0)
    near = [jnp.zeros((TILE, TILE), F32) for _ in range(3)]
    key_total = jnp.zeros((HDIM + AUG, LMAX), F32)
    val_total = jnp.zeros((HDIM, LMAX), F32)
    for block in range(LMAX // ABLOCK):
        low = block * ABLOCK
        prob = prob_ref[0, :, low : low + ABLOCK]
        grad_out = go_ref[:, low : low + ABLOCK]
        soft = prob.astype(F32)
        grad_prob = dot(v_ref[...], grad_out, TN)
        wide = wide_ref[:, low : low + ABLOCK]
        inner = jnp.sum(grad_out.astype(F32) * wide, axis=0, keepdims=True)
        grad_scores = (soft * (grad_prob - inner)).astype(BF16)
        gq_ref[:, low : low + ABLOCK] = (dot(k_ref[...], grad_scores, NN) * scale).astype(BF16)
        key_total = key_total + dot(queries[:, low : low + ABLOCK], grad_scores, NT)
        val_total = val_total + dot(grad_out, prob, NT)
        for sub in range(ABLOCK // TILE):
            place = block * (ABLOCK // TILE) + sub
            for shift in (-1, 0, 1):
                at = place + shift
                if 0 <= at < blocks:
                    piece = grad_scores[at * TILE : (at + 1) * TILE, sub * TILE : (sub + 1) * TILE]
                    near[shift + 1] = near[shift + 1] + piece.astype(F32)
    gk_ref[...] = (key_total[:HDIM] * scale).astype(BF16)
    gv_ref[...] = val_total.astype(BF16)
    sums = key_total[HDIM : HDIM + blocks]
    sums_ref[0] = sums
    shifts = (
        lax.broadcasted_iota(jnp.int32, (blocks, LMAX), 1) // TILE
        - lax.broadcasted_iota(jnp.int32, (blocks, LMAX), 0)
    )

    def fold(tile):
        return jnp.sum(tile, axis=0, keepdims=True)

    def far(chosen):
        return folded(fold(jnp.where(chosen, sums, 0.0)))

    before, same, after = near
    for sign, base, other, shift in ((-1, 0, before, -1), (1, 16, after, 1)):
        near_offset = sign * offsets(0)
        far_offset = sign * offsets(shift)
        floor = 0 if sign < 0 else 1
        last = fold(jnp.where(near_offset >= floor, same, 0.0)) + fold(
            jnp.where(far_offset >= floor, other, 0.0)
        )
        for count, step in enumerate(NEAR_STEPS):
            following = fold(jnp.where(near_offset >= step, same, 0.0)) + fold(
                jnp.where(far_offset >= step, other, 0.0)
            )
            near_ref[0, base + count : base + count + 1] = last - following
            last = following
        near_ref[0, base + 15 : base + 16] = last + far(sign * shifts >= 2)


def attend_back(side, qkv, prob, grad_attended, wide, heads):
    blocks = LMAX // TILE
    rows = jax.ShapeDtypeStruct((heads * HDIM, LMAX), BF16)
    spec = pl.BlockSpec((HDIM, LMAX), lambda h: (h, 0))
    return call(
        attend_back_kernel,
        "attend_back",
        heads * 8 * LMAX * LMAX * HDIM * 4,
        heads * LMAX * LMAX * 2,
        28,
        side=side,
        grid=(heads,),
        in_specs=[
            spec,
            pl.BlockSpec((HDIM, LMAX), lambda h: (heads + h, 0)),
            pl.BlockSpec((HDIM, LMAX), lambda h: (2 * heads + h, 0)),
            pl.BlockSpec((1, LMAX, LMAX), lambda h: (h, 0, 0)),
            spec,
            spec,
        ],
        out_specs=[
            spec,
            spec,
            spec,
            pl.BlockSpec((1, blocks, LMAX), lambda h: (h, 0, 0)),
            pl.BlockSpec((1, BUCKETS, TILE), lambda h: (h, 0, 0)),
        ],
        out_shape=[
            rows,
            rows,
            rows,
            jax.ShapeDtypeStruct((heads, blocks, LMAX), F32),
            jax.ShapeDtypeStruct((heads, BUCKETS, TILE), F32),
        ],
    )(qkv, qkv, qkv, prob, grad_attended, wide)


def ffn_kernel(gate_ref, up_ref, down_ref, x_ref, cot_ref, hid_ref, gg_ref, gu_ref):
    gate = dot(gate_ref[...], x_ref[...], TN)
    up = dot(up_ref[...], x_ref[...], TN)
    grad = dot(down_ref[...], cot_ref[...], TN)
    square = gate * gate
    bend = jnp.tanh(GELU_C * gate * (1.0 + 0.044715 * square))
    half = 0.5 * (1.0 + bend)
    gelu = gate * half
    slope = half + 0.5 * gate * (1.0 - bend * bend) * (GELU_C * (1.0 + 3 * 0.044715 * square))
    hid_ref[...] = (gelu * up).astype(BF16)
    gg_ref[...] = (grad * up * slope).astype(BF16)
    gu_ref[...] = (grad * gelu).astype(BF16)


def ffn(w_gate, w_up, w_down_t, normed, cot):
    units = w_gate.shape[1]
    width = 256
    weight = pl.BlockSpec((D, width), lambda i: (0, i))
    whole = fixed_spec((D, LMAX))
    out = pl.BlockSpec((width, LMAX), lambda i: (i, 0))
    shape = jax.ShapeDtypeStruct((units, LMAX), BF16)
    return call(
        ffn_kernel,
        "ffn",
        6 * D * units * LMAX,
        3 * D * units * 2 + 2 * D * LMAX * 2 + 3 * units * LMAX * 2,
        28,
        grid=(units // width,),
        in_specs=[weight, weight, weight, whole, whole],
        out_specs=[out, out, out],
        out_shape=[shape, shape, shape],
    )(w_gate, w_up, w_down_t, normed, cot)


def weight_grad_kernel(a_own, a_peer, b_own, b_peer, out_ref):
    total = dot(a_own[...], b_own[...], NT) + dot(a_peer[...], b_peer[...], NT)
    out_ref[...] = total.astype(BF16)


def weight_grad(a_own, a_peer, b_own, b_peer):
    units = a_own.shape[0]
    width = 256
    left = pl.BlockSpec((width, LMAX), lambda i: (i, 0))
    whole = fixed_spec((D, LMAX))
    return call(
        weight_grad_kernel,
        "weight_grad",
        4 * D * units * LMAX,
        4 * D * LMAX + 4 * units * LMAX + 2 * units * D,
        28,
        grid=(units // width,),
        in_specs=[left, left, whole, whole],
        out_specs=pl.BlockSpec((width, D), lambda i: (i, 0)),
        out_shape=jax.ShapeDtypeStruct((units, D), BF16),
    )(a_own, a_peer, b_own, b_peer)


def project_kernel(count, *refs):
    total = dot(refs[0][...], refs[count][...], NN)
    for i in range(1, count):
        total = total + dot(refs[i][...], refs[count + i][...], NN)
    refs[-1][...] = total.astype(refs[-1].dtype)


def project(side, weights, values, dtype):
    count = len(weights)
    units = weights[0].shape[1]
    width = D // 4
    weight = pl.BlockSpec((width, units), lambda i: (i, 0))
    whole = fixed_spec((units, LMAX))
    return call(
        functools.partial(project_kernel, count),
        "project",
        2 * count * D * units * LMAX,
        2 * count * (D * units + units * LMAX) + 4 * D * LMAX,
        28,
        side=side,
        grid=(D // width,),
        in_specs=[weight] * count + [whole] * count,
        out_specs=pl.BlockSpec((width, LMAX), lambda i: (i, 0)),
        out_shape=jax.ShapeDtypeStruct((D, LMAX), dtype),
    )(*weights, *values)


def fold_kernel(bit_ref, keep_ref, came_ref, keep_out, give_out):
    mine = bit_ref[0]
    for out, which in ((keep_out, mine), (give_out, 1 - mine)):
        total = keep_ref[:, which].astype(F32) + came_ref[:, which].astype(F32)
        out[...] = total.astype(BF16)


def fold(bit, keep, came):
    outer, _, rows, width = keep.shape
    steps = 2 if outer % 2 == 0 else 1
    block = pl.BlockSpec((outer // steps, 2, rows, width), lambda i: (i, 0, 0, 0))
    out = pl.BlockSpec((outer // steps, rows, width), lambda i: (i, 0, 0))
    shape = jax.ShapeDtypeStruct((outer, rows, width), BF16)
    return call(
        fold_kernel,
        "fold",
        4 * keep.size,
        6 * keep.size,
        16,
        grid=(steps,),
        in_specs=[SMEM, block, block],
        out_specs=[out, out],
        out_shape=[shape, shape],
    )(bit.reshape(1), keep, came)


def across(values, bit):
    size = lax.axis_size("dp")
    return lax.ppermute(values, "dp", [(i, i ^ (1 << bit)) for i in range(size)])


def bit_of(bit):
    return (lax.axis_index("dp") >> bit) & 1


def stacked(values, came, mine, axis):
    return jnp.where(mine == 0, jnp.stack([values, came], axis), jnp.stack([came, values], axis))


def sum_everywhere(keep, came):
    bits = lax.axis_size("dp").bit_length() - 1
    rows = keep.shape[1] // 4
    keep, came = (v.reshape(4, 2, 2, rows, D) for v in (keep, came))
    keep_x, give_x = fold(
        bit_of(0), keep[:2].reshape(4, 2, rows, D), came[:2].reshape(4, 2, rows, D)
    )
    keep_y, give_y = fold(
        bit_of(1), keep[2:].reshape(2, 2, 2 * rows, D), came[2:].reshape(2, 2, 2 * rows, D)
    )
    came_x, came_y = across(give_x, 0), across(give_y, 1)
    keep_x, give_x = fold(
        bit_of(1), keep_x.reshape(2, 2, rows, D), came_x.reshape(2, 2, rows, D)
    )
    keep_y, give_y = fold(
        bit_of(0), keep_y.reshape(2, 2, rows, D), came_y.reshape(2, 2, rows, D)
    )
    came_x, came_y = across(give_x, 1), across(give_y, 0)
    keep = jnp.concatenate([keep_x, keep_y], axis=0).reshape(2, 2, rows, D)
    came = jnp.concatenate([came_x, came_y], axis=0).reshape(2, 2, rows, D)
    keep, give = fold(bit_of(2), keep, came)
    came = across(give, 2)
    keep, give = fold(bit_of(3), keep.reshape(1, 2, rows, D), came.reshape(1, 2, rows, D))
    came = across(give, 3)
    total = (keep.astype(F32) + came.astype(F32)).astype(BF16)
    for bit in range(4, bits):
        total = (total.astype(F32) + across(total, bit).astype(F32)).astype(BF16)
    total = stacked(total, across(total, 3), bit_of(3), 1)
    total = stacked(total, across(total, 2), bit_of(2), 2).reshape(4, rows, D)
    total_x, total_y = total[:2], total[2:]
    total_x = stacked(total_x, across(total_x, 1), bit_of(1), 1)
    total_y = stacked(total_y, across(total_y, 0), bit_of(0), 1)
    total_x = stacked(total_x, across(total_x, 0), bit_of(0), 2)
    total_y = stacked(total_y, across(total_y, 1), bit_of(1), 1)
    return [v.reshape(4 * rows, D).astype(F32) for v in (*total_x, *total_y)]


def sum_small(values):
    bits = lax.axis_size("dp").bit_length() - 1
    values = values + swap(values)
    for bit in range(bits):
        values = values + across(values, bit)
    return values


def halve(values, order):
    size = lax.axis_size("dp")
    bits = size.bit_length() - 1
    index = lax.axis_index("dp")
    rows = values.shape[0] // size
    values = values.reshape((2,) * bits + (rows, values.shape[1]))
    left = list(range(bits - 1, -1, -1))
    for step, bit in enumerate(order):
        axis = left.index(bit)
        left.pop(axis)
        mine = (index >> bit) & 1
        keep = lax.dynamic_index_in_dim(values, mine, axis, keepdims=False)
        give = lax.dynamic_index_in_dim(values, 1 - mine, axis, keepdims=False)
        came = lax.ppermute(give, "dp", [(i, i ^ (1 << bit)) for i in range(size)])
        total = keep.astype(F32) + came.astype(F32)
        values = total if step == bits - 1 else total.astype(BF16)
    return values


def swap(values):
    return lax.ppermute(values, "mp", [(0, 1), (1, 0)])


def body(
    tokens,
    cotangent,
    lengths,
    keep_mask,
    ln_attn,
    w_query,
    w_key,
    w_value,
    w_attn_out,
    rel_table,
    w_delete,
    ln_ffn,
    w_gate,
    w_up,
    w_ffn_out,
):
    dev_count = lax.axis_size("dp")
    bits = dev_count.bit_length() - 1
    part = lax.axis_index("mp")
    inner = 2 * w_query.shape[1]
    heads = inner // HDIM
    half = tokens.shape[1]
    first = part == 0
    part_ref = part.reshape(1).astype(jnp.int32)

    def in_parts(own, peer, axis):
        return jnp.where(
            first, jnp.concatenate([own, peer], axis), jnp.concatenate([peer, own], axis)
        )

    def home(values):
        mine = lax.dynamic_slice_in_dim(values, part * half, half, 0)
        other = lax.dynamic_slice_in_dim(values, (1 - part) * half, half, 0)
        return spread(part_ref, slot, mine, swap(other)).T

    own_weights = (w_query.T, w_key.T, w_value.T, w_attn_out)
    slot, count, stack = places(part_ref, lengths, keep_mask.reshape(1, ROWS_DEV), own_weights)
    came_stack = swap(stack)
    own_tokens, peer_tokens = compact(part_ref, slot, tokens.T)
    came_tokens = swap(peer_tokens)
    own_cot, peer_cot, w_qkv, w_out = compact_join(
        part_ref, slot, cotangent.T, stack, came_stack
    )
    came_cot_own, came_cot_peer = swap(peer_cot), swap(own_cot)
    table = in_parts(rel_table, swap(rel_table), 1)
    strip = bias_strip(table, heads)
    columns = jnp.stack([ln_attn, ln_ffn, w_delete.astype(F32)], axis=1)

    state, normed_one, qkv, gate_rows, del_logit, scale_one = input_part(
        part_ref, own_tokens, came_tokens, columns, w_qkv, count
    )
    prob, attended, wide, cot_own, cot_peer = attend(
        part_ref, qkv, gate_rows, strip, own_cot, peer_cot, came_cot_own, came_cot_peer, heads
    )
    mid, normed_two, scale_two = middle_part(w_out, attended, state, columns)
    w_down_t = w_ffn_out.T
    share = w_gate.shape[1] // dev_count
    if bits == 4 and share % 16 == 0:
        cut = (share // 2 + 15) // 16 * 16
        one = feed(0, cut, w_gate, w_up, w_down_t, normed_two, cot_own, cot_peer, ())
        two = feed(1, cut, w_gate, w_up, w_down_t, normed_two, cot_own, cot_peer, one[4:8])
        keep_x, give_x, keep_y, give_y = two[4:8]
        up_x = (keep_x, across(give_x, 0))
        up_y = (keep_y, across(give_y, 1))
        grad_mid, grad_attn, grad_attended, sum_ffn = after_feed(
            (one[0], two[0], one[1], two[1]), mid, cot_own, columns, scale_two, w_out
        )
        grad_q, grad_k, grad_v, sums, near = attend_back(
            (), qkv, prob, grad_attended, wide, heads
        )
        keep, give = head_grads(part_ref, grad_q, grad_k, grad_v, normed_one, attended, grad_attn)
        totals, grad_up, small, state_own, state_came = tail(
            keep, give, up_x, up_y, sum_ffn, near.reshape(heads * BUCKETS, TILE),
            grad_q, grad_k, grad_v, w_qkv, normed_one, state, grad_mid, scale_one, del_logit, sums,
            columns,
        )
        mixed_parts = (one[2], two[2], one[3], two[3])
        mixed = home(add_mixed(mixed_parts, mid))
        total_q, total_v, total_k, total_out = totals.reshape(4, inner // 2, D).astype(F32)
        grad_tokens = spread(part_ref, slot, state_own, state_came).T
        grad_ln_ffn, grad_ln_attn, grad_w_delete = small[0], small[1], small[2]
        grad_table = small[3, : heads * BUCKETS].reshape(heads, BUCKETS).T
        grad_down, grad_gate = jnp.where(bit_of(3) == 0, one[8], two[8])
    else:
        normed_two_peer = swap(normed_two)
        hid_own, gg_own, gu_own = ffn(w_gate, w_up, w_down_t, normed_two, cot_own)
        hid_peer, gg_peer, gu_peer = ffn(w_gate, w_up, w_down_t, normed_two_peer, cot_peer)
        order = tuple(range(bits))
        grad_down = halve(weight_grad(hid_own, hid_peer, cot_own, cot_peer), order)
        grad_gate = halve(weight_grad(gg_own, gg_peer, normed_two, normed_two_peer), order)
        grad_up = halve(weight_grad(gu_own, gu_peer, normed_two, normed_two_peer), order)
        back_peer = project((), (w_gate, w_up), (gg_peer, gu_peer), BF16)
        grad_mid, grad_attn, grad_attended, sum_ffn = middle_back(
            w_gate, w_up, gg_own, gu_own, swap(back_peer), mid, cot_own, columns, scale_two, w_out
        )
        grad_q, grad_k, grad_v, sums, near = attend_back(
            (), qkv, prob, grad_attended, wide, heads
        )
        keep, give = head_grads(part_ref, grad_q, grad_k, grad_v, normed_one, attended, grad_attn)
        total_q, total_v, total_k, total_out = sum_everywhere(keep, swap(give))
        grad_state, sum_attn, sum_delete = input_back(
            (), grad_q, grad_k, grad_v, w_qkv, normed_one, state, grad_mid, scale_one, del_logit,
            sums, columns,
        )
        grad_tokens = home(grad_state)
        grad_table = jnp.sum(near, axis=2).T
        small = jnp.concatenate(
            [jnp.sum(v, axis=1) for v in (sum_ffn, sum_attn, sum_delete)]
            + [grad_table.reshape(-1)]
        )
        small = sum_small(small)
        grad_ln_ffn, grad_ln_attn = small[:D], small[D : 2 * D]
        grad_w_delete = small[2 * D : 3 * D]
        grad_table = small[3 * D :].reshape(BUCKETS, heads)
        mixed_peer = project((), (w_down_t,), (hid_peer,), BF16)
        mixed = home(mixed_part(w_down_t, hid_own, swap(mixed_peer), mid))

    def own_half(values):
        return lax.dynamic_slice_in_dim(values, part * half, half, 0)

    return (
        mixed,
        grad_tokens,
        own_half(grad_ln_attn),
        total_q.T,
        total_k.T,
        total_v.T,
        total_out,
        lax.dynamic_slice_in_dim(grad_table, part * (heads // 2), heads // 2, 1),
        grad_w_delete,
        own_half(grad_ln_ffn),
        grad_gate.T,
        grad_up.T,
        grad_down,
    )


def solution(mesh):
    return jax.shard_map(
        body,
        mesh=mesh,
        in_specs=(
            P("dp", "mp"),
            P("dp", "mp"),
            P("dp"),
            P("dp"),
            P(),
            P(None, "mp"),
            P(None, "mp"),
            P(None, "mp"),
            P("mp", None),
            P(None, "mp"),
            P(),
            P(),
            P(None, "mp"),
            P(None, "mp"),
            P("mp", None),
        ),
        out_specs=(
            P("dp", "mp"),
            P("dp", "mp"),
            P("mp"),
            P(None, "mp"),
            P(None, "mp"),
            P(None, "mp"),
            P("mp", None),
            P(None, "mp"),
            P(),
            P("mp"),
            P(None, ("mp", "dp")),
            P(None, ("mp", "dp")),
            P(("mp", "dp"), None),
        ),
        check_vma=False,
    )
```

```python
import functools

import jax
import jax.numpy as jnp
import numpy as np
from jax import lax
from jax.experimental import pallas as pl
from jax.experimental.pallas import tpu as pltpu
from jax.sharding import PartitionSpec as P

D = 1472
HDIM = 64
BUCKETS = 32
LMAX = 1024
ROWS_DEV = 2048

EPSILON = 1e-06
DELETE_DEPTH = 4.0
NEG_LARGE = -1e30
NEAR_STEPS = (1, 2, 3, 4, 5, 6, 7, 8, 12, 16, 23, 32, 46, 64, 91)
TILE = 128
QBLOCK = 256
ABLOCK = 512
AUG = 16
F32 = jnp.float32
BF16 = jnp.bfloat16
GELU_C = float(np.sqrt(2.0 / np.pi))

NN = (((1,), (0,)), ((), ()))
TN = (((0,), (0,)), ((), ()))
NT = (((1,), (1,)), ((), ()))


def dot(a, b, dims):
    return lax.dot_general(a, b, dims, preferred_element_type=F32)


def with_side(kernel, inputs, outputs, pairs, bits_ref, *refs):
    first = inputs + 2 * pairs
    last = first + outputs + 2 * pairs
    kernel(*refs[:inputs], *refs[first : first + outputs], *refs[last:])
    for pair in range(pairs):
        keep_ref, came_ref = refs[inputs + 2 * pair : inputs + 2 * pair + 2]
        outs = refs[first + outputs + 2 * pair : first + outputs + 2 * pair + 2]
        mine = bits_ref[pair]
        for out, which in zip(outs, (mine, 1 - mine)):
            total = keep_ref[:, which].astype(F32) + came_ref[:, which].astype(F32)
            out[...] = total.astype(BF16)


def call(kernel, name, flops, nbytes, limit, side=(), **kw):
    for _, keep, came in side:
        nbytes += 6 * keep.size
    extra = ()
    outputs = 1
    if side:
        single = not isinstance(kw["out_shape"], list)
        out_specs = [kw["out_specs"]] if single else list(kw["out_specs"])
        out_shape = [kw["out_shape"]] if single else list(kw["out_shape"])
        outputs, inputs = len(out_shape), len(kw["in_specs"])
        in_specs = list(kw["in_specs"])
        for _, keep, came in side:
            outer, _, rows, width = keep.shape
            block = pl.BlockSpec(
                (1, 2, rows, width), lambda i, n=outer: (jnp.minimum(i, n - 1), 0, 0, 0)
            )
            out = pl.BlockSpec(
                (1, rows, width), lambda i, n=outer: (jnp.minimum(i, n - 1), 0, 0)
            )
            in_specs += [block, block]
            out_specs += [out, out]
            out_shape += [jax.ShapeDtypeStruct((outer, rows, width), BF16)] * 2
            extra += (keep, came)
        kernel = functools.partial(with_side, kernel, inputs, outputs, len(side))
        kw.update(in_specs=[SMEM] + in_specs, out_specs=out_specs, out_shape=out_shape)
    run = pl.pallas_call(
        kernel,
        name=name,
        cost_estimate=pl.CostEstimate(
            flops=int(flops), bytes_accessed=int(nbytes), transcendentals=0
        ),
        compiler_params=pltpu.CompilerParams(vmem_limit_bytes=limit << 20),
        **kw,
    )
    if not side:
        return run

    def launch(*args):
        out = run(jnp.stack([bit for bit, _, _ in side]), *args, *extra)
        main = out[0] if single else out[:outputs]
        return main, out[outputs:]

    return launch


VMEM = pl.BlockSpec(memory_space=pltpu.VMEM)
SMEM = pl.BlockSpec(memory_space=pltpu.SMEM)
ANY = pl.BlockSpec(memory_space=pl.ANY)


def place_kernel(
    part_ref, length_ref, mask_ref, q_ref, k_ref, v_ref, out_ref, slot_ref, count_ref, stack_ref
):
    for i, ref in enumerate((q_ref, k_ref, v_ref, out_ref)):
        stack_ref[i] = ref[...]
    mask = mask_ref[...]
    rows = lax.broadcasted_iota(jnp.int32, (1, ROWS_DEV), 1)
    first = (rows < length_ref[0]).astype(jnp.int32)
    pieces = []
    before = jnp.zeros((1, 1), F32)
    ahead = lax.broadcasted_iota(jnp.int32, (QBLOCK, QBLOCK), 0) <= lax.broadcasted_iota(
        jnp.int32, (QBLOCK, QBLOCK), 1
    )
    ahead = ahead.astype(F32).astype(BF16)
    flags = mask.astype(F32).astype(BF16)
    for block in range(ROWS_DEV // QBLOCK):
        part = flags[:, block * QBLOCK : (block + 1) * QBLOCK]
        ranks = dot(jnp.broadcast_to(part, (16, QBLOCK)), ahead, NN)[:1] + before
        before = ranks[:, QBLOCK - 1 :]
        pieces.append(ranks)
    ranks = jnp.concatenate(pieces, axis=1).astype(jnp.int32)
    kept_first = jnp.sum(mask * first, axis=1, keepdims=True)
    total = jnp.sum(mask, axis=1, keepdims=True)
    rank = ranks - 1 + jnp.where(first > 0, 0, LMAX - kept_first)
    slot_ref[...] = jnp.where(mask > 0, rank, -1)
    count = jnp.where(part_ref[0] == 0, kept_first, total - kept_first)
    count_ref[...] = jnp.broadcast_to(count, (1, 128))


def places(part, lengths, mask, weights):
    return call(
        place_kernel,
        "places",
        1e6,
        1e5,
        16,
        in_specs=[SMEM, SMEM, VMEM] + [VMEM] * 4,
        out_specs=[VMEM, VMEM, VMEM],
        out_shape=[
            jax.ShapeDtypeStruct((1, ROWS_DEV), jnp.int32),
            jax.ShapeDtypeStruct((1, 128), jnp.int32),
            jax.ShapeDtypeStruct((4, *weights[0].shape), BF16),
        ],
    )(part, lengths, mask, *weights)


def compact_half(item, slot_ref, x_ref, out_ref):
    for block in range(LMAX // QBLOCK):
        width = ROWS_DEV - 512 - block * QBLOCK
        start = pl.multiple_of(item * 512 + block * QBLOCK, 128)
        ids = item * LMAX + block * QBLOCK + lax.broadcasted_iota(jnp.int32, (QBLOCK, 1), 0)
        hot = (slot_ref[:, pl.ds(start, width)] == ids).astype(F32).astype(BF16)
        rows = dot(x_ref[:, pl.ds(start, width)], hot, NT)
        out_ref[:, block * QBLOCK : (block + 1) * QBLOCK] = rows.astype(BF16)


def compact_kernel(part_ref, slot_ref, x_ref, own_ref, peer_ref):
    compact_half(part_ref[0], slot_ref, x_ref, own_ref)
    compact_half(1 - part_ref[0], slot_ref, x_ref, peer_ref)


def halves(part, own, came, whole, hold, sems):
    size = own.shape[0]
    copies_in, copies_out = [], []
    for i, (ref, place) in enumerate(((own, part), (came, 1 - part))):
        copies_in.append(pltpu.make_async_copy(ref, hold.at[i], sems.at[0, i]))
        target = whole.at[pl.ds(pl.multiple_of(place * size, 16), size)]
        copies_out.append(pltpu.make_async_copy(hold.at[i], target, sems.at[1, i]))
    return copies_in, copies_out


def compact_join_kernel(
    part_ref, slot_ref, x_ref, stack_ref, came_ref, own_ref, peer_ref, qkv_ref, out_ref, hold, sems
):
    part = part_ref[0]
    inner = out_ref.shape[0]
    copies_in, copies_out = [], []
    for i in range(4):
        whole = qkv_ref.at[pl.ds(i * inner, inner)] if i < 3 else out_ref
        ins, outs = halves(part, stack_ref.at[i], came_ref.at[i], whole, hold.at[i], sems.at[i])
        copies_in += ins
        copies_out += outs
    for copy in copies_in:
        copy.start()
    compact_half(part, slot_ref, x_ref, own_ref)
    for copy, following in zip(copies_in, copies_out):
        copy.wait()
        following.start()
    compact_half(1 - part, slot_ref, x_ref, peer_ref)
    for copy in copies_out:
        copy.wait()


def compact_join(part, slot, columns, stack, came):
    width = columns.shape[0]
    inner = 2 * stack.shape[1]
    shape = jax.ShapeDtypeStruct((width, LMAX), BF16)
    return call(
        compact_join_kernel,
        "compact_join",
        2 * width * 2 * 4608 * 256,
        width * 2048 * 4,
        24,
        in_specs=[SMEM, VMEM, VMEM, ANY, ANY],
        out_specs=[VMEM, VMEM, ANY, ANY],
        out_shape=[
            shape,
            shape,
            jax.ShapeDtypeStruct((3 * inner, D), BF16),
            jax.ShapeDtypeStruct((inner, D), BF16),
        ],
        scratch_shapes=[
            pltpu.VMEM((4, 2, inner // 2, D), BF16), pltpu.SemaphoreType.DMA((4, 2, 2))
        ],
    )(part, slot, columns, stack, came)


def compact(part, slot, columns):
    width = columns.shape[0]
    shape = jax.ShapeDtypeStruct((width, LMAX), BF16)
    return call(
        compact_kernel,
        "compact",
        2 * width * 2 * 4608 * 256,
        width * 2048 * 4,
        16,
        in_specs=[SMEM, VMEM, VMEM],
        out_specs=[VMEM, VMEM],
        out_shape=[shape, shape],
    )(part, slot, columns)


def spread_kernel(part_ref, slot_ref, own_ref, peer_ref, out_ref):
    first = part_ref[0] == 0
    items = (
        jnp.where(first, own_ref[...], peer_ref[...]),
        jnp.where(first, peer_ref[...], own_ref[...]),
    )
    for block in range(ROWS_DEV // QBLOCK):
        end = (block + 1) * QBLOCK
        slots = slot_ref[:, end - QBLOCK : end]
        total = None
        for item in range(2):
            reach = min(end - 512 * item, LMAX)
            if reach <= 0 or (item == 0 and end > LMAX):
                continue
            ids = item * LMAX + lax.broadcasted_iota(jnp.int32, (reach, 1), 0)
            hot = (slots == ids).astype(F32).astype(BF16)
            part = dot(items[item][:, :reach], hot, NN)
            total = part if total is None else total + part
        out_ref[:, end - QBLOCK : end] = total.astype(BF16)


def spread(part, slot, own, peer):
    width = own.shape[0]
    return call(
        spread_kernel,
        "spread",
        2 * width * 7168 * 256,
        width * 2048 * 4,
        16,
        in_specs=[SMEM, VMEM, VMEM, VMEM],
        out_specs=VMEM,
        out_shape=jax.ShapeDtypeStruct((width, ROWS_DEV), BF16),
    )(part, slot, own, peer)


COLUMNS = 3
ROWS = pl.BlockSpec((D, QBLOCK), lambda i: (0, i))
LINE = pl.BlockSpec((1, QBLOCK), lambda i: (0, i))
COLUMN = pl.BlockSpec((D, COLUMNS), lambda i: (0, 0))
SUMS = pl.BlockSpec((D, 128), lambda i: (0, 0))


def fixed_spec(shape):
    return pl.BlockSpec(shape, lambda i: (0,) * len(shape), pipeline_mode=pl.Buffered(1))


def whole_spec(array):
    return fixed_spec(array.shape)


def line(rows=1, dtype=F32):
    return jax.ShapeDtypeStruct((rows, LMAX), dtype)


def folded(values):
    return sum(values[:, i * 128 : (i + 1) * 128] for i in range(values.shape[1] // 128))


def input_kernel(
    part_ref, own_ref, came_ref, gain_ref, weight_ref, count_ref,
    state_ref, normed_ref, qkv_ref, gate_ref, logit_ref, scale_ref,
):
    first = part_ref[0] == 0
    own, came = own_ref[...], came_ref[...]
    half = own.shape[0]
    state_ref[:half] = jnp.where(first, own, came)
    state_ref[half:] = jnp.where(first, came, own)
    state = state_ref[...].astype(F32)
    scale = lax.rsqrt(jnp.sum(state * state, axis=0, keepdims=True) / D + EPSILON)
    normed = (state * scale * gain_ref[:, 0:1]).astype(BF16)
    normed_ref[...] = normed
    scale_ref[...] = scale
    qkv_ref[...] = dot(weight_ref[...], normed, NN).astype(BF16)
    logit = jnp.sum(normed.astype(F32) * gain_ref[:, 2:3], axis=0, keepdims=True)
    logit_ref[...] = logit
    gate = -DELETE_DEPTH * jax.nn.sigmoid(-logit)
    rows = pl.program_id(0) * QBLOCK + lax.broadcasted_iota(jnp.int32, (1, QBLOCK), 1)
    gate = jnp.where(rows < count_ref[:, :1], gate, NEG_LARGE)
    place = lax.broadcasted_iota(jnp.int32, (AUG, QBLOCK), 0)
    gate_ref[...] = jnp.where(place == 0, gate, 0.0).astype(BF16)


def input_part(part, own, came, gain, weights, count):
    inner = weights.shape[0]
    half = pl.BlockSpec((own.shape[0], QBLOCK), lambda i: (0, i))
    return call(
        input_kernel,
        "norm_project",
        2 * D * LMAX * weights.shape[0],
        D * LMAX * 10,
        48,
        grid=(LMAX // QBLOCK,),
        in_specs=[SMEM, half, half, COLUMN, whole_spec(weights), whole_spec(count)],
        out_specs=[
            ROWS,
            ROWS,
            pl.BlockSpec((inner, QBLOCK), lambda i: (0, i)),
            pl.BlockSpec((AUG, QBLOCK), lambda i: (0, i)),
            LINE,
            LINE,
        ],
        out_shape=[line(D, BF16), line(D, BF16), line(inner, BF16), line(AUG, BF16), line(), line()],
    )(part, own, came, gain, weights, count)


def middle_kernel(weight_ref, attended_ref, state_ref, gain_ref, mid_ref, normed_ref, scale_ref):
    mid = state_ref[...].astype(F32) + dot(weight_ref[...], attended_ref[...], TN)
    scale = lax.rsqrt(jnp.sum(mid * mid, axis=0, keepdims=True) / D + EPSILON)
    mid_ref[...] = mid
    scale_ref[...] = scale
    normed_ref[...] = (mid * scale * gain_ref[:, 1:2]).astype(BF16)


def middle_part(weights, attended, state, gain):
    inner = attended.shape[0]
    return call(
        middle_kernel,
        "attention_out_norm",
        2 * D * LMAX * inner,
        D * LMAX * 8,
        48,
        grid=(LMAX // QBLOCK,),
        in_specs=[
            whole_spec(weights),
            pl.BlockSpec((inner, QBLOCK), lambda i: (0, i)),
            ROWS,
            COLUMN,
        ],
        out_specs=[ROWS, ROWS, LINE],
        out_shape=[line(D), line(D, BF16), line()],
    )(weights, attended, state, gain)


def middle_back_kernel(
    gate_ref, up_ref, gg_ref, gu_ref, came_ref, mid_ref, cot_ref, gain_ref, scale_ref, weight_ref,
    grad_mid_ref, grad_attn_ref, attended_ref, sums_ref,
):
    grad = dot(gate_ref[...], gg_ref[...], NN) + dot(up_ref[...], gu_ref[...], NN)
    grad = grad + came_ref[...].astype(F32)
    mid, scale = mid_ref[...], scale_ref[...]
    weighted = grad * gain_ref[:, 1:2]
    inner = jnp.sum(weighted * mid, axis=0, keepdims=True)
    grad_mid = (
        cot_ref[...].astype(F32) + scale * weighted - mid * (scale * scale * scale * inner / D)
    )
    grad_mid_ref[...] = grad_mid
    grad_attn = grad_mid.astype(BF16)
    grad_attn_ref[...] = grad_attn
    attended_ref[...] = dot(weight_ref[...], grad_attn, NN).astype(BF16)

    @pl.when(pl.program_id(0) == 0)
    def _():
        sums_ref[...] = jnp.zeros_like(sums_ref)

    sums_ref[...] += folded(grad * (mid * scale))


def middle_back(w_gate, w_up, gg, gu, came, mid, cot, gain, scale, w_out):
    inner, units = w_out.shape[0], w_gate.shape[1]
    unit_rows = pl.BlockSpec((units, QBLOCK), lambda i: (0, i))
    return call(
        middle_back_kernel,
        "norm_back",
        4 * D * LMAX * units,
        D * LMAX * 20 + 4 * D * units,
        48,
        grid=(LMAX // QBLOCK,),
        in_specs=[
            whole_spec(w_gate), whole_spec(w_up), unit_rows, unit_rows, ROWS, ROWS, ROWS, COLUMN,
            LINE, whole_spec(w_out),
        ],
        out_specs=[ROWS, ROWS, pl.BlockSpec((inner, QBLOCK), lambda i: (0, i)), SUMS],
        out_shape=[
            line(D), line(D, BF16), line(inner, BF16), jax.ShapeDtypeStruct((D, 128), F32),
        ],
    )(w_gate, w_up, gg, gu, came, mid, cot, gain, scale, w_out)


def input_back_block(q, k, v, weight_ref, normed, state, grad_mid, scale, logit, sums, columns):
    heads = sums.shape[0]
    gate = sums[0]
    for head in range(1, heads):
        gate = gate + sums[head]
    gate = jnp.sum(gate, axis=0, keepdims=True)
    grad_logit = gate * DELETE_DEPTH * jax.nn.sigmoid(logit) * jax.nn.sigmoid(-logit)
    inner = q.shape[0]
    grad = dot(weight_ref[:inner], q, TN)
    grad = grad + dot(weight_ref[inner : 2 * inner], k, TN)
    grad = grad + dot(weight_ref[2 * inner : 3 * inner], v, TN)
    grad = grad + columns[:, 2:3] * grad_logit
    state = state.astype(F32)
    weighted = grad * columns[:, 0:1]
    total = jnp.sum(weighted * state, axis=0, keepdims=True)
    grad_state = grad_mid + scale * weighted - state * (scale * scale * scale * total / D)
    gain_part = folded(grad * (state * scale))
    delete_part = folded(normed.astype(F32) * grad_logit)
    return grad_state.astype(BF16), gain_part, delete_part


def input_back_kernel(
    q_ref, k_ref, v_ref, weight_ref, normed_ref, state_ref, grad_mid_ref, scale_ref, logit_ref,
    sums_ref, columns_ref, grad_ref, gain_sum_ref, delete_sum_ref,
):
    grad_ref[...], gain_part, delete_part = input_back_block(
        q_ref[...], k_ref[...], v_ref[...], weight_ref, normed_ref[...], state_ref[...],
        grad_mid_ref[...], scale_ref[...], logit_ref[...], sums_ref[...], columns_ref[...],
    )

    @pl.when(pl.program_id(0) == 0)
    def _():
        gain_sum_ref[...] = jnp.zeros_like(gain_sum_ref)
        delete_sum_ref[...] = jnp.zeros_like(delete_sum_ref)

    gain_sum_ref[...] += gain_part
    delete_sum_ref[...] += delete_part


def input_back(side, q, k, v, weights, normed, state, grad_mid, scale, logit, sums, gain):
    inner = q.shape[0]
    head_rows = pl.BlockSpec((inner, QBLOCK), lambda i: (0, i))
    return call(
        input_back_kernel,
        "project_norm_back",
        6 * D * LMAX * inner,
        D * LMAX * 12,
        48,
        side=side,
        grid=(LMAX // QBLOCK,),
        in_specs=[
            head_rows, head_rows, head_rows, whole_spec(weights), ROWS, ROWS, ROWS, LINE, LINE,
            pl.BlockSpec((sums.shape[0], sums.shape[1], QBLOCK), lambda i: (0, 0, i)),
            COLUMN,
        ],
        out_specs=[ROWS, SUMS, SUMS],
        out_shape=[
            line(D, BF16),
            jax.ShapeDtypeStruct((D, 128), F32),
            jax.ShapeDtypeStruct((D, 128), F32),
        ],
    )(q, k, v, weights, normed, state, grad_mid, scale, logit, sums, gain)


def mixed_kernel(down_ref, hid_ref, came_ref, mid_ref, out_ref):
    mixed = mid_ref[...] + dot(down_ref[...], hid_ref[...], NN)
    out_ref[...] = (mixed + came_ref[...].astype(F32)).astype(BF16)


def mixed_part(down, hid, came, mid):
    width = D // 4
    units = down.shape[1]
    rows = pl.BlockSpec((width, LMAX), lambda i: (i, 0))
    return call(
        mixed_kernel,
        "mixed",
        2 * D * LMAX * units,
        D * LMAX * 8 + D * units * 2,
        48,
        grid=(D // width,),
        in_specs=[pl.BlockSpec((width, units), lambda i: (i, 0)), whole_spec(hid), rows, rows],
        out_specs=rows,
        out_shape=line(D, BF16),
    )(down, hid, came, mid)


def head_grad_kernel(part_ref, q_ref, v_ref, k_ref, attended_ref, normed_ref, back_ref, *outs):
    keep_ref, give_ref, hold = outs
    part = part_ref[0]
    rows = hold.shape[0] // 2
    pieces = (
        (q_ref, normed_ref), (v_ref, normed_ref), (k_ref, normed_ref), (attended_ref, back_ref),
    )
    for place, (left, right) in enumerate(pieces):
        hold[...] = dot(left[...], right[...], NT).astype(BF16)
        keep_ref[place] = hold[pl.ds(pl.multiple_of(part * rows, 16), rows)]
        give_ref[place] = hold[pl.ds(pl.multiple_of((1 - part) * rows, 16), rows)]


def head_grads(part, q, k, v, normed, attended, back):
    inner = q.shape[0]
    shape = jax.ShapeDtypeStruct((4, inner // 2, D), BF16)
    return call(
        head_grad_kernel,
        "head_grads",
        8 * D * LMAX * inner,
        D * LMAX * 4 + 4 * LMAX * inner * 2 + 16 * inner * D,
        36,
        in_specs=[SMEM] + [VMEM] * 6,
        out_specs=[VMEM, VMEM],
        out_shape=[shape, shape],
        scratch_shapes=[pltpu.VMEM((inner, D), BF16)],
    )(part, q, v, k, attended, normed, back)


MESH = pl.DeviceIdType.MESH


class Sender:
    def __init__(self, send_sems, recv_sems):
        self.send_sems, self.recv_sems, self.made = send_sems, recv_sems, []

    def start(self, source, target, device):
        place = len(self.made)
        copy = pltpu.make_async_remote_copy(
            src_ref=source,
            dst_ref=target,
            send_sem=self.send_sems.at[place],
            recv_sem=self.recv_sems.at[place],
            device_id=device,
            device_id_type=MESH,
        )
        copy.start()
        self.made.append(copy)
        return copy

    def finish(self):
        for copy in self.made:
            copy.wait_send()


def arrived(copies):
    for copy in copies:
        copy.wait_recv()


def plus(first, *others):
    total = first.astype(F32)
    for other in others:
        total = total + other.astype(F32)
    return total


def neighbours():
    me, part = lax.axis_index("dp"), lax.axis_index("mp")
    x, y, z = me % 2, (me // 2) % 2, me // 4
    across_x, across_y = 1 - 2 * x, 2 - 4 * y
    planes = [(z + k) % 4 for k in range(1, 4)]
    return dict(
        x=x,
        y=y,
        z=z,
        part=part,
        planes=planes,
        to_core=(me, 1 - part),
        to_x=(me + across_x, part),
        to_y=(me + across_y, part),
        to_corner=(me + across_x + across_y, part),
        to_plane=[(p * 4 + me % 4, part) for p in planes],
    )


def meet(devices):
    barrier = pltpu.get_barrier_semaphore()
    for device in devices:
        pl.semaphore_signal(barrier, inc=1, device_id=device, device_id_type=MESH)
    pl.semaphore_wait(barrier, len(devices))


CHUNK = 16


def tail_kernel(
    keep_ref, give_ref, keep_x, came_x, keep_y, came_y, ffn_sum_ref, near_ref,
    scale_ref, logit_ref, sums_ref, columns_ref,
    q_hbm, k_hbm, v_hbm, normed_hbm, state_hbm, grad_mid_hbm, mix_one, mix_two, mix_three, mix_four,
    mid_hbm, weight_hbm,
    out_ref, share_ref, vector_ref, own_ref, came_grad_ref, own_mixed_ref, came_mixed_ref,
    came_ref, total, from_x, from_y, sum_x, sum_y, last_x, last_y, plane_sum, from_planes,
    give_x, give_y, second_x, second_y, whole, from_whole,
    vector, vector_core, vector_near, vector_far, sent_grad, sent_mixed, block_hold,
    head_hold, half_hold, wide_hold, weight_ref, load_sems, weight_sem, send_sems, recv_sems,
):
    loads = {}

    def load_block(block):
        cols = slice(block * QBLOCK, (block + 1) * QBLOCK)
        slot = block % 2
        pairs = [
            (source.at[:, cols], head_hold.at[slot, i])
            for i, source in enumerate((q_hbm, k_hbm, v_hbm))
        ]
        pairs += [
            (source.at[:, cols], half_hold.at[slot, i])
            for i, source in enumerate((normed_hbm, state_hbm))
        ]
        pairs.append((grad_mid_hbm.at[:, cols], wide_hold.at[slot]))
        start_loads(("grad", block), slot, pairs)

    def load_mixed(block):
        cols = slice(block * QBLOCK, (block + 1) * QBLOCK)
        slot = block % 2
        pairs = [
            (source.at[:, cols], half_hold.at[slot, i])
            for i, source in enumerate((mix_one, mix_two, mix_three, mix_four))
        ]
        pairs.append((mid_hbm.at[:, cols], wide_hold.at[slot]))
        start_loads(("mixed", block), slot, pairs)

    def start_loads(key, slot, pairs):
        loads[key] = []
        for i, (source, target) in enumerate(pairs):
            copy = pltpu.make_async_copy(source, target, load_sems.at[slot, i])
            copy.start()
            loads[key].append(copy)

    weight_load = pltpu.make_async_copy(weight_hbm, weight_ref, weight_sem)
    weight_load.start()
    load_block(0)
    load_block(1)
    at = neighbours()
    x, y, z = at["x"], at["y"], at["z"]
    to_x, to_y = at["to_x"], at["to_y"]
    rows = keep_ref.shape[3]
    chunks = [slice(c * CHUNK, (c + 1) * CHUNK) for c in range(rows // CHUNK)]
    sender = Sender(send_sems, recv_sems)
    meet([at["to_core"], to_x, to_y, at["to_corner"], *at["to_plane"]])

    cores = [
        sender.start(give_ref.at[:, :, :, c], came_ref.at[:, :, :, c], at["to_core"])
        for c in chunks
    ]
    give_x[...] = plus(keep_x[:, 1 - y], came_x[:, 1 - y]).astype(BF16)
    give_y[...] = plus(keep_y[:, 1 - x], came_y[:, 1 - x]).astype(BF16)

    def first(c):
        arrived([cores[c]])
        c = chunks[c]
        total[:, :, :, c] = plus(keep_ref[:, :, :, c], came_ref[:, :, :, c]).astype(BF16)
        return [
            sender.start(total.at[0:2, :, 1 - x, c], from_x.at[:, :, c], to_x),
            sender.start(total.at[2:4, 1 - y, :, c], from_y.at[:, :, c], to_y),
        ]

    def second(c, copies):
        arrived(copies)
        c = chunks[c]
        sum_x[:, :, c] = plus(total[0:2, :, x, c], from_x[:, :, c]).astype(BF16)
        sum_y[:, :, c] = plus(total[2:4, y, :, c], from_y[:, :, c]).astype(BF16)
        return [
            sender.start(sum_x.at[:, 1 - y, c], last_x.at[:, c], to_y),
            sender.start(sum_y.at[:, 1 - x, c], last_y.at[:, c], to_x),
        ]

    def third(c, copies):
        arrived(copies)
        c = chunks[c]
        plane_sum[0:2, c] = plus(sum_x[:, y, c], last_x[:, c]).astype(BF16)
        plane_sum[2:4, c] = plus(sum_y[:, x, c], last_y[:, c]).astype(BF16)
        return [
            sender.start(plane_sum.at[p, c], from_planes.at[k, c], device)
            for k, (p, device) in enumerate(zip(at["planes"], at["to_plane"]))
        ]

    def fourth(c, copies):
        arrived(copies)
        c = chunks[c]
        got = [from_planes[k, c] for k in range(3)]
        out_ref[z, y, x, c] = plus(plane_sum[z, c], *got).astype(BF16)
        here = out_ref.at[z, y, x, c]
        return [sender.start(here, here, device) for device in at["to_plane"]]

    def fifth(c, copies):
        arrived(copies)
        c = chunks[c]
        here_x, here_y = out_ref.at[0:2, y, x, c], out_ref.at[2:4, y, x, c]
        return [sender.start(here_x, here_x, to_y), sender.start(here_y, here_y, to_x)]

    def sixth(c, copies):
        arrived(copies)
        c = chunks[c]
        here_x, here_y = out_ref.at[0:2, :, x, c], out_ref.at[2:4, y, :, c]
        return [sender.start(here_x, here_x, to_x), sender.start(here_y, here_y, to_y)]

    stages = [first, second, third, fourth, fifth, sixth]
    flying = [None] * len(chunks)

    def advance(c, stage):
        flying[c] = stages[stage](c, flying[c]) if stage else first(c)

    half = own_ref.shape[0]
    mine = pl.ds(pl.multiple_of(at["part"] * half, 16), half)
    other = pl.ds(pl.multiple_of((1 - at["part"]) * half, 16), half)
    parts = []
    came_grads = []

    def part_out(cols, values, out_ref, sent_ref, came_ref):
        block_hold[...] = values
        out_ref[:, cols] = block_hold[mine]
        sent_ref[:, cols] = block_hold[other]
        came_grads.append(
            sender.start(sent_ref.at[:, cols], came_ref.at[:, cols], at["to_core"])
        )

    def compute(block):
        if block == 0:
            weight_load.wait()
        for copy in loads["grad", block]:
            copy.wait()
        cols = slice(block * QBLOCK, (block + 1) * QBLOCK)
        slot = block % 2
        grad, gain_part, delete_part = input_back_block(
            head_hold[slot, 0], head_hold[slot, 1], head_hold[slot, 2], weight_ref,
            half_hold[slot, 0], half_hold[slot, 1], wide_hold[slot], scale_ref[:, cols],
            logit_ref[:, cols], sums_ref[:, :, cols], columns_ref[...],
        )
        part_out(cols, grad, own_ref, sent_grad, came_grad_ref)
        parts.append((gain_part, delete_part))
        if block < 2:
            load_block(block + 2)
        else:
            load_mixed(block - 2)

    def compute_mixed(block):
        for copy in loads["mixed", block]:
            copy.wait()
        cols = slice(block * QBLOCK, (block + 1) * QBLOCK)
        slot = block % 2
        values = plus(wide_hold[slot], *[half_hold[slot, i] for i in range(4)]).astype(BF16)
        part_out(cols, values, own_mixed_ref, sent_mixed, came_mixed_ref)
        if block < 2:
            load_mixed(block + 2)

    ones = jnp.ones((8, 128), F32)

    def line_of(values):
        return lax.dot_general(
            ones, values, NT, preferred_element_type=F32, precision=lax.Precision.HIGHEST
        )[:1]

    cut = keep_x.shape[2]
    advance(0, 0)
    compute(0)
    advance(0, 1)
    advance(1, 0)
    compute(1)
    advance(0, 2)
    advance(1, 1)
    advance(2, 0)
    compute(2)
    advance(0, 3)
    advance(1, 2)
    advance(2, 1)
    seconds = [
        sender.start(give_x, second_x, to_y),
        sender.start(give_y, second_y, to_x),
    ]
    compute(3)
    advance(0, 4)
    advance(1, 3)
    advance(2, 2)
    vector[...] = jnp.zeros_like(vector)
    vector[0:1] = line_of(ffn_sum_ref[...])
    vector[1:2] = line_of(sum(p[0] for p in parts))
    vector[2:3] = line_of(sum(p[1] for p in parts))
    vector[3:4, : near_ref.shape[0]] = line_of(near_ref[...])
    vectors = [sender.start(vector, vector_core, at["to_core"])]
    advance(0, 5)
    advance(1, 4)
    compute_mixed(0)
    advance(2, 3)
    arrived(seconds)
    whole[:, :cut] = plus(keep_x[:, y], came_x[:, y], second_x[...]).astype(BF16)
    whole[:, cut:] = plus(keep_y[:, x], came_y[:, x], second_y[...]).astype(BF16)
    wholes = [
        sender.start(whole.at[p], from_whole.at[k], device)
        for k, (p, device) in enumerate(zip(at["planes"], at["to_plane"]))
    ]
    arrived(vectors)
    vector_core[...] = vector_core[...] + vector[...]
    vectors = [
        sender.start(vector_core, vector_near.at[k], device)
        for k, device in enumerate((to_x, to_y, at["to_corner"]))
    ]
    advance(1, 5)
    compute_mixed(1)
    advance(2, 4)
    compute_mixed(2)
    arrived(vectors)
    vector_ref[...] = vector_core[...] + vector_near[0] + vector_near[1] + vector_near[2]
    vectors = [
        sender.start(vector_ref, vector_far.at[k], device)
        for k, device in enumerate(at["to_plane"])
    ]
    advance(2, 5)
    compute_mixed(3)
    arrived(wholes)
    share_ref[...] = plus(whole[z], from_whole[0], from_whole[1], from_whole[2])
    for copies in flying:
        arrived(copies)
    arrived(came_grads)
    arrived(vectors)
    sender.finish()
    vector_ref[...] = vector_ref[...] + vector_far[0] + vector_far[1] + vector_far[2]


def tail(keep, give, up_x, up_y, ffn_sum, near, lines, far):
    rows = keep.shape[1] // 4
    (keep_x, came_x), (keep_y, came_y) = up_x, up_y
    cut, rest = keep_x.shape[2], keep_y.shape[2]
    share = cut + rest
    shape = (4, 2, 2, rows, D)
    copies = 80
    heads = far[0].shape[0]

    def hold(*dims, dtype=BF16):
        return pltpu.VMEM(dims, dtype)

    return pl.pallas_call(
        tail_kernel,
        name="tail",
        in_specs=[VMEM] * (8 + len(lines)) + [ANY] * len(far),
        out_specs=[VMEM] * 7,
        out_shape=[
            jax.ShapeDtypeStruct(shape, BF16),
            jax.ShapeDtypeStruct((share, D), F32),
            jax.ShapeDtypeStruct((8, D), F32),
            *[jax.ShapeDtypeStruct((D // 2, LMAX), BF16)] * 4,
        ],
        scratch_shapes=[
            hold(*shape), hold(*shape), hold(2, 2, rows, D), hold(2, 2, rows, D),
            hold(2, 2, rows, D), hold(2, 2, rows, D), hold(2, rows, D), hold(2, rows, D),
            hold(4, rows, D), hold(3, rows, D),
            hold(4, cut, D), hold(4, rest, D), hold(4, cut, D), hold(4, rest, D),
            hold(4, share, D), hold(3, share, D),
            hold(8, D, dtype=F32), hold(8, D, dtype=F32), hold(3, 8, D, dtype=F32),
            hold(3, 8, D, dtype=F32), hold(D // 2, LMAX), hold(D // 2, LMAX), hold(D, QBLOCK),
            hold(2, 3, heads, QBLOCK), hold(2, 4, D, QBLOCK), hold(2, D, QBLOCK, dtype=F32),
            hold(3 * heads, D),
            pltpu.SemaphoreType.DMA((2, 6)),
            pltpu.SemaphoreType.DMA,
            pltpu.SemaphoreType.DMA((copies,)),
            pltpu.SemaphoreType.DMA((copies,)),
        ],
        cost_estimate=pl.CostEstimate(
            flops=6 * D * LMAX * 384, bytes_accessed=60 << 20, transcendentals=0
        ),
        compiler_params=pltpu.CompilerParams(
            vmem_limit_bytes=63 << 20, collective_id=1, has_side_effects=True
        ),
    )(keep.reshape(shape), give.reshape(shape), keep_x, came_x, keep_y, came_y, ffn_sum, near, *lines, *far)


PLANES = 2


def feed_kernel(half, cut, *refs):
    (
        gate_hbm, up_hbm, down_hbm, normed_hbm, cot_own_hbm, cot_peer_hbm, *rest
    ) = refs
    if half:
        rest = rest[4:]
    (
        grad_own_hbm, grad_came_hbm, mixed_own_hbm, mixed_came_hbm,
        keep_x_hbm, give_x_hbm, keep_y_hbm, give_y_hbm, share_ref,
        weight, normed, cot, hidden, staged, blocks, up_blocks,
        came_x, came_y, last_x, last_y, from_planes,
        load_sems, store_sems, up_sems, send_sems, recv_sems, plane_send, plane_recv,
    ) = rest
    at = neighbours()
    x, y, z = at["x"], at["y"], at["z"]
    to_core, to_x, to_y = at["to_core"], at["to_x"], at["to_y"]
    units = weight.shape[2]
    rows = units // PLANES
    share = rows // 4
    sender = Sender(send_sems, recv_sems)
    order = (0, 1) if half == 0 else (1, 0)

    def load(place, source, target):
        copy = pltpu.make_async_copy(source, target, load_sems.at[place])
        copy.start()
        return copy

    columns = pl.ds(half * units, units)
    loads = [
        load(0, gate_hbm.at[:, columns], weight.at[0]),
        load(1, normed_hbm, normed.at[0]),
        load(2, up_hbm.at[:, columns], weight.at[1]),
        load(3, down_hbm.at[:, columns], weight.at[2]),
        load(4, cot_own_hbm, cot.at[0]),
        load(5, cot_peer_hbm, cot.at[1]),
    ]
    meet([to_core, to_x, to_y, *at["to_plane"]])
    exchange = sender.start(normed_hbm, normed.at[1], to_core)

    def activate(side, low, size):
        def step(block, carry):
            cols = pl.ds(pl.multiple_of(block * 512, 512), 512)
            span = slice(low, low + size)
            value = normed[side, :, cols]
            gate = dot(weight[0, :, span], value, TN)
            up = dot(weight[1, :, span], value, TN)
            grad = dot(weight[2, :, span], cot[side, :, cols], TN)
            square = gate * gate
            bend = jnp.tanh(GELU_C * gate * (1.0 + 0.044715 * square))
            whole = 0.5 * (1.0 + bend)
            gelu = gate * whole
            slope = whole + 0.5 * gate * (1.0 - bend * bend) * (
                GELU_C * (1.0 + 3 * 0.044715 * square)
            )
            hidden[0, side, span, cols] = (gelu * up).astype(BF16)
            hidden[1, side, span, cols] = (grad * up * slope).astype(BF16)
            hidden[2, side, span, cols] = (grad * gelu).astype(BF16)
            return carry

        lax.fori_loop(0, LMAX // 512, step, 0)

    def weight_block(matrix, plane, target):
        other = cot if matrix == 0 else normed
        span = slice(plane * rows, (plane + 1) * rows)
        for low, high in ((0, 768), (768, D)):
            total = dot(hidden[matrix, 0, span], other[0, low:high], NT)
            total = total + dot(hidden[matrix, 1, span], other[1, low:high], NT)
            target[:, :, :, low:high] = total.astype(BF16).reshape(2, 2, share, high - low)

    def first(b):
        block = blocks.at[b]
        return [
            sender.start(block.at[:, 1 - x, :cut], came_x.at[b], to_x),
            sender.start(block.at[1 - y, :, cut:], came_y.at[b], to_y),
        ]

    def second(b, copies):
        arrived(copies)
        block = blocks.at[b]
        block[:, x, :cut] = plus(block[:, x, :cut], came_x[b]).astype(BF16)
        block[y, :, cut:] = plus(block[y, :, cut:], came_y[b]).astype(BF16)
        return [
            sender.start(block.at[1 - y, x, :cut], last_x.at[b], to_y),
            sender.start(block.at[y, 1 - x, cut:], last_y.at[b], to_x),
        ]

    def plane_of(b):
        return half * PLANES + order[b // 2]

    def inward(b, source_plane):
        step = -1 if source_plane > plane_of(b) else 1
        me = lax.axis_index("dp")
        side = 0 if step < 0 else 1
        return pltpu.make_async_remote_copy(
            src_ref=blocks.at[b, y, x],
            dst_ref=from_planes.at[b, side],
            send_sem=plane_send.at[b],
            recv_sem=plane_recv.at[b, side],
            device_id=((source_plane + step) * 4 + me % 4, at["part"]),
            device_id_type=MESH,
        )

    def third(b, copies):
        arrived(copies)
        block = blocks.at[b]
        block[y, x, :cut] = plus(block[y, x, :cut], last_x[b]).astype(BF16)
        block[y, x, cut:] = plus(block[y, x, cut:], last_y[b]).astype(BF16)
        for end in (0, 3):
            if end != plane_of(b):

                @pl.when(z == end)
                def _(end=end):
                    inward(b, end).start()

    def hop(b, distance):
        for plane, side in ((3 - distance, 0), (distance, 1)):
            outside = plane > plane_of(b) if side == 0 else plane < plane_of(b)
            if outside:

                @pl.when(z == plane)
                def _(plane=plane, side=side):
                    inward(b, plane + 1 if side == 0 else plane - 1).wait_recv()
                    blocks[b, y, x] = plus(blocks[b, y, x], from_planes[b, side]).astype(BF16)
                    inward(b, plane).start()

    def final(b):
        plane = plane_of(b)

        @pl.when(z == plane)
        def _():
            got = []
            for side, exists in ((0, plane < 3), (1, plane > 0)):
                if exists:
                    inward(b, plane + 1 if side == 0 else plane - 1).wait_recv()
                    got.append(from_planes[b, side])
            share_ref[b % 2] = plus(blocks[b, y, x], *got)

    def finish_send(b):
        for plane in range(4):
            if plane != plane_of(b):

                @pl.when(z == plane)
                def _(plane=plane):
                    inward(b, plane).wait_send()

    up_copies = []

    def up_block(plane):
        weight_block(2, plane, up_blocks.at[plane])
        block = up_blocks.at[plane]
        to = half * PLANES + plane
        for i, (source, target) in enumerate(
            (
                (block.at[:, x, :cut], keep_x_hbm),
                (block.at[:, 1 - x, :cut], give_x_hbm),
                (block.at[y, :, cut:], keep_y_hbm),
                (block.at[1 - y, :, cut:], give_y_hbm),
            )
        ):
            copy = pltpu.make_async_copy(source, target.at[to], up_sems.at[plane, i])
            copy.start()
            up_copies.append(copy)

    def project_into(slot, side, pairs):
        width = D // 4

        def step(block, carry):
            span = pl.ds(pl.multiple_of(block * width, 16), width)
            total = dot(weight[pairs[0][0], span], hidden[pairs[0][1], side], NN)
            for which, matrix in pairs[1:]:
                total = total + dot(weight[which, span], hidden[matrix, side], NN)
            staged[slot, span] = total.astype(BF16)
            return carry

        lax.fori_loop(0, 4, step, 0)

    ahead_size = 512
    tiles = ((0, ahead_size), (ahead_size, units - ahead_size))
    if half:
        tiles = ((units - ahead_size, ahead_size), (0, units - ahead_size))
    for copy in loads[:5]:
        copy.wait()
    activate(0, *tiles[0])
    loads[5].wait()
    exchange.wait_recv()
    activate(1, *tiles[0])
    flying = {}
    weight_block(0, order[0], blocks.at[0])
    flying[0] = first(0)
    weight_block(1, order[0], blocks.at[1])
    flying[1] = first(1)
    activate(0, *tiles[1])
    flying[0] = second(0, flying[0])
    activate(1, *tiles[1])
    weight_block(0, order[1], blocks.at[2])
    flying[1] = second(1, flying[1])
    flying[2] = first(2)
    third(0, flying[0])
    weight_block(1, order[1], blocks.at[3])
    flying[3] = first(3)
    third(1, flying[1])
    up_block(0)
    hop(0, 1)
    flying[2] = second(2, flying[2])
    up_block(1)
    hop(1, 1)
    hop(0, 2)
    back = ((0, 1), (1, 2))
    ahead = ((2, 0),)
    project_into(0, 1, back)
    sent = [sender.start(staged.at[0], grad_came_hbm, to_core)]
    flying[3] = second(3, flying[3])
    hop(1, 2)
    third(2, flying[2])
    project_into(1, 1, ahead)
    sent.append(sender.start(staged.at[1], mixed_came_hbm, to_core))
    hop(2, 1)
    final(0)
    sent[0].wait_send()
    project_into(0, 0, back)
    store_one = pltpu.make_async_copy(staged.at[0], grad_own_hbm, store_sems.at[0])
    store_one.start()
    third(3, flying[3])
    hop(2, 2)
    final(1)
    sent[1].wait_send()
    project_into(1, 0, ahead)
    store_two = pltpu.make_async_copy(staged.at[1], mixed_own_hbm, store_sems.at[1])
    store_two.start()
    hop(3, 1)
    final(2)
    hop(3, 2)
    final(3)
    for b in range(4):
        finish_send(b)
    for copy in sent:
        copy.wait_recv()
    for copy in sender.made:
        if all(copy is not other for other in sent):
            copy.wait_send()
    for copy in up_copies + [store_one, store_two]:
        copy.wait()


def feed(half, cut, w_gate, w_up, w_down, normed, cot_own, cot_peer, pieces):
    units = w_gate.shape[1] // 2
    share = units // PLANES // 4
    rest = share - cut
    hbm = line(D, BF16)

    def hold(*dims, dtype=BF16):
        return pltpu.VMEM(dims, dtype)

    def piece(rows):
        return jax.ShapeDtypeStruct((4, 2, rows, D), BF16)

    inputs = 6 + len(pieces)
    copies = 24
    return pl.pallas_call(
        functools.partial(feed_kernel, half, cut),
        name="feed_forward",
        in_specs=[ANY] * inputs,
        out_specs=[ANY] * 8 + [VMEM],
        out_shape=[
            hbm, hbm, hbm, hbm, piece(cut), piece(cut), piece(rest), piece(rest),
            jax.ShapeDtypeStruct((2, share, D), F32),
        ],
        input_output_aliases={6 + i: 4 + i for i in range(len(pieces))},
        scratch_shapes=[
            hold(3, D, units), hold(2, D, LMAX), hold(2, D, LMAX), hold(3, 2, units, LMAX),
            hold(2, D, LMAX), hold(4, 2, 2, share, D), hold(2, 2, 2, share, D),
            hold(4, 2, cut, D), hold(4, 2, rest, D), hold(4, cut, D), hold(4, rest, D),
            hold(4, 2, share, D),
            pltpu.SemaphoreType.DMA((6,)),
            pltpu.SemaphoreType.DMA((2,)),
            pltpu.SemaphoreType.DMA((2, 4)),
            pltpu.SemaphoreType.DMA((copies,)),
            pltpu.SemaphoreType.DMA((copies,)),
            pltpu.SemaphoreType.DMA((4,)),
            pltpu.SemaphoreType.DMA((4, 2)),
        ],
        cost_estimate=pl.CostEstimate(
            flops=18 * 2 * D * LMAX * units, bytes_accessed=60 << 20, transcendentals=0
        ),
        compiler_params=pltpu.CompilerParams(
            vmem_limit_bytes=63 << 20, collective_id=2 + half, has_side_effects=True
        ),
    )(w_gate, w_up, w_down, normed, cot_own, cot_peer, *pieces)


def after_feed_kernel(
    own_one, own_two, came_one, came_two, mid_ref, cot_ref, columns_ref, scale_ref, weight_ref,
    grad_mid_ref, grad_attn_ref, attended_ref, sums_ref,
):
    grad = plus(own_one[...], own_two[...], came_one[...], came_two[...])
    mid, scale = mid_ref[...], scale_ref[...]
    weighted = grad * columns_ref[:, 1:2]
    inner = jnp.sum(weighted * mid, axis=0, keepdims=True)
    grad_mid = (
        cot_ref[...].astype(F32) + scale * weighted - mid * (scale * scale * scale * inner / D)
    )
    grad_mid_ref[...] = grad_mid
    grad_attn = grad_mid.astype(BF16)
    grad_attn_ref[...] = grad_attn
    attended_ref[...] = dot(weight_ref[...], grad_attn, NN).astype(BF16)

    @pl.when(pl.program_id(0) == 0)
    def _():
        sums_ref[...] = jnp.zeros_like(sums_ref)

    sums_ref[...] += folded(grad * (mid * scale))


def after_feed(parts, mid, cot, columns, scale, w_out):
    inner = w_out.shape[0]
    return call(
        after_feed_kernel,
        "norm_back",
        2 * D * LMAX * inner,
        D * LMAX * 26,
        48,
        grid=(LMAX // QBLOCK,),
        in_specs=[ROWS] * 6 + [COLUMN, LINE, whole_spec(w_out)],
        out_specs=[ROWS, ROWS, pl.BlockSpec((inner, QBLOCK), lambda i: (0, i)), SUMS],
        out_shape=[
            line(D), line(D, BF16), line(inner, BF16), jax.ShapeDtypeStruct((D, 128), F32),
        ],
    )(*parts, mid, cot, columns, scale, w_out)


STRIP = LMAX + LMAX - TILE


def offsets(shift):
    keys = lax.broadcasted_iota(jnp.int32, (TILE, TILE), 0)
    queries = lax.broadcasted_iota(jnp.int32, (TILE, TILE), 1)
    return shift * TILE + keys - queries


def strip_kernel(table_ref, strip_ref):
    head = pl.program_id(0)
    middle = LMAX - TILE

    def value(bucket):
        return table_ref[bucket, head]

    def side(distance, base, start):
        tile = jnp.full((TILE, TILE), start, F32)
        for count, step in enumerate(NEAR_STEPS):
            tile = jnp.where(distance >= step, value(base + count + 1), tile)
        return tile

    strip_ref[0, : middle - TILE, :] = jnp.full((middle - TILE, TILE), value(15), F32)
    strip_ref[0, middle + 2 * TILE :, :] = jnp.full((STRIP - middle - 2 * TILE, TILE), value(31), F32)
    before = offsets(-1)
    strip_ref[0, middle - TILE : middle, :] = side(-before, 0, value(0))
    relative = offsets(0)
    strip_ref[0, middle : middle + TILE, :] = jnp.where(
        relative > 0, side(relative, 16, value(0)), side(-relative, 0, value(0))
    )
    after = offsets(1)
    strip_ref[0, middle + TILE : middle + 2 * TILE, :] = side(after, 16, value(0))


def bias_strip(table, heads):
    return call(
        strip_kernel,
        "bias_strip",
        heads * 3e6,
        heads * STRIP * TILE * 4,
        8,
        grid=(heads,),
        in_specs=[SMEM],
        out_specs=pl.BlockSpec((1, STRIP, TILE), lambda h: (h, 0, 0)),
        out_shape=jax.ShapeDtypeStruct((heads, STRIP, TILE), F32),
    )(table)


def attend_kernel(
    part_ref, q_ref, k_ref, v_ref, gate_ref, strip_ref, own_ref, peer_ref, came_own_ref, came_peer_ref,
    prob_ref, out_ref, wide_ref, cot_own_ref, cot_peer_ref, hold, sems,
):
    head = pl.program_id(0)
    part = part_ref[0]
    copies_in, copies_out = halves(part, own_ref, came_own_ref, cot_own_ref, hold.at[0], sems.at[0])
    ins, outs = halves(part, peer_ref, came_peer_ref, cot_peer_ref, hold.at[1], sems.at[1])
    copies_in, copies_out = copies_in + ins, copies_out + outs

    @pl.when(head == 0)
    def _():
        for copy in copies_in:
            copy.start()

    @pl.when(head == 2)
    def _():
        for copy, following in zip(copies_in, copies_out):
            copy.wait()
            following.start()

    ones = (lax.broadcasted_iota(jnp.int32, (AUG, LMAX), 0) == 0).astype(F32).astype(BF16)
    scale = HDIM ** (-0.5)
    queries = jnp.concatenate([(q_ref[...].astype(F32) * scale).astype(BF16), ones], axis=0)
    keys = jnp.concatenate([k_ref[...], gate_ref[...]], axis=0)
    for block in range(LMAX // ABLOCK):
        low = block * ABLOCK
        scores = dot(keys, queries[:, low : low + ABLOCK], TN)
        bias = []
        for sub in range(ABLOCK // TILE):
            start = LMAX - TILE - (low + sub * TILE)
            bias.append(strip_ref[0, start : start + LMAX, :])
        scores = scores + jnp.concatenate(bias, axis=1)
        top = jnp.max(scores, axis=0, keepdims=True)
        weights = jnp.exp(scores - top)
        total = jnp.sum(weights, axis=0, keepdims=True)
        prob = (weights * (1.0 / total)).astype(BF16)
        prob_ref[0, :, low : low + ABLOCK] = prob
        out = dot(v_ref[...], prob, NN)
        wide_ref[:, low : low + ABLOCK] = out
        out_ref[:, low : low + ABLOCK] = out.astype(BF16)

    @pl.when(head == pl.num_programs(0) - 1)
    def _():
        for copy in copies_out:
            copy.wait()


def attend(part, qkv, gate, strip, own, peer, came_own, came_peer, heads):
    return call(
        attend_kernel,
        "attend",
        heads * 4 * LMAX * LMAX * HDIM * 4,
        heads * LMAX * LMAX * 2,
        48,
        grid=(heads,),
        in_specs=[
            SMEM,
            pl.BlockSpec((HDIM, LMAX), lambda h: (h, 0)),
            pl.BlockSpec((HDIM, LMAX), lambda h: (heads + h, 0)),
            pl.BlockSpec((HDIM, LMAX), lambda h: (2 * heads + h, 0)),
            pl.BlockSpec((AUG, LMAX), lambda h: (0, 0)),
            pl.BlockSpec((1, STRIP, TILE), lambda h: (h, 0, 0)),
            ANY, ANY, ANY, ANY,
        ],
        out_specs=[
            pl.BlockSpec((1, LMAX, LMAX), lambda h: (h, 0, 0)),
            pl.BlockSpec((HDIM, LMAX), lambda h: (h, 0)),
            pl.BlockSpec((HDIM, LMAX), lambda h: (h, 0)),
            ANY, ANY,
        ],
        out_shape=[
            jax.ShapeDtypeStruct((heads, LMAX, LMAX), BF16),
            jax.ShapeDtypeStruct((heads * HDIM, LMAX), BF16),
            jax.ShapeDtypeStruct((heads * HDIM, LMAX), F32),
            line(D, BF16), line(D, BF16),
        ],
        scratch_shapes=[
            pltpu.VMEM((2, 2, D // 2, LMAX), BF16), pltpu.SemaphoreType.DMA((2, 2, 2))
        ],
    )(part, qkv, qkv, qkv, gate, strip, own, peer, came_own, came_peer)


def attend_back_kernel(
    q_ref, k_ref, v_ref, prob_ref, go_ref, wide_ref, gq_ref, gk_ref, gv_ref, sums_ref, near_ref
):
    scale = HDIM ** (-0.5)
    blocks = LMAX // TILE
    member = (
        lax.broadcasted_iota(jnp.int32, (AUG, LMAX), 0)
        == lax.broadcasted_iota(jnp.int32, (AUG, LMAX), 1) // TILE
    )
    queries = jnp.concatenate([q_ref[...], member.astype(F32).astype(BF16)], axis=0)
    near = [jnp.zeros((TILE, TILE), F32) for _ in range(3)]
    key_total = jnp.zeros((HDIM + AUG, LMAX), F32)
    val_total = jnp.zeros((HDIM, LMAX), F32)
    for block in range(LMAX // ABLOCK):
        low = block * ABLOCK
        prob = prob_ref[0, :, low : low + ABLOCK]
        grad_out = go_ref[:, low : low + ABLOCK]
        soft = prob.astype(F32)
        grad_prob = dot(v_ref[...], grad_out, TN)
        wide = wide_ref[:, low : low + ABLOCK]
        inner = jnp.sum(grad_out.astype(F32) * wide, axis=0, keepdims=True)
        grad_scores = (soft * (grad_prob - inner)).astype(BF16)
        gq_ref[:, low : low + ABLOCK] = (dot(k_ref[...], grad_scores, NN) * scale).astype(BF16)
        key_total = key_total + dot(queries[:, low : low + ABLOCK], grad_scores, NT)
        val_total = val_total + dot(grad_out, prob, NT)
        for sub in range(ABLOCK // TILE):
            place = block * (ABLOCK // TILE) + sub
            for shift in (-1, 0, 1):
                at = place + shift
                if 0 <= at < blocks:
                    piece = grad_scores[at * TILE : (at + 1) * TILE, sub * TILE : (sub + 1) * TILE]
                    near[shift + 1] = near[shift + 1] + piece.astype(F32)
    gk_ref[...] = (key_total[:HDIM] * scale).astype(BF16)
    gv_ref[...] = val_total.astype(BF16)
    sums = key_total[HDIM : HDIM + blocks]
    sums_ref[0] = sums
    shifts = (
        lax.broadcasted_iota(jnp.int32, (blocks, LMAX), 1) // TILE
        - lax.broadcasted_iota(jnp.int32, (blocks, LMAX), 0)
    )

    def fold(tile):
        return jnp.sum(tile, axis=0, keepdims=True)

    def far(chosen):
        return folded(fold(jnp.where(chosen, sums, 0.0)))

    before, same, after = near
    for sign, base, other, shift in ((-1, 0, before, -1), (1, 16, after, 1)):
        near_offset = sign * offsets(0)
        far_offset = sign * offsets(shift)
        floor = 0 if sign < 0 else 1
        last = fold(jnp.where(near_offset >= floor, same, 0.0)) + fold(
            jnp.where(far_offset >= floor, other, 0.0)
        )
        for count, step in enumerate(NEAR_STEPS):
            following = fold(jnp.where(near_offset >= step, same, 0.0)) + fold(
                jnp.where(far_offset >= step, other, 0.0)
            )
            near_ref[0, base + count : base + count + 1] = last - following
            last = following
        near_ref[0, base + 15 : base + 16] = last + far(sign * shifts >= 2)


def attend_back(side, qkv, prob, grad_attended, wide, heads):
    blocks = LMAX // TILE
    rows = jax.ShapeDtypeStruct((heads * HDIM, LMAX), BF16)
    spec = pl.BlockSpec((HDIM, LMAX), lambda h: (h, 0))
    return call(
        attend_back_kernel,
        "attend_back",
        heads * 8 * LMAX * LMAX * HDIM * 4,
        heads * LMAX * LMAX * 2,
        48,
        side=side,
        grid=(heads,),
        in_specs=[
            spec,
            pl.BlockSpec((HDIM, LMAX), lambda h: (heads + h, 0)),
            pl.BlockSpec((HDIM, LMAX), lambda h: (2 * heads + h, 0)),
            pl.BlockSpec((1, LMAX, LMAX), lambda h: (h, 0, 0)),
            spec,
            spec,
        ],
        out_specs=[
            spec,
            spec,
            spec,
            pl.BlockSpec((1, blocks, LMAX), lambda h: (h, 0, 0)),
            pl.BlockSpec((1, BUCKETS, TILE), lambda h: (h, 0, 0)),
        ],
        out_shape=[
            rows,
            rows,
            rows,
            jax.ShapeDtypeStruct((heads, blocks, LMAX), F32),
            jax.ShapeDtypeStruct((heads, BUCKETS, TILE), F32),
        ],
    )(qkv, qkv, qkv, prob, grad_attended, wide)


def ffn_kernel(gate_ref, up_ref, down_ref, x_ref, cot_ref, hid_ref, gg_ref, gu_ref):
    gate = dot(gate_ref[...], x_ref[...], TN)
    up = dot(up_ref[...], x_ref[...], TN)
    grad = dot(down_ref[...], cot_ref[...], TN)
    square = gate * gate
    bend = jnp.tanh(GELU_C * gate * (1.0 + 0.044715 * square))
    half = 0.5 * (1.0 + bend)
    gelu = gate * half
    slope = half + 0.5 * gate * (1.0 - bend * bend) * (GELU_C * (1.0 + 3 * 0.044715 * square))
    hid_ref[...] = (gelu * up).astype(BF16)
    gg_ref[...] = (grad * up * slope).astype(BF16)
    gu_ref[...] = (grad * gelu).astype(BF16)


def ffn(w_gate, w_up, w_down_t, normed, cot):
    units = w_gate.shape[1]
    width = 256
    weight = pl.BlockSpec((D, width), lambda i: (0, i))
    whole = fixed_spec((D, LMAX))
    out = pl.BlockSpec((width, LMAX), lambda i: (i, 0))
    shape = jax.ShapeDtypeStruct((units, LMAX), BF16)
    return call(
        ffn_kernel,
        "ffn",
        6 * D * units * LMAX,
        3 * D * units * 2 + 2 * D * LMAX * 2 + 3 * units * LMAX * 2,
        48,
        grid=(units // width,),
        in_specs=[weight, weight, weight, whole, whole],
        out_specs=[out, out, out],
        out_shape=[shape, shape, shape],
    )(w_gate, w_up, w_down_t, normed, cot)


def weight_grad_kernel(a_own, a_peer, b_own, b_peer, out_ref):
    total = dot(a_own[...], b_own[...], NT) + dot(a_peer[...], b_peer[...], NT)
    out_ref[...] = total.astype(BF16)


def weight_grad(a_own, a_peer, b_own, b_peer):
    units = a_own.shape[0]
    width = 256
    left = pl.BlockSpec((width, LMAX), lambda i: (i, 0))
    whole = fixed_spec((D, LMAX))
    return call(
        weight_grad_kernel,
        "weight_grad",
        4 * D * units * LMAX,
        4 * D * LMAX + 4 * units * LMAX + 2 * units * D,
        48,
        grid=(units // width,),
        in_specs=[left, left, whole, whole],
        out_specs=pl.BlockSpec((width, D), lambda i: (i, 0)),
        out_shape=jax.ShapeDtypeStruct((units, D), BF16),
    )(a_own, a_peer, b_own, b_peer)


def project_kernel(count, *refs):
    total = dot(refs[0][...], refs[count][...], NN)
    for i in range(1, count):
        total = total + dot(refs[i][...], refs[count + i][...], NN)
    refs[-1][...] = total.astype(refs[-1].dtype)


def project(side, weights, values, dtype):
    count = len(weights)
    units = weights[0].shape[1]
    width = D // 4
    weight = pl.BlockSpec((width, units), lambda i: (i, 0))
    whole = fixed_spec((units, LMAX))
    return call(
        functools.partial(project_kernel, count),
        "project",
        2 * count * D * units * LMAX,
        2 * count * (D * units + units * LMAX) + 4 * D * LMAX,
        48,
        side=side,
        grid=(D // width,),
        in_specs=[weight] * count + [whole] * count,
        out_specs=pl.BlockSpec((width, LMAX), lambda i: (i, 0)),
        out_shape=jax.ShapeDtypeStruct((D, LMAX), dtype),
    )(*weights, *values)


def fold_kernel(bit_ref, keep_ref, came_ref, keep_out, give_out):
    mine = bit_ref[0]
    for out, which in ((keep_out, mine), (give_out, 1 - mine)):
        total = keep_ref[:, which].astype(F32) + came_ref[:, which].astype(F32)
        out[...] = total.astype(BF16)


def fold(bit, keep, came):
    outer, _, rows, width = keep.shape
    steps = 2 if outer % 2 == 0 else 1
    block = pl.BlockSpec((outer // steps, 2, rows, width), lambda i: (i, 0, 0, 0))
    out = pl.BlockSpec((outer // steps, rows, width), lambda i: (i, 0, 0))
    shape = jax.ShapeDtypeStruct((outer, rows, width), BF16)
    return call(
        fold_kernel,
        "fold",
        4 * keep.size,
        6 * keep.size,
        48,
        grid=(steps,),
        in_specs=[SMEM, block, block],
        out_specs=[out, out],
        out_shape=[shape, shape],
    )(bit.reshape(1), keep, came)


def across(values, bit):
    size = lax.axis_size("dp")
    return lax.ppermute(values, "dp", [(i, i ^ (1 << bit)) for i in range(size)])


def bit_of(bit):
    return (lax.axis_index("dp") >> bit) & 1


def stacked(values, came, mine, axis):
    return jnp.where(mine == 0, jnp.stack([values, came], axis), jnp.stack([came, values], axis))


def sum_everywhere(keep, came):
    bits = lax.axis_size("dp").bit_length() - 1
    rows = keep.shape[1] // 4
    keep, came = (v.reshape(4, 2, 2, rows, D) for v in (keep, came))
    keep_x, give_x = fold(
        bit_of(0), keep[:2].reshape(4, 2, rows, D), came[:2].reshape(4, 2, rows, D)
    )
    keep_y, give_y = fold(
        bit_of(1), keep[2:].reshape(2, 2, 2 * rows, D), came[2:].reshape(2, 2, 2 * rows, D)
    )
    came_x, came_y = across(give_x, 0), across(give_y, 1)
    keep_x, give_x = fold(
        bit_of(1), keep_x.reshape(2, 2, rows, D), came_x.reshape(2, 2, rows, D)
    )
    keep_y, give_y = fold(
        bit_of(0), keep_y.reshape(2, 2, rows, D), came_y.reshape(2, 2, rows, D)
    )
    came_x, came_y = across(give_x, 1), across(give_y, 0)
    keep = jnp.concatenate([keep_x, keep_y], axis=0).reshape(2, 2, rows, D)
    came = jnp.concatenate([came_x, came_y], axis=0).reshape(2, 2, rows, D)
    keep, give = fold(bit_of(2), keep, came)
    came = across(give, 2)
    keep, give = fold(bit_of(3), keep.reshape(1, 2, rows, D), came.reshape(1, 2, rows, D))
    came = across(give, 3)
    total = (keep.astype(F32) + came.astype(F32)).astype(BF16)
    for bit in range(4, bits):
        total = (total.astype(F32) + across(total, bit).astype(F32)).astype(BF16)
    total = stacked(total, across(total, 3), bit_of(3), 1)
    total = stacked(total, across(total, 2), bit_of(2), 2).reshape(4, rows, D)
    total_x, total_y = total[:2], total[2:]
    total_x = stacked(total_x, across(total_x, 1), bit_of(1), 1)
    total_y = stacked(total_y, across(total_y, 0), bit_of(0), 1)
    total_x = stacked(total_x, across(total_x, 0), bit_of(0), 2)
    total_y = stacked(total_y, across(total_y, 1), bit_of(1), 1)
    return [v.reshape(4 * rows, D).astype(F32) for v in (*total_x, *total_y)]


def sum_small(values):
    bits = lax.axis_size("dp").bit_length() - 1
    values = values + swap(values)
    for bit in range(bits):
        values = values + across(values, bit)
    return values


def halve(values, order):
    size = lax.axis_size("dp")
    bits = size.bit_length() - 1
    index = lax.axis_index("dp")
    rows = values.shape[0] // size
    values = values.reshape((2,) * bits + (rows, values.shape[1]))
    left = list(range(bits - 1, -1, -1))
    for step, bit in enumerate(order):
        axis = left.index(bit)
        left.pop(axis)
        mine = (index >> bit) & 1
        keep = lax.dynamic_index_in_dim(values, mine, axis, keepdims=False)
        give = lax.dynamic_index_in_dim(values, 1 - mine, axis, keepdims=False)
        came = lax.ppermute(give, "dp", [(i, i ^ (1 << bit)) for i in range(size)])
        total = keep.astype(F32) + came.astype(F32)
        values = total if step == bits - 1 else total.astype(BF16)
    return values


def swap(values):
    return lax.ppermute(values, "mp", [(0, 1), (1, 0)])


def body(
    tokens,
    cotangent,
    lengths,
    keep_mask,
    ln_attn,
    w_query,
    w_key,
    w_value,
    w_attn_out,
    rel_table,
    w_delete,
    ln_ffn,
    w_gate,
    w_up,
    w_ffn_out,
):
    dev_count = lax.axis_size("dp")
    bits = dev_count.bit_length() - 1
    part = lax.axis_index("mp")
    inner = 2 * w_query.shape[1]
    heads = inner // HDIM
    half = tokens.shape[1]
    first = part == 0
    part_ref = part.reshape(1).astype(jnp.int32)

    def in_parts(own, peer, axis):
        return jnp.where(
            first, jnp.concatenate([own, peer], axis), jnp.concatenate([peer, own], axis)
        )

    def home(values):
        mine = lax.dynamic_slice_in_dim(values, part * half, half, 0)
        other = lax.dynamic_slice_in_dim(values, (1 - part) * half, half, 0)
        return spread(part_ref, slot, mine, swap(other)).T

    own_weights = (w_query.T, w_key.T, w_value.T, w_attn_out)
    slot, count, stack = places(part_ref, lengths, keep_mask.reshape(1, ROWS_DEV), own_weights)
    came_stack = swap(stack)
    own_tokens, peer_tokens = compact(part_ref, slot, tokens.T)
    came_tokens = swap(peer_tokens)
    own_cot, peer_cot, w_qkv, w_out = compact_join(
        part_ref, slot, cotangent.T, stack, came_stack
    )
    came_cot_own, came_cot_peer = swap(peer_cot), swap(own_cot)
    table = in_parts(rel_table, swap(rel_table), 1)
    strip = bias_strip(table, heads)
    columns = jnp.stack([ln_attn, ln_ffn, w_delete.astype(F32)], axis=1)

    state, normed_one, qkv, gate_rows, del_logit, scale_one = input_part(
        part_ref, own_tokens, came_tokens, columns, w_qkv, count
    )
    prob, attended, wide, cot_own, cot_peer = attend(
        part_ref, qkv, gate_rows, strip, own_cot, peer_cot, came_cot_own, came_cot_peer, heads
    )
    mid, normed_two, scale_two = middle_part(w_out, attended, state, columns)
    w_down_t = w_ffn_out.T
    share = w_gate.shape[1] // dev_count
    if bits == 4 and share % 16 == 0:
        cut = (share // 2 + 15) // 16 * 16
        one = feed(0, cut, w_gate, w_up, w_down_t, normed_two, cot_own, cot_peer, ())
        two = feed(1, cut, w_gate, w_up, w_down_t, normed_two, cot_own, cot_peer, one[4:8])
        keep_x, give_x, keep_y, give_y = two[4:8]
        up_x = (keep_x, across(give_x, 0))
        up_y = (keep_y, across(give_y, 1))
        grad_mid, grad_attn, grad_attended, sum_ffn = after_feed(
            (one[0], two[0], one[1], two[1]), mid, cot_own, columns, scale_two, w_out
        )
        grad_q, grad_k, grad_v, sums, near = attend_back(
            (), qkv, prob, grad_attended, wide, heads
        )
        keep, give = head_grads(part_ref, grad_q, grad_k, grad_v, normed_one, attended, grad_attn)
        totals, grad_up, small, state_own, state_came, mixed_own, mixed_came = tail(
            keep, give, up_x, up_y, sum_ffn, near.reshape(heads * BUCKETS, TILE),
            (scale_one, del_logit, sums, columns),
            (
                grad_q, grad_k, grad_v, normed_one, state, grad_mid, one[2], two[2], one[3], two[3],
                mid, w_qkv,
            ),
        )
        mixed = spread(part_ref, slot, mixed_own, mixed_came).T
        total_q, total_v, total_k, total_out = totals.reshape(4, inner // 2, D).astype(F32)
        grad_tokens = spread(part_ref, slot, state_own, state_came).T
        grad_ln_ffn, grad_ln_attn, grad_w_delete = small[0], small[1], small[2]
        grad_table = small[3, : heads * BUCKETS].reshape(heads, BUCKETS).T
        grad_down, grad_gate = jnp.where(bit_of(3) == 0, one[8], two[8])
    else:
        normed_two_peer = swap(normed_two)
        hid_own, gg_own, gu_own = ffn(w_gate, w_up, w_down_t, normed_two, cot_own)
        hid_peer, gg_peer, gu_peer = ffn(w_gate, w_up, w_down_t, normed_two_peer, cot_peer)
        order = tuple(range(bits))
        grad_down = halve(weight_grad(hid_own, hid_peer, cot_own, cot_peer), order)
        grad_gate = halve(weight_grad(gg_own, gg_peer, normed_two, normed_two_peer), order)
        grad_up = halve(weight_grad(gu_own, gu_peer, normed_two, normed_two_peer), order)
        back_peer = project((), (w_gate, w_up), (gg_peer, gu_peer), BF16)
        grad_mid, grad_attn, grad_attended, sum_ffn = middle_back(
            w_gate, w_up, gg_own, gu_own, swap(back_peer), mid, cot_own, columns, scale_two, w_out
        )
        grad_q, grad_k, grad_v, sums, near = attend_back(
            (), qkv, prob, grad_attended, wide, heads
        )
        keep, give = head_grads(part_ref, grad_q, grad_k, grad_v, normed_one, attended, grad_attn)
        total_q, total_v, total_k, total_out = sum_everywhere(keep, swap(give))
        grad_state, sum_attn, sum_delete = input_back(
            (), grad_q, grad_k, grad_v, w_qkv, normed_one, state, grad_mid, scale_one, del_logit,
            sums, columns,
        )
        grad_tokens = home(grad_state)
        grad_table = jnp.sum(near, axis=2).T
        small = jnp.concatenate(
            [jnp.sum(v, axis=1) for v in (sum_ffn, sum_attn, sum_delete)]
            + [grad_table.reshape(-1)]
        )
        small = sum_small(small)
        grad_ln_ffn, grad_ln_attn = small[:D], small[D : 2 * D]
        grad_w_delete = small[2 * D : 3 * D]
        grad_table = small[3 * D :].reshape(BUCKETS, heads)
        mixed_peer = project((), (w_down_t,), (hid_peer,), BF16)
        mixed = home(mixed_part(w_down_t, hid_own, swap(mixed_peer), mid))

    def own_half(values):
        return lax.dynamic_slice_in_dim(values, part * half, half, 0)

    return (
        mixed,
        grad_tokens,
        own_half(grad_ln_attn),
        total_q.T,
        total_k.T,
        total_v.T,
        total_out,
        lax.dynamic_slice_in_dim(grad_table, part * (heads // 2), heads // 2, 1),
        grad_w_delete,
        own_half(grad_ln_ffn),
        grad_gate.T,
        grad_up.T,
        grad_down,
    )


def solution(mesh):
    return jax.shard_map(
        body,
        mesh=mesh,
        in_specs=(
            P("dp", "mp"),
            P("dp", "mp"),
            P("dp"),
            P("dp"),
            P(),
            P(None, "mp"),
            P(None, "mp"),
            P(None, "mp"),
            P("mp", None),
            P(None, "mp"),
            P(),
            P(),
            P(None, "mp"),
            P(None, "mp"),
            P("mp", None),
        ),
        out_specs=(
            P("dp", "mp"),
            P("dp", "mp"),
            P("mp"),
            P(None, "mp"),
            P(None, "mp"),
            P(None, "mp"),
            P("mp", None),
            P(None, "mp"),
            P(),
            P("mp"),
            P(None, ("mp", "dp")),
            P(None, ("mp", "dp")),
            P(("mp", "dp"), None),
        ),
        check_vma=False,
    )
```

```python
import functools

import jax
import jax.numpy as jnp
import numpy as np
from jax import lax
from jax.experimental import pallas as pl
from jax.experimental.pallas import tpu as pltpu
from jax.sharding import PartitionSpec as P

D = 1472
HDIM = 64
BUCKETS = 32
LMAX = 1024
ROWS_DEV = 2048

EPSILON = 1e-06
DELETE_DEPTH = 4.0
NEG_LARGE = -1e30
NEAR_STEPS = (1, 2, 3, 4, 5, 6, 7, 8, 12, 16, 23, 32, 46, 64, 91)
TILE = 128
QBLOCK = 256
ABLOCK = 512
AUG = 16
F32 = jnp.float32
BF16 = jnp.bfloat16
GELU_C = float(np.sqrt(2.0 / np.pi))

NN = (((1,), (0,)), ((), ()))
TN = (((0,), (0,)), ((), ()))
NT = (((1,), (1,)), ((), ()))


def dot(a, b, dims):
    return lax.dot_general(a, b, dims, preferred_element_type=F32)


def with_side(kernel, inputs, outputs, pairs, bits_ref, *refs):
    first = inputs + 2 * pairs
    last = first + outputs + 2 * pairs
    kernel(*refs[:inputs], *refs[first : first + outputs], *refs[last:])
    for pair in range(pairs):
        keep_ref, came_ref = refs[inputs + 2 * pair : inputs + 2 * pair + 2]
        outs = refs[first + outputs + 2 * pair : first + outputs + 2 * pair + 2]
        mine = bits_ref[pair]
        for out, which in zip(outs, (mine, 1 - mine)):
            total = keep_ref[:, which].astype(F32) + came_ref[:, which].astype(F32)
            out[...] = total.astype(BF16)


def call(kernel, name, flops, nbytes, limit, side=(), **kw):
    for _, keep, came in side:
        nbytes += 6 * keep.size
    extra = ()
    outputs = 1
    if side:
        single = not isinstance(kw["out_shape"], list)
        out_specs = [kw["out_specs"]] if single else list(kw["out_specs"])
        out_shape = [kw["out_shape"]] if single else list(kw["out_shape"])
        outputs, inputs = len(out_shape), len(kw["in_specs"])
        in_specs = list(kw["in_specs"])
        for _, keep, came in side:
            outer, _, rows, width = keep.shape
            block = pl.BlockSpec(
                (1, 2, rows, width), lambda i, n=outer: (jnp.minimum(i, n - 1), 0, 0, 0)
            )
            out = pl.BlockSpec(
                (1, rows, width), lambda i, n=outer: (jnp.minimum(i, n - 1), 0, 0)
            )
            in_specs += [block, block]
            out_specs += [out, out]
            out_shape += [jax.ShapeDtypeStruct((outer, rows, width), BF16)] * 2
            extra += (keep, came)
        kernel = functools.partial(with_side, kernel, inputs, outputs, len(side))
        kw.update(in_specs=[SMEM] + in_specs, out_specs=out_specs, out_shape=out_shape)
    run = pl.pallas_call(
        kernel,
        name=name,
        cost_estimate=pl.CostEstimate(
            flops=int(flops), bytes_accessed=int(nbytes), transcendentals=0
        ),
        compiler_params=pltpu.CompilerParams(vmem_limit_bytes=limit << 20),
        **kw,
    )
    if not side:
        return run

    def launch(*args):
        out = run(jnp.stack([bit for bit, _, _ in side]), *args, *extra)
        main = out[0] if single else out[:outputs]
        return main, out[outputs:]

    return launch


VMEM = pl.BlockSpec(memory_space=pltpu.VMEM)
SMEM = pl.BlockSpec(memory_space=pltpu.SMEM)
ANY = pl.BlockSpec(memory_space=pl.ANY)


def place_kernel(
    part_ref, length_ref, mask_ref, q_ref, k_ref, v_ref, out_ref, slot_ref, count_ref, stack_ref
):
    for i, ref in enumerate((q_ref, k_ref, v_ref, out_ref)):
        stack_ref[i] = ref[...]
    mask = mask_ref[...]
    rows = lax.broadcasted_iota(jnp.int32, (1, ROWS_DEV), 1)
    first = (rows < length_ref[0]).astype(jnp.int32)
    pieces = []
    before = jnp.zeros((1, 1), F32)
    ahead = lax.broadcasted_iota(jnp.int32, (QBLOCK, QBLOCK), 0) <= lax.broadcasted_iota(
        jnp.int32, (QBLOCK, QBLOCK), 1
    )
    ahead = ahead.astype(F32).astype(BF16)
    flags = mask.astype(F32).astype(BF16)
    for block in range(ROWS_DEV // QBLOCK):
        part = flags[:, block * QBLOCK : (block + 1) * QBLOCK]
        ranks = dot(jnp.broadcast_to(part, (16, QBLOCK)), ahead, NN)[:1] + before
        before = ranks[:, QBLOCK - 1 :]
        pieces.append(ranks)
    ranks = jnp.concatenate(pieces, axis=1).astype(jnp.int32)
    kept_first = jnp.sum(mask * first, axis=1, keepdims=True)
    total = jnp.sum(mask, axis=1, keepdims=True)
    rank = ranks - 1 + jnp.where(first > 0, 0, LMAX - kept_first)
    slot_ref[...] = jnp.where(mask > 0, rank, -1)
    count = jnp.where(part_ref[0] == 0, kept_first, total - kept_first)
    count_ref[...] = jnp.broadcast_to(count, (1, 128))


def places(part, lengths, mask, weights):
    return call(
        place_kernel,
        "places",
        1e6,
        1e5,
        16,
        in_specs=[SMEM, SMEM, VMEM] + [VMEM] * 4,
        out_specs=[VMEM, VMEM, VMEM],
        out_shape=[
            jax.ShapeDtypeStruct((1, ROWS_DEV), jnp.int32),
            jax.ShapeDtypeStruct((1, 128), jnp.int32),
            jax.ShapeDtypeStruct((4, *weights[0].shape), BF16),
        ],
    )(part, lengths, mask, *weights)


def compact_half(item, slot_ref, x_ref, out_ref):
    for block in range(LMAX // QBLOCK):
        width = ROWS_DEV - 512 - block * QBLOCK
        start = pl.multiple_of(item * 512 + block * QBLOCK, 128)
        ids = item * LMAX + block * QBLOCK + lax.broadcasted_iota(jnp.int32, (QBLOCK, 1), 0)
        hot = (slot_ref[:, pl.ds(start, width)] == ids).astype(F32).astype(BF16)
        rows = dot(x_ref[:, pl.ds(start, width)], hot, NT)
        out_ref[:, block * QBLOCK : (block + 1) * QBLOCK] = rows.astype(BF16)


def compact_kernel(part_ref, slot_ref, x_ref, own_ref, peer_ref):
    compact_half(part_ref[0], slot_ref, x_ref, own_ref)
    compact_half(1 - part_ref[0], slot_ref, x_ref, peer_ref)


def halves(part, own, came, whole, hold, sems):
    size = own.shape[0]
    copies_in, copies_out = [], []
    for i, (ref, place) in enumerate(((own, part), (came, 1 - part))):
        copies_in.append(pltpu.make_async_copy(ref, hold.at[i], sems.at[0, i]))
        target = whole.at[pl.ds(pl.multiple_of(place * size, 16), size)]
        copies_out.append(pltpu.make_async_copy(hold.at[i], target, sems.at[1, i]))
    return copies_in, copies_out


def compact_join_kernel(
    part_ref, slot_ref, x_ref, stack_ref, came_ref, own_ref, peer_ref, qkv_ref, out_ref, hold, sems
):
    part = part_ref[0]
    inner = out_ref.shape[0]
    copies_in, copies_out = [], []
    for i in range(4):
        whole = qkv_ref.at[pl.ds(i * inner, inner)] if i < 3 else out_ref
        ins, outs = halves(part, stack_ref.at[i], came_ref.at[i], whole, hold.at[i], sems.at[i])
        copies_in += ins
        copies_out += outs
    for copy in copies_in:
        copy.start()
    compact_half(part, slot_ref, x_ref, own_ref)
    for copy, following in zip(copies_in, copies_out):
        copy.wait()
        following.start()
    compact_half(1 - part, slot_ref, x_ref, peer_ref)
    for copy in copies_out:
        copy.wait()


def compact_join(part, slot, columns, stack, came):
    width = columns.shape[0]
    inner = 2 * stack.shape[1]
    shape = jax.ShapeDtypeStruct((width, LMAX), BF16)
    return call(
        compact_join_kernel,
        "compact_join",
        2 * width * 2 * 4608 * 256,
        width * 2048 * 4,
        24,
        in_specs=[SMEM, VMEM, VMEM, ANY, ANY],
        out_specs=[VMEM, VMEM, ANY, ANY],
        out_shape=[
            shape,
            shape,
            jax.ShapeDtypeStruct((3 * inner, D), BF16),
            jax.ShapeDtypeStruct((inner, D), BF16),
        ],
        scratch_shapes=[
            pltpu.VMEM((4, 2, inner // 2, D), BF16), pltpu.SemaphoreType.DMA((4, 2, 2))
        ],
    )(part, slot, columns, stack, came)


def compact(part, slot, columns):
    width = columns.shape[0]
    shape = jax.ShapeDtypeStruct((width, LMAX), BF16)
    return call(
        compact_kernel,
        "compact",
        2 * width * 2 * 4608 * 256,
        width * 2048 * 4,
        16,
        in_specs=[SMEM, VMEM, VMEM],
        out_specs=[VMEM, VMEM],
        out_shape=[shape, shape],
    )(part, slot, columns)


def spread_kernel(part_ref, slot_ref, own_ref, peer_ref, out_ref):
    first = part_ref[0] == 0
    items = (
        jnp.where(first, own_ref[...], peer_ref[...]),
        jnp.where(first, peer_ref[...], own_ref[...]),
    )
    for block in range(ROWS_DEV // QBLOCK):
        end = (block + 1) * QBLOCK
        slots = slot_ref[:, end - QBLOCK : end]
        total = None
        for item in range(2):
            reach = min(end - 512 * item, LMAX)
            if reach <= 0 or (item == 0 and end > LMAX):
                continue
            ids = item * LMAX + lax.broadcasted_iota(jnp.int32, (reach, 1), 0)
            hot = (slots == ids).astype(F32).astype(BF16)
            part = dot(items[item][:, :reach], hot, NN)
            total = part if total is None else total + part
        out_ref[:, end - QBLOCK : end] = total.astype(BF16)


def spread(part, slot, own, peer):
    width = own.shape[0]
    return call(
        spread_kernel,
        "spread",
        2 * width * 7168 * 256,
        width * 2048 * 4,
        16,
        in_specs=[SMEM, VMEM, VMEM, VMEM],
        out_specs=VMEM,
        out_shape=jax.ShapeDtypeStruct((width, ROWS_DEV), BF16),
    )(part, slot, own, peer)


COLUMNS = 3
ROWS = pl.BlockSpec((D, QBLOCK), lambda i: (0, i))
LINE = pl.BlockSpec((1, QBLOCK), lambda i: (0, i))
COLUMN = pl.BlockSpec((D, COLUMNS), lambda i: (0, 0))
SUMS = pl.BlockSpec((D, 128), lambda i: (0, 0))


def fixed_spec(shape):
    return pl.BlockSpec(shape, lambda i: (0,) * len(shape), pipeline_mode=pl.Buffered(1))


def whole_spec(array):
    return fixed_spec(array.shape)


def line(rows=1, dtype=F32):
    return jax.ShapeDtypeStruct((rows, LMAX), dtype)


def folded(values):
    return sum(values[:, i * 128 : (i + 1) * 128] for i in range(values.shape[1] // 128))


def input_kernel(
    part_ref, own_ref, came_ref, gain_ref, weight_ref, count_ref,
    state_ref, normed_ref, qkv_ref, gate_ref, logit_ref, scale_ref,
):
    first = part_ref[0] == 0
    own, came = own_ref[...], came_ref[...]
    half = own.shape[0]
    state_ref[:half] = jnp.where(first, own, came)
    state_ref[half:] = jnp.where(first, came, own)
    state = state_ref[...].astype(F32)
    scale = lax.rsqrt(jnp.sum(state * state, axis=0, keepdims=True) / D + EPSILON)
    normed = (state * scale * gain_ref[:, 0:1]).astype(BF16)
    normed_ref[...] = normed
    scale_ref[...] = scale
    qkv_ref[...] = dot(weight_ref[...], normed, NN).astype(BF16)
    logit = jnp.sum(normed.astype(F32) * gain_ref[:, 2:3], axis=0, keepdims=True)
    logit_ref[...] = logit
    gate = -DELETE_DEPTH * jax.nn.sigmoid(-logit)
    rows = pl.program_id(0) * QBLOCK + lax.broadcasted_iota(jnp.int32, (1, QBLOCK), 1)
    gate = jnp.where(rows < count_ref[:, :1], gate, NEG_LARGE)
    place = lax.broadcasted_iota(jnp.int32, (AUG, QBLOCK), 0)
    gate_ref[...] = jnp.where(place == 0, gate, 0.0).astype(BF16)


def input_part(part, own, came, gain, weights, count):
    inner = weights.shape[0]
    half = pl.BlockSpec((own.shape[0], QBLOCK), lambda i: (0, i))
    return call(
        input_kernel,
        "norm_project",
        2 * D * LMAX * weights.shape[0],
        D * LMAX * 10,
        48,
        grid=(LMAX // QBLOCK,),
        in_specs=[SMEM, half, half, COLUMN, whole_spec(weights), whole_spec(count)],
        out_specs=[
            ROWS,
            ROWS,
            pl.BlockSpec((inner, QBLOCK), lambda i: (0, i)),
            pl.BlockSpec((AUG, QBLOCK), lambda i: (0, i)),
            LINE,
            LINE,
        ],
        out_shape=[line(D, BF16), line(D, BF16), line(inner, BF16), line(AUG, BF16), line(), line()],
    )(part, own, came, gain, weights, count)


def middle_kernel(weight_ref, attended_ref, state_ref, gain_ref, mid_ref, normed_ref, scale_ref):
    mid = state_ref[...].astype(F32) + dot(weight_ref[...], attended_ref[...], TN)
    scale = lax.rsqrt(jnp.sum(mid * mid, axis=0, keepdims=True) / D + EPSILON)
    mid_ref[...] = mid
    scale_ref[...] = scale
    normed_ref[...] = (mid * scale * gain_ref[:, 1:2]).astype(BF16)


def middle_part(weights, attended, state, gain):
    inner = attended.shape[0]
    return call(
        middle_kernel,
        "attention_out_norm",
        2 * D * LMAX * inner,
        D * LMAX * 8,
        48,
        grid=(LMAX // QBLOCK,),
        in_specs=[
            whole_spec(weights),
            pl.BlockSpec((inner, QBLOCK), lambda i: (0, i)),
            ROWS,
            COLUMN,
        ],
        out_specs=[ROWS, ROWS, LINE],
        out_shape=[line(D), line(D, BF16), line()],
    )(weights, attended, state, gain)


def middle_back_kernel(
    gate_ref, up_ref, gg_ref, gu_ref, came_ref, mid_ref, cot_ref, gain_ref, scale_ref, weight_ref,
    grad_mid_ref, grad_attn_ref, attended_ref, sums_ref,
):
    grad = dot(gate_ref[...], gg_ref[...], NN) + dot(up_ref[...], gu_ref[...], NN)
    grad = grad + came_ref[...].astype(F32)
    mid, scale = mid_ref[...], scale_ref[...]
    weighted = grad * gain_ref[:, 1:2]
    inner = jnp.sum(weighted * mid, axis=0, keepdims=True)
    grad_mid = (
        cot_ref[...].astype(F32) + scale * weighted - mid * (scale * scale * scale * inner / D)
    )
    grad_mid_ref[...] = grad_mid
    grad_attn = grad_mid.astype(BF16)
    grad_attn_ref[...] = grad_attn
    attended_ref[...] = dot(weight_ref[...], grad_attn, NN).astype(BF16)

    @pl.when(pl.program_id(0) == 0)
    def _():
        sums_ref[...] = jnp.zeros_like(sums_ref)

    sums_ref[...] += folded(grad * (mid * scale))


def middle_back(w_gate, w_up, gg, gu, came, mid, cot, gain, scale, w_out):
    inner, units = w_out.shape[0], w_gate.shape[1]
    unit_rows = pl.BlockSpec((units, QBLOCK), lambda i: (0, i))
    return call(
        middle_back_kernel,
        "norm_back",
        4 * D * LMAX * units,
        D * LMAX * 20 + 4 * D * units,
        48,
        grid=(LMAX // QBLOCK,),
        in_specs=[
            whole_spec(w_gate), whole_spec(w_up), unit_rows, unit_rows, ROWS, ROWS, ROWS, COLUMN,
            LINE, whole_spec(w_out),
        ],
        out_specs=[ROWS, ROWS, pl.BlockSpec((inner, QBLOCK), lambda i: (0, i)), SUMS],
        out_shape=[
            line(D), line(D, BF16), line(inner, BF16), jax.ShapeDtypeStruct((D, 128), F32),
        ],
    )(w_gate, w_up, gg, gu, came, mid, cot, gain, scale, w_out)


def input_back_block(q, k, v, weight_ref, normed, state, grad_mid, scale, logit, sums, columns):
    heads = sums.shape[0]
    gate = sums[0]
    for head in range(1, heads):
        gate = gate + sums[head]
    gate = jnp.sum(gate, axis=0, keepdims=True)
    grad_logit = gate * DELETE_DEPTH * jax.nn.sigmoid(logit) * jax.nn.sigmoid(-logit)
    inner = q.shape[0]
    grad = dot(weight_ref[:inner], q, TN)
    grad = grad + dot(weight_ref[inner : 2 * inner], k, TN)
    grad = grad + dot(weight_ref[2 * inner : 3 * inner], v, TN)
    grad = grad + columns[:, 2:3] * grad_logit
    state = state.astype(F32)
    weighted = grad * columns[:, 0:1]
    total = jnp.sum(weighted * state, axis=0, keepdims=True)
    grad_state = grad_mid + scale * weighted - state * (scale * scale * scale * total / D)
    gain_part = folded(grad * (state * scale))
    delete_part = folded(normed.astype(F32) * grad_logit)
    return grad_state.astype(BF16), gain_part, delete_part


def input_back_kernel(
    q_ref, k_ref, v_ref, weight_ref, normed_ref, state_ref, grad_mid_ref, scale_ref, logit_ref,
    sums_ref, columns_ref, grad_ref, gain_sum_ref, delete_sum_ref,
):
    grad_ref[...], gain_part, delete_part = input_back_block(
        q_ref[...], k_ref[...], v_ref[...], weight_ref, normed_ref[...], state_ref[...],
        grad_mid_ref[...], scale_ref[...], logit_ref[...], sums_ref[...], columns_ref[...],
    )

    @pl.when(pl.program_id(0) == 0)
    def _():
        gain_sum_ref[...] = jnp.zeros_like(gain_sum_ref)
        delete_sum_ref[...] = jnp.zeros_like(delete_sum_ref)

    gain_sum_ref[...] += gain_part
    delete_sum_ref[...] += delete_part


def input_back(side, q, k, v, weights, normed, state, grad_mid, scale, logit, sums, gain):
    inner = q.shape[0]
    head_rows = pl.BlockSpec((inner, QBLOCK), lambda i: (0, i))
    return call(
        input_back_kernel,
        "project_norm_back",
        6 * D * LMAX * inner,
        D * LMAX * 12,
        48,
        side=side,
        grid=(LMAX // QBLOCK,),
        in_specs=[
            head_rows, head_rows, head_rows, whole_spec(weights), ROWS, ROWS, ROWS, LINE, LINE,
            pl.BlockSpec((sums.shape[0], sums.shape[1], QBLOCK), lambda i: (0, 0, i)),
            COLUMN,
        ],
        out_specs=[ROWS, SUMS, SUMS],
        out_shape=[
            line(D, BF16),
            jax.ShapeDtypeStruct((D, 128), F32),
            jax.ShapeDtypeStruct((D, 128), F32),
        ],
    )(q, k, v, weights, normed, state, grad_mid, scale, logit, sums, gain)


def mixed_kernel(down_ref, hid_ref, came_ref, mid_ref, out_ref):
    mixed = mid_ref[...] + dot(down_ref[...], hid_ref[...], NN)
    out_ref[...] = (mixed + came_ref[...].astype(F32)).astype(BF16)


def mixed_part(down, hid, came, mid):
    width = D // 4
    units = down.shape[1]
    rows = pl.BlockSpec((width, LMAX), lambda i: (i, 0))
    return call(
        mixed_kernel,
        "mixed",
        2 * D * LMAX * units,
        D * LMAX * 8 + D * units * 2,
        48,
        grid=(D // width,),
        in_specs=[pl.BlockSpec((width, units), lambda i: (i, 0)), whole_spec(hid), rows, rows],
        out_specs=rows,
        out_shape=line(D, BF16),
    )(down, hid, came, mid)


def head_grad_kernel(part_ref, q_ref, v_ref, k_ref, attended_ref, normed_ref, back_ref, *outs):
    keep_ref, give_ref, hold = outs
    part = part_ref[0]
    rows = hold.shape[0] // 2
    pieces = (
        (q_ref, normed_ref), (v_ref, normed_ref), (k_ref, normed_ref), (attended_ref, back_ref),
    )
    for place, (left, right) in enumerate(pieces):
        hold[...] = dot(left[...], right[...], NT).astype(BF16)
        keep_ref[place] = hold[pl.ds(pl.multiple_of(part * rows, 16), rows)]
        give_ref[place] = hold[pl.ds(pl.multiple_of((1 - part) * rows, 16), rows)]


def head_grads(part, q, k, v, normed, attended, back):
    inner = q.shape[0]
    shape = jax.ShapeDtypeStruct((4, inner // 2, D), BF16)
    return call(
        head_grad_kernel,
        "head_grads",
        8 * D * LMAX * inner,
        D * LMAX * 4 + 4 * LMAX * inner * 2 + 16 * inner * D,
        36,
        in_specs=[SMEM] + [VMEM] * 6,
        out_specs=[VMEM, VMEM],
        out_shape=[shape, shape],
        scratch_shapes=[pltpu.VMEM((inner, D), BF16)],
    )(part, q, v, k, attended, normed, back)


MESH = pl.DeviceIdType.MESH


class Sender:
    def __init__(self, send_sems, recv_sems):
        self.send_sems, self.recv_sems, self.made = send_sems, recv_sems, []

    def start(self, source, target, device):
        place = len(self.made)
        copy = pltpu.make_async_remote_copy(
            src_ref=source,
            dst_ref=target,
            send_sem=self.send_sems.at[place],
            recv_sem=self.recv_sems.at[place],
            device_id=device,
            device_id_type=MESH,
        )
        copy.start()
        self.made.append(copy)
        return copy

    def finish(self):
        for copy in self.made:
            copy.wait_send()


def arrived(copies):
    for copy in copies:
        copy.wait_recv()


def plus(first, *others):
    total = first.astype(F32)
    for other in others:
        total = total + other.astype(F32)
    return total


def neighbours():
    me, part = lax.axis_index("dp"), lax.axis_index("mp")
    x, y, z = me % 2, (me // 2) % 2, me // 4
    across_x, across_y = 1 - 2 * x, 2 - 4 * y
    planes = [(z + k) % 4 for k in range(1, 4)]
    return dict(
        x=x,
        y=y,
        z=z,
        part=part,
        planes=planes,
        to_core=(me, 1 - part),
        to_x=(me + across_x, part),
        to_y=(me + across_y, part),
        to_corner=(me + across_x + across_y, part),
        to_plane=[(p * 4 + me % 4, part) for p in planes],
    )


def meet(devices):
    barrier = pltpu.get_barrier_semaphore()
    for device in devices:
        pl.semaphore_signal(barrier, inc=1, device_id=device, device_id_type=MESH)
    pl.semaphore_wait(barrier, len(devices))


CHUNK = 16


def tail_kernel(
    keep_ref, give_ref, keep_x, came_x, keep_y, came_y, ffn_sum_ref, near_ref,
    scale_ref, logit_ref, sums_ref, columns_ref,
    q_hbm, k_hbm, v_hbm, normed_hbm, state_hbm, grad_mid_hbm, mix_one, mix_two, mix_three, mix_four,
    mid_hbm, weight_hbm,
    out_ref, share_ref, vector_ref, own_ref, came_grad_ref, own_mixed_ref, came_mixed_ref,
    came_ref, total, from_x, from_y, sum_x, sum_y, last_x, last_y, plane_sum, from_planes,
    whole, from_whole,
    vector, vector_core, vector_near, vector_far, sent_grad, sent_mixed, block_hold,
    head_hold, half_hold, wide_hold, weight_ref, load_sems, weight_sem, send_sems, recv_sems,
):
    loads = {}

    def load_block(block):
        cols = slice(block * QBLOCK, (block + 1) * QBLOCK)
        slot = block % 2
        pairs = [
            (source.at[:, cols], head_hold.at[slot, i])
            for i, source in enumerate((q_hbm, k_hbm, v_hbm))
        ]
        pairs += [
            (source.at[:, cols], half_hold.at[slot, i])
            for i, source in enumerate((normed_hbm, state_hbm))
        ]
        pairs.append((grad_mid_hbm.at[:, cols], wide_hold.at[slot]))
        start_loads(("grad", block), slot, pairs)

    def load_mixed(block):
        cols = slice(block * QBLOCK, (block + 1) * QBLOCK)
        slot = block % 2
        pairs = [
            (source.at[:, cols], half_hold.at[slot, i])
            for i, source in enumerate((mix_one, mix_two, mix_three, mix_four))
        ]
        pairs.append((mid_hbm.at[:, cols], wide_hold.at[slot]))
        start_loads(("mixed", block), slot, pairs)

    def start_loads(key, slot, pairs):
        loads[key] = []
        for i, (source, target) in enumerate(pairs):
            copy = pltpu.make_async_copy(source, target, load_sems.at[slot, i])
            copy.start()
            loads[key].append(copy)

    weight_load = pltpu.make_async_copy(weight_hbm, weight_ref, weight_sem)
    weight_load.start()
    load_block(0)
    load_block(1)
    at = neighbours()
    x, y, z = at["x"], at["y"], at["z"]
    to_x, to_y = at["to_x"], at["to_y"]
    rows = keep_ref.shape[3]
    chunks = [slice(c * CHUNK, (c + 1) * CHUNK) for c in range(rows // CHUNK)]
    sender = Sender(send_sems, recv_sems)
    meet([at["to_core"], to_x, to_y, at["to_corner"], *at["to_plane"]])

    cores = [
        sender.start(give_ref.at[:, :, :, c], came_ref.at[:, :, :, c], at["to_core"])
        for c in chunks
    ]
    cut = keep_x.shape[1]
    whole[:, :cut] = plus(keep_x[...], came_x[...]).astype(BF16)
    whole[:, cut:] = plus(keep_y[...], came_y[...]).astype(BF16)
    wholes = [
        sender.start(whole.at[p], from_whole.at[k], device)
        for k, (p, device) in enumerate(zip(at["planes"], at["to_plane"]))
    ]

    def first(c):
        arrived([cores[c]])
        c = chunks[c]
        total[:, :, :, c] = plus(keep_ref[:, :, :, c], came_ref[:, :, :, c]).astype(BF16)
        return [
            sender.start(total.at[0:2, :, 1 - x, c], from_x.at[:, :, c], to_x),
            sender.start(total.at[2:4, 1 - y, :, c], from_y.at[:, :, c], to_y),
        ]

    def second(c, copies):
        arrived(copies)
        c = chunks[c]
        sum_x[:, :, c] = plus(total[0:2, :, x, c], from_x[:, :, c]).astype(BF16)
        sum_y[:, :, c] = plus(total[2:4, y, :, c], from_y[:, :, c]).astype(BF16)
        return [
            sender.start(sum_x.at[:, 1 - y, c], last_x.at[:, c], to_y),
            sender.start(sum_y.at[:, 1 - x, c], last_y.at[:, c], to_x),
        ]

    def third(c, copies):
        arrived(copies)
        c = chunks[c]
        plane_sum[0:2, c] = plus(sum_x[:, y, c], last_x[:, c]).astype(BF16)
        plane_sum[2:4, c] = plus(sum_y[:, x, c], last_y[:, c]).astype(BF16)
        return [
            sender.start(plane_sum.at[p, c], from_planes.at[k, c], device)
            for k, (p, device) in enumerate(zip(at["planes"], at["to_plane"]))
        ]

    def fourth(c, copies):
        arrived(copies)
        c = chunks[c]
        got = [from_planes[k, c] for k in range(3)]
        out_ref[z, y, x, c] = plus(plane_sum[z, c], *got).astype(BF16)
        here = out_ref.at[z, y, x, c]
        return [sender.start(here, here, device) for device in at["to_plane"]]

    def fifth(c, copies):
        arrived(copies)
        c = chunks[c]
        here_x, here_y = out_ref.at[0:2, y, x, c], out_ref.at[2:4, y, x, c]
        return [sender.start(here_x, here_x, to_y), sender.start(here_y, here_y, to_x)]

    def sixth(c, copies):
        arrived(copies)
        c = chunks[c]
        here_x, here_y = out_ref.at[0:2, :, x, c], out_ref.at[2:4, y, :, c]
        return [sender.start(here_x, here_x, to_x), sender.start(here_y, here_y, to_y)]

    stages = [first, second, third, fourth, fifth, sixth]
    flying = [None] * len(chunks)

    def advance(c, stage):
        flying[c] = stages[stage](c, flying[c]) if stage else first(c)

    half = own_ref.shape[0]
    mine = pl.ds(pl.multiple_of(at["part"] * half, 16), half)
    other = pl.ds(pl.multiple_of((1 - at["part"]) * half, 16), half)
    parts = []
    came_grads = []

    def part_out(cols, values, out_ref, sent_ref, came_ref):
        block_hold[...] = values
        out_ref[:, cols] = block_hold[mine]
        sent_ref[:, cols] = block_hold[other]
        came_grads.append(
            sender.start(sent_ref.at[:, cols], came_ref.at[:, cols], at["to_core"])
        )

    def compute(block):
        if block == 0:
            weight_load.wait()
        for copy in loads["grad", block]:
            copy.wait()
        cols = slice(block * QBLOCK, (block + 1) * QBLOCK)
        slot = block % 2
        grad, gain_part, delete_part = input_back_block(
            head_hold[slot, 0], head_hold[slot, 1], head_hold[slot, 2], weight_ref,
            half_hold[slot, 0], half_hold[slot, 1], wide_hold[slot], scale_ref[:, cols],
            logit_ref[:, cols], sums_ref[:, :, cols], columns_ref[...],
        )
        part_out(cols, grad, own_ref, sent_grad, came_grad_ref)
        parts.append((gain_part, delete_part))
        if block < 2:
            load_block(block + 2)
        else:
            load_mixed(block - 2)

    def compute_mixed(block):
        for copy in loads["mixed", block]:
            copy.wait()
        cols = slice(block * QBLOCK, (block + 1) * QBLOCK)
        slot = block % 2
        values = plus(wide_hold[slot], *[half_hold[slot, i] for i in range(4)]).astype(BF16)
        part_out(cols, values, own_mixed_ref, sent_mixed, came_mixed_ref)
        if block < 2:
            load_mixed(block + 2)

    ones = jnp.ones((8, 128), F32)

    def line_of(values):
        return lax.dot_general(
            ones, values, NT, preferred_element_type=F32, precision=lax.Precision.HIGHEST
        )[:1]

    advance(0, 0)
    compute(0)
    advance(0, 1)
    advance(1, 0)
    compute(1)
    advance(0, 2)
    advance(1, 1)
    advance(2, 0)
    compute(2)
    advance(0, 3)
    advance(1, 2)
    advance(2, 1)
    compute(3)
    advance(0, 4)
    advance(1, 3)
    advance(2, 2)
    vector[...] = jnp.zeros_like(vector)
    vector[0:1] = line_of(ffn_sum_ref[...])
    vector[1:2] = line_of(sum(p[0] for p in parts))
    vector[2:3] = line_of(sum(p[1] for p in parts))
    vector[3:4, : near_ref.shape[0]] = line_of(near_ref[...])
    vectors = [sender.start(vector, vector_core, at["to_core"])]
    advance(0, 5)
    advance(1, 4)
    compute_mixed(0)
    advance(2, 3)
    arrived(vectors)
    vector_core[...] = vector_core[...] + vector[...]
    vectors = [
        sender.start(vector_core, vector_near.at[k], device)
        for k, device in enumerate((to_x, to_y, at["to_corner"]))
    ]
    advance(1, 5)
    compute_mixed(1)
    advance(2, 4)
    compute_mixed(2)
    arrived(vectors)
    vector_ref[...] = vector_core[...] + vector_near[0] + vector_near[1] + vector_near[2]
    vectors = [
        sender.start(vector_ref, vector_far.at[k], device)
        for k, device in enumerate(at["to_plane"])
    ]
    advance(2, 5)
    compute_mixed(3)
    arrived(wholes)
    share_ref[...] = plus(whole[z], from_whole[0], from_whole[1], from_whole[2])
    for copies in flying:
        arrived(copies)
    arrived(came_grads)
    arrived(vectors)
    sender.finish()
    vector_ref[...] = vector_ref[...] + vector_far[0] + vector_far[1] + vector_far[2]


def tail(keep, give, up_x, up_y, ffn_sum, near, lines, far):
    rows = keep.shape[1] // 4
    (keep_x, came_x), (keep_y, came_y) = up_x, up_y
    cut, rest = keep_x.shape[1], keep_y.shape[1]
    share = cut + rest
    shape = (4, 2, 2, rows, D)
    copies = 80
    heads = far[0].shape[0]

    def hold(*dims, dtype=BF16):
        return pltpu.VMEM(dims, dtype)

    return pl.pallas_call(
        tail_kernel,
        name="tail",
        in_specs=[VMEM] * (8 + len(lines)) + [ANY] * len(far),
        out_specs=[VMEM] * 7,
        out_shape=[
            jax.ShapeDtypeStruct(shape, BF16),
            jax.ShapeDtypeStruct((share, D), F32),
            jax.ShapeDtypeStruct((8, D), F32),
            *[jax.ShapeDtypeStruct((D // 2, LMAX), BF16)] * 4,
        ],
        scratch_shapes=[
            hold(*shape), hold(*shape), hold(2, 2, rows, D), hold(2, 2, rows, D),
            hold(2, 2, rows, D), hold(2, 2, rows, D), hold(2, rows, D), hold(2, rows, D),
            hold(4, rows, D), hold(3, rows, D),
            hold(4, share, D), hold(3, share, D),
            hold(8, D, dtype=F32), hold(8, D, dtype=F32), hold(3, 8, D, dtype=F32),
            hold(3, 8, D, dtype=F32), hold(D // 2, LMAX), hold(D // 2, LMAX), hold(D, QBLOCK),
            hold(2, 3, heads, QBLOCK), hold(2, 4, D, QBLOCK), hold(2, D, QBLOCK, dtype=F32),
            hold(3 * heads, D),
            pltpu.SemaphoreType.DMA((2, 6)),
            pltpu.SemaphoreType.DMA,
            pltpu.SemaphoreType.DMA((copies,)),
            pltpu.SemaphoreType.DMA((copies,)),
        ],
        cost_estimate=pl.CostEstimate(
            flops=6 * D * LMAX * 384, bytes_accessed=60 << 20, transcendentals=0
        ),
        compiler_params=pltpu.CompilerParams(
            vmem_limit_bytes=63 << 20, collective_id=1, has_side_effects=True
        ),
    )(keep.reshape(shape), give.reshape(shape), keep_x, came_x, keep_y, came_y, ffn_sum, near, *lines, *far)


PLANES = 2


def feed_kernel(half, cut, *refs):
    (
        gate_hbm, up_hbm, down_hbm, normed_hbm, cot_own_hbm, cot_peer_hbm, *rest
    ) = refs
    if half:
        rest = rest[4:]
    (
        grad_own_hbm, grad_came_hbm, mixed_own_hbm, mixed_came_hbm,
        keep_x_hbm, give_x_hbm, keep_y_hbm, give_y_hbm, share_ref,
        weight, normed, cot, hidden, staged, blocks, up_blocks,
        came_x, came_y, last_x, last_y, from_planes,
        load_sems, store_sems, up_sems, send_sems, recv_sems, plane_send, plane_recv,
    ) = rest
    at = neighbours()
    x, y, z = at["x"], at["y"], at["z"]
    to_core, to_x, to_y = at["to_core"], at["to_x"], at["to_y"]
    units = weight.shape[2]
    rows = units // PLANES
    share = rows // 4
    sender = Sender(send_sems, recv_sems)
    order = (0, 1) if half == 0 else (1, 0)

    def load(place, source, target):
        copy = pltpu.make_async_copy(source, target, load_sems.at[place])
        copy.start()
        return copy

    columns = pl.ds(half * units, units)
    loads = [
        load(0, gate_hbm.at[:, columns], weight.at[0]),
        load(1, normed_hbm, normed.at[0]),
        load(2, up_hbm.at[:, columns], weight.at[1]),
        load(3, down_hbm.at[:, columns], weight.at[2]),
        load(4, cot_own_hbm, cot.at[0]),
        load(5, cot_peer_hbm, cot.at[1]),
    ]
    meet([to_core, to_x, to_y, *at["to_plane"]])
    exchange = sender.start(normed_hbm, normed.at[1], to_core)

    def activate(side, low, size):
        def step(block, carry):
            cols = pl.ds(pl.multiple_of(block * 512, 512), 512)
            span = slice(low, low + size)
            value = normed[side, :, cols]
            gate = dot(weight[0, :, span], value, TN)
            up = dot(weight[1, :, span], value, TN)
            grad = dot(weight[2, :, span], cot[side, :, cols], TN)
            square = gate * gate
            bend = jnp.tanh(GELU_C * gate * (1.0 + 0.044715 * square))
            whole = 0.5 * (1.0 + bend)
            gelu = gate * whole
            slope = whole + 0.5 * gate * (1.0 - bend * bend) * (
                GELU_C * (1.0 + 3 * 0.044715 * square)
            )
            hidden[0, side, span, cols] = (gelu * up).astype(BF16)
            hidden[1, side, span, cols] = (grad * up * slope).astype(BF16)
            hidden[2, side, span, cols] = (grad * gelu).astype(BF16)
            return carry

        lax.fori_loop(0, LMAX // 512, step, 0)

    def weight_block(matrix, plane, target):
        other = cot if matrix == 0 else normed
        span = slice(plane * rows, (plane + 1) * rows)
        for low, high in ((0, 768), (768, D)):
            total = dot(hidden[matrix, 0, span], other[0, low:high], NT)
            total = total + dot(hidden[matrix, 1, span], other[1, low:high], NT)
            target[:, :, :, low:high] = total.astype(BF16).reshape(2, 2, share, high - low)

    def first(b):
        block = blocks.at[b]
        return [
            sender.start(block.at[:, 1 - x, :cut], came_x.at[b], to_x),
            sender.start(block.at[1 - y, :, cut:], came_y.at[b], to_y),
        ]

    def second(b, copies):
        arrived(copies)
        block = blocks.at[b]
        block[:, x, :cut] = plus(block[:, x, :cut], came_x[b]).astype(BF16)
        block[y, :, cut:] = plus(block[y, :, cut:], came_y[b]).astype(BF16)
        return [
            sender.start(block.at[1 - y, x, :cut], last_x.at[b], to_y),
            sender.start(block.at[y, 1 - x, cut:], last_y.at[b], to_x),
        ]

    def plane_of(b):
        return half * PLANES + order[b // 2]

    def inward(b, source_plane):
        step = -1 if source_plane > plane_of(b) else 1
        me = lax.axis_index("dp")
        side = 0 if step < 0 else 1
        return pltpu.make_async_remote_copy(
            src_ref=blocks.at[b, y, x],
            dst_ref=from_planes.at[b, side],
            send_sem=plane_send.at[b],
            recv_sem=plane_recv.at[b, side],
            device_id=((source_plane + step) * 4 + me % 4, at["part"]),
            device_id_type=MESH,
        )

    def third(b, copies):
        arrived(copies)
        block = blocks.at[b]
        block[y, x, :cut] = plus(block[y, x, :cut], last_x[b]).astype(BF16)
        block[y, x, cut:] = plus(block[y, x, cut:], last_y[b]).astype(BF16)
        for end in (0, 3):
            if end != plane_of(b):

                @pl.when(z == end)
                def _(end=end):
                    inward(b, end).start()

    def hop(b, distance):
        for plane, side in ((3 - distance, 0), (distance, 1)):
            outside = plane > plane_of(b) if side == 0 else plane < plane_of(b)
            if outside:

                @pl.when(z == plane)
                def _(plane=plane, side=side):
                    inward(b, plane + 1 if side == 0 else plane - 1).wait_recv()
                    blocks[b, y, x] = plus(blocks[b, y, x], from_planes[b, side]).astype(BF16)
                    inward(b, plane).start()

    def final(b):
        plane = plane_of(b)

        @pl.when(z == plane)
        def _():
            got = []
            for side, exists in ((0, plane < 3), (1, plane > 0)):
                if exists:
                    inward(b, plane + 1 if side == 0 else plane - 1).wait_recv()
                    got.append(from_planes[b, side])
            share_ref[b % 2] = plus(blocks[b, y, x], *got)

    def finish_send(b):
        for plane in range(4):
            if plane != plane_of(b):

                @pl.when(z == plane)
                def _(plane=plane):
                    inward(b, plane).wait_send()

    up_copies = []

    def up_block(plane):
        weight_block(2, plane, up_blocks.at[plane])
        block = up_blocks.at[plane]
        to = half * PLANES + plane
        for i, (source, target) in enumerate(
            (
                (block.at[:, x, :cut], keep_x_hbm),
                (block.at[:, 1 - x, :cut], give_x_hbm),
                (block.at[y, :, cut:], keep_y_hbm),
                (block.at[1 - y, :, cut:], give_y_hbm),
            )
        ):
            copy = pltpu.make_async_copy(source, target.at[to], up_sems.at[plane, i])
            copy.start()
            up_copies.append(copy)

    def project_into(slot, side, pairs):
        width = D // 4

        def step(block, carry):
            span = pl.ds(pl.multiple_of(block * width, 16), width)
            total = dot(weight[pairs[0][0], span], hidden[pairs[0][1], side], NN)
            for which, matrix in pairs[1:]:
                total = total + dot(weight[which, span], hidden[matrix, side], NN)
            staged[slot, span] = total.astype(BF16)
            return carry

        lax.fori_loop(0, 4, step, 0)

    ahead_size = 512
    tiles = ((0, ahead_size), (ahead_size, units - ahead_size))
    if half:
        tiles = ((units - ahead_size, ahead_size), (0, units - ahead_size))
    for copy in loads[:5]:
        copy.wait()
    activate(0, *tiles[0])
    loads[5].wait()
    exchange.wait_recv()
    activate(1, *tiles[0])
    flying = {}
    weight_block(0, order[0], blocks.at[0])
    flying[0] = first(0)
    weight_block(1, order[0], blocks.at[1])
    flying[1] = first(1)
    activate(0, *tiles[1])
    flying[0] = second(0, flying[0])
    activate(1, *tiles[1])
    weight_block(0, order[1], blocks.at[2])
    flying[1] = second(1, flying[1])
    flying[2] = first(2)
    third(0, flying[0])
    weight_block(1, order[1], blocks.at[3])
    flying[3] = first(3)
    third(1, flying[1])
    up_block(0)
    hop(0, 1)
    flying[2] = second(2, flying[2])
    up_block(1)
    hop(1, 1)
    hop(0, 2)
    back = ((0, 1), (1, 2))
    ahead = ((2, 0),)
    project_into(0, 1, back)
    sent = [sender.start(staged.at[0], grad_came_hbm, to_core)]
    flying[3] = second(3, flying[3])
    hop(1, 2)
    third(2, flying[2])
    project_into(1, 1, ahead)
    sent.append(sender.start(staged.at[1], mixed_came_hbm, to_core))
    hop(2, 1)
    final(0)
    sent[0].wait_send()
    project_into(0, 0, back)
    store_one = pltpu.make_async_copy(staged.at[0], grad_own_hbm, store_sems.at[0])
    store_one.start()
    third(3, flying[3])
    hop(2, 2)
    final(1)
    sent[1].wait_send()
    project_into(1, 0, ahead)
    store_two = pltpu.make_async_copy(staged.at[1], mixed_own_hbm, store_sems.at[1])
    store_two.start()
    hop(3, 1)
    final(2)
    hop(3, 2)
    final(3)
    for b in range(4):
        finish_send(b)
    for copy in sent:
        copy.wait_recv()
    for copy in sender.made:
        if all(copy is not other for other in sent):
            copy.wait_send()
    for copy in up_copies + [store_one, store_two]:
        copy.wait()


def feed(half, cut, w_gate, w_up, w_down, normed, cot_own, cot_peer, pieces):
    units = w_gate.shape[1] // 2
    share = units // PLANES // 4
    rest = share - cut
    hbm = line(D, BF16)

    def hold(*dims, dtype=BF16):
        return pltpu.VMEM(dims, dtype)

    def piece(rows):
        return jax.ShapeDtypeStruct((4, 2, rows, D), BF16)

    inputs = 6 + len(pieces)
    copies = 24
    return pl.pallas_call(
        functools.partial(feed_kernel, half, cut),
        name="feed_forward",
        in_specs=[ANY] * inputs,
        out_specs=[ANY] * 8 + [VMEM],
        out_shape=[
            hbm, hbm, hbm, hbm, piece(cut), piece(cut), piece(rest), piece(rest),
            jax.ShapeDtypeStruct((2, share, D), F32),
        ],
        input_output_aliases={6 + i: 4 + i for i in range(len(pieces))},
        scratch_shapes=[
            hold(3, D, units), hold(2, D, LMAX), hold(2, D, LMAX), hold(3, 2, units, LMAX),
            hold(2, D, LMAX), hold(4, 2, 2, share, D), hold(2, 2, 2, share, D),
            hold(4, 2, cut, D), hold(4, 2, rest, D), hold(4, cut, D), hold(4, rest, D),
            hold(4, 2, share, D),
            pltpu.SemaphoreType.DMA((6,)),
            pltpu.SemaphoreType.DMA((2,)),
            pltpu.SemaphoreType.DMA((2, 4)),
            pltpu.SemaphoreType.DMA((copies,)),
            pltpu.SemaphoreType.DMA((copies,)),
            pltpu.SemaphoreType.DMA((4,)),
            pltpu.SemaphoreType.DMA((4, 2)),
        ],
        cost_estimate=pl.CostEstimate(
            flops=18 * 2 * D * LMAX * units, bytes_accessed=60 << 20, transcendentals=0
        ),
        compiler_params=pltpu.CompilerParams(
            vmem_limit_bytes=63 << 20, collective_id=2 + half, has_side_effects=True
        ),
    )(w_gate, w_up, w_down, normed, cot_own, cot_peer, *pieces)


def after_feed_kernel(
    own_one, own_two, came_one, came_two, mid_ref, cot_ref, columns_ref, scale_ref, weight_ref,
    grad_mid_ref, grad_attn_ref, attended_ref, sums_ref,
):
    grad = plus(own_one[...], own_two[...], came_one[...], came_two[...])
    mid, scale = mid_ref[...], scale_ref[...]
    weighted = grad * columns_ref[:, 1:2]
    inner = jnp.sum(weighted * mid, axis=0, keepdims=True)
    grad_mid = (
        cot_ref[...].astype(F32) + scale * weighted - mid * (scale * scale * scale * inner / D)
    )
    grad_mid_ref[...] = grad_mid
    grad_attn = grad_mid.astype(BF16)
    grad_attn_ref[...] = grad_attn
    attended_ref[...] = dot(weight_ref[...], grad_attn, NN).astype(BF16)

    @pl.when(pl.program_id(0) == 0)
    def _():
        sums_ref[...] = jnp.zeros_like(sums_ref)

    sums_ref[...] += folded(grad * (mid * scale))


def after_feed(parts, mid, cot, columns, scale, w_out):
    inner = w_out.shape[0]
    return call(
        after_feed_kernel,
        "norm_back",
        2 * D * LMAX * inner,
        D * LMAX * 26,
        48,
        grid=(LMAX // QBLOCK,),
        in_specs=[ROWS] * 6 + [COLUMN, LINE, whole_spec(w_out)],
        out_specs=[ROWS, ROWS, pl.BlockSpec((inner, QBLOCK), lambda i: (0, i)), SUMS],
        out_shape=[
            line(D), line(D, BF16), line(inner, BF16), jax.ShapeDtypeStruct((D, 128), F32),
        ],
    )(*parts, mid, cot, columns, scale, w_out)


STRIP = LMAX + LMAX - TILE


def offsets(shift):
    keys = lax.broadcasted_iota(jnp.int32, (TILE, TILE), 0)
    queries = lax.broadcasted_iota(jnp.int32, (TILE, TILE), 1)
    return shift * TILE + keys - queries


def strip_kernel(table_ref, strip_ref):
    head = pl.program_id(0)
    middle = LMAX - TILE

    def value(bucket):
        return table_ref[bucket, head]

    def side(distance, base, start):
        tile = jnp.full((TILE, TILE), start, F32)
        for count, step in enumerate(NEAR_STEPS):
            tile = jnp.where(distance >= step, value(base + count + 1), tile)
        return tile

    strip_ref[0, : middle - TILE, :] = jnp.full((middle - TILE, TILE), value(15), F32)
    strip_ref[0, middle + 2 * TILE :, :] = jnp.full((STRIP - middle - 2 * TILE, TILE), value(31), F32)
    before = offsets(-1)
    strip_ref[0, middle - TILE : middle, :] = side(-before, 0, value(0))
    relative = offsets(0)
    strip_ref[0, middle : middle + TILE, :] = jnp.where(
        relative > 0, side(relative, 16, value(0)), side(-relative, 0, value(0))
    )
    after = offsets(1)
    strip_ref[0, middle + TILE : middle + 2 * TILE, :] = side(after, 16, value(0))


def bias_strip(table, heads):
    return call(
        strip_kernel,
        "bias_strip",
        heads * 3e6,
        heads * STRIP * TILE * 4,
        8,
        grid=(heads,),
        in_specs=[SMEM],
        out_specs=pl.BlockSpec((1, STRIP, TILE), lambda h: (h, 0, 0)),
        out_shape=jax.ShapeDtypeStruct((heads, STRIP, TILE), F32),
    )(table)


def attend_kernel(
    part_ref, q_ref, k_ref, v_ref, gate_ref, strip_ref, own_ref, peer_ref, came_own_ref, came_peer_ref,
    prob_ref, out_ref, wide_ref, cot_own_ref, cot_peer_ref, hold, sems,
):
    head = pl.program_id(0)
    part = part_ref[0]
    copies_in, copies_out = halves(part, own_ref, came_own_ref, cot_own_ref, hold.at[0], sems.at[0])
    ins, outs = halves(part, peer_ref, came_peer_ref, cot_peer_ref, hold.at[1], sems.at[1])
    copies_in, copies_out = copies_in + ins, copies_out + outs

    @pl.when(head == 0)
    def _():
        for copy in copies_in:
            copy.start()

    @pl.when(head == 2)
    def _():
        for copy, following in zip(copies_in, copies_out):
            copy.wait()
            following.start()

    ones = (lax.broadcasted_iota(jnp.int32, (AUG, LMAX), 0) == 0).astype(F32).astype(BF16)
    scale = HDIM ** (-0.5)
    queries = jnp.concatenate([(q_ref[...].astype(F32) * scale).astype(BF16), ones], axis=0)
    keys = jnp.concatenate([k_ref[...], gate_ref[...]], axis=0)
    for block in range(LMAX // ABLOCK):
        low = block * ABLOCK
        scores = dot(keys, queries[:, low : low + ABLOCK], TN)
        bias = []
        for sub in range(ABLOCK // TILE):
            start = LMAX - TILE - (low + sub * TILE)
            bias.append(strip_ref[0, start : start + LMAX, :])
        scores = scores + jnp.concatenate(bias, axis=1)
        top = jnp.max(scores, axis=0, keepdims=True)
        weights = jnp.exp(scores - top)
        total = jnp.sum(weights, axis=0, keepdims=True)
        prob = (weights * (1.0 / total)).astype(BF16)
        prob_ref[0, :, low : low + ABLOCK] = prob
        out = dot(v_ref[...], prob, NN)
        wide_ref[:, low : low + ABLOCK] = out
        out_ref[:, low : low + ABLOCK] = out.astype(BF16)

    @pl.when(head == pl.num_programs(0) - 1)
    def _():
        for copy in copies_out:
            copy.wait()


def attend(part, qkv, gate, strip, own, peer, came_own, came_peer, heads):
    return call(
        attend_kernel,
        "attend",
        heads * 4 * LMAX * LMAX * HDIM * 4,
        heads * LMAX * LMAX * 2,
        48,
        grid=(heads,),
        in_specs=[
            SMEM,
            pl.BlockSpec((HDIM, LMAX), lambda h: (h, 0)),
            pl.BlockSpec((HDIM, LMAX), lambda h: (heads + h, 0)),
            pl.BlockSpec((HDIM, LMAX), lambda h: (2 * heads + h, 0)),
            pl.BlockSpec((AUG, LMAX), lambda h: (0, 0)),
            pl.BlockSpec((1, STRIP, TILE), lambda h: (h, 0, 0)),
            ANY, ANY, ANY, ANY,
        ],
        out_specs=[
            pl.BlockSpec((1, LMAX, LMAX), lambda h: (h, 0, 0)),
            pl.BlockSpec((HDIM, LMAX), lambda h: (h, 0)),
            pl.BlockSpec((HDIM, LMAX), lambda h: (h, 0)),
            ANY, ANY,
        ],
        out_shape=[
            jax.ShapeDtypeStruct((heads, LMAX, LMAX), BF16),
            jax.ShapeDtypeStruct((heads * HDIM, LMAX), BF16),
            jax.ShapeDtypeStruct((heads * HDIM, LMAX), F32),
            line(D, BF16), line(D, BF16),
        ],
        scratch_shapes=[
            pltpu.VMEM((2, 2, D // 2, LMAX), BF16), pltpu.SemaphoreType.DMA((2, 2, 2))
        ],
    )(part, qkv, qkv, qkv, gate, strip, own, peer, came_own, came_peer)


def attend_back_kernel(
    q_ref, k_ref, v_ref, prob_ref, go_ref, wide_ref, gq_ref, gk_ref, gv_ref, sums_ref, near_ref
):
    scale = HDIM ** (-0.5)
    blocks = LMAX // TILE
    member = (
        lax.broadcasted_iota(jnp.int32, (AUG, LMAX), 0)
        == lax.broadcasted_iota(jnp.int32, (AUG, LMAX), 1) // TILE
    )
    queries = jnp.concatenate([q_ref[...], member.astype(F32).astype(BF16)], axis=0)
    near = [jnp.zeros((TILE, TILE), F32) for _ in range(3)]
    key_total = jnp.zeros((HDIM + AUG, LMAX), F32)
    val_total = jnp.zeros((HDIM, LMAX), F32)
    for block in range(LMAX // ABLOCK):
        low = block * ABLOCK
        prob = prob_ref[0, :, low : low + ABLOCK]
        grad_out = go_ref[:, low : low + ABLOCK]
        soft = prob.astype(F32)
        grad_prob = dot(v_ref[...], grad_out, TN)
        wide = wide_ref[:, low : low + ABLOCK]
        inner = jnp.sum(grad_out.astype(F32) * wide, axis=0, keepdims=True)
        grad_scores = (soft * (grad_prob - inner)).astype(BF16)
        gq_ref[:, low : low + ABLOCK] = (dot(k_ref[...], grad_scores, NN) * scale).astype(BF16)
        key_total = key_total + dot(queries[:, low : low + ABLOCK], grad_scores, NT)
        val_total = val_total + dot(grad_out, prob, NT)
        for sub in range(ABLOCK // TILE):
            place = block * (ABLOCK // TILE) + sub
            for shift in (-1, 0, 1):
                at = place + shift
                if 0 <= at < blocks:
                    piece = grad_scores[at * TILE : (at + 1) * TILE, sub * TILE : (sub + 1) * TILE]
                    near[shift + 1] = near[shift + 1] + piece.astype(F32)
    gk_ref[...] = (key_total[:HDIM] * scale).astype(BF16)
    gv_ref[...] = val_total.astype(BF16)
    sums = key_total[HDIM : HDIM + blocks]
    sums_ref[0] = sums
    shifts = (
        lax.broadcasted_iota(jnp.int32, (blocks, LMAX), 1) // TILE
        - lax.broadcasted_iota(jnp.int32, (blocks, LMAX), 0)
    )

    def fold(tile):
        return jnp.sum(tile, axis=0, keepdims=True)

    def far(chosen):
        return folded(fold(jnp.where(chosen, sums, 0.0)))

    before, same, after = near
    for sign, base, other, shift in ((-1, 0, before, -1), (1, 16, after, 1)):
        near_offset = sign * offsets(0)
        far_offset = sign * offsets(shift)
        floor = 0 if sign < 0 else 1
        last = fold(jnp.where(near_offset >= floor, same, 0.0)) + fold(
            jnp.where(far_offset >= floor, other, 0.0)
        )
        for count, step in enumerate(NEAR_STEPS):
            following = fold(jnp.where(near_offset >= step, same, 0.0)) + fold(
                jnp.where(far_offset >= step, other, 0.0)
            )
            near_ref[0, base + count : base + count + 1] = last - following
            last = following
        near_ref[0, base + 15 : base + 16] = last + far(sign * shifts >= 2)


def attend_back(side, qkv, prob, grad_attended, wide, heads):
    blocks = LMAX // TILE
    rows = jax.ShapeDtypeStruct((heads * HDIM, LMAX), BF16)
    spec = pl.BlockSpec((HDIM, LMAX), lambda h: (h, 0))
    return call(
        attend_back_kernel,
        "attend_back",
        heads * 8 * LMAX * LMAX * HDIM * 4,
        heads * LMAX * LMAX * 2,
        48,
        side=side,
        grid=(heads,),
        in_specs=[
            spec,
            pl.BlockSpec((HDIM, LMAX), lambda h: (heads + h, 0)),
            pl.BlockSpec((HDIM, LMAX), lambda h: (2 * heads + h, 0)),
            pl.BlockSpec((1, LMAX, LMAX), lambda h: (h, 0, 0)),
            spec,
            spec,
        ],
        out_specs=[
            spec,
            spec,
            spec,
            pl.BlockSpec((1, blocks, LMAX), lambda h: (h, 0, 0)),
            pl.BlockSpec((1, BUCKETS, TILE), lambda h: (h, 0, 0)),
        ],
        out_shape=[
            rows,
            rows,
            rows,
            jax.ShapeDtypeStruct((heads, blocks, LMAX), F32),
            jax.ShapeDtypeStruct((heads, BUCKETS, TILE), F32),
        ],
    )(qkv, qkv, qkv, prob, grad_attended, wide)


def ffn_kernel(gate_ref, up_ref, down_ref, x_ref, cot_ref, hid_ref, gg_ref, gu_ref):
    gate = dot(gate_ref[...], x_ref[...], TN)
    up = dot(up_ref[...], x_ref[...], TN)
    grad = dot(down_ref[...], cot_ref[...], TN)
    square = gate * gate
    bend = jnp.tanh(GELU_C * gate * (1.0 + 0.044715 * square))
    half = 0.5 * (1.0 + bend)
    gelu = gate * half
    slope = half + 0.5 * gate * (1.0 - bend * bend) * (GELU_C * (1.0 + 3 * 0.044715 * square))
    hid_ref[...] = (gelu * up).astype(BF16)
    gg_ref[...] = (grad * up * slope).astype(BF16)
    gu_ref[...] = (grad * gelu).astype(BF16)


def ffn(w_gate, w_up, w_down_t, normed, cot):
    units = w_gate.shape[1]
    width = 256
    weight = pl.BlockSpec((D, width), lambda i: (0, i))
    whole = fixed_spec((D, LMAX))
    out = pl.BlockSpec((width, LMAX), lambda i: (i, 0))
    shape = jax.ShapeDtypeStruct((units, LMAX), BF16)
    return call(
        ffn_kernel,
        "ffn",
        6 * D * units * LMAX,
        3 * D * units * 2 + 2 * D * LMAX * 2 + 3 * units * LMAX * 2,
        48,
        grid=(units // width,),
        in_specs=[weight, weight, weight, whole, whole],
        out_specs=[out, out, out],
        out_shape=[shape, shape, shape],
    )(w_gate, w_up, w_down_t, normed, cot)


def weight_grad_kernel(a_own, a_peer, b_own, b_peer, out_ref):
    total = dot(a_own[...], b_own[...], NT) + dot(a_peer[...], b_peer[...], NT)
    out_ref[...] = total.astype(BF16)


def weight_grad(a_own, a_peer, b_own, b_peer):
    units = a_own.shape[0]
    width = 256
    left = pl.BlockSpec((width, LMAX), lambda i: (i, 0))
    whole = fixed_spec((D, LMAX))
    return call(
        weight_grad_kernel,
        "weight_grad",
        4 * D * units * LMAX,
        4 * D * LMAX + 4 * units * LMAX + 2 * units * D,
        48,
        grid=(units // width,),
        in_specs=[left, left, whole, whole],
        out_specs=pl.BlockSpec((width, D), lambda i: (i, 0)),
        out_shape=jax.ShapeDtypeStruct((units, D), BF16),
    )(a_own, a_peer, b_own, b_peer)


def project_kernel(count, *refs):
    total = dot(refs[0][...], refs[count][...], NN)
    for i in range(1, count):
        total = total + dot(refs[i][...], refs[count + i][...], NN)
    refs[-1][...] = total.astype(refs[-1].dtype)


def project(side, weights, values, dtype):
    count = len(weights)
    units = weights[0].shape[1]
    width = D // 4
    weight = pl.BlockSpec((width, units), lambda i: (i, 0))
    whole = fixed_spec((units, LMAX))
    return call(
        functools.partial(project_kernel, count),
        "project",
        2 * count * D * units * LMAX,
        2 * count * (D * units + units * LMAX) + 4 * D * LMAX,
        48,
        side=side,
        grid=(D // width,),
        in_specs=[weight] * count + [whole] * count,
        out_specs=pl.BlockSpec((width, LMAX), lambda i: (i, 0)),
        out_shape=jax.ShapeDtypeStruct((D, LMAX), dtype),
    )(*weights, *values)


def fold_kernel(bit_ref, keep_ref, came_ref, keep_out, give_out):
    mine = bit_ref[0]
    for out, which in ((keep_out, mine), (give_out, 1 - mine)):
        total = keep_ref[:, which].astype(F32) + came_ref[:, which].astype(F32)
        out[...] = total.astype(BF16)


def fold(bit, keep, came):
    outer, _, rows, width = keep.shape
    steps = 2 if outer % 2 == 0 else 1
    block = pl.BlockSpec((outer // steps, 2, rows, width), lambda i: (i, 0, 0, 0))
    out = pl.BlockSpec((outer // steps, rows, width), lambda i: (i, 0, 0))
    shape = jax.ShapeDtypeStruct((outer, rows, width), BF16)
    return call(
        fold_kernel,
        "fold",
        4 * keep.size,
        6 * keep.size,
        48,
        grid=(steps,),
        in_specs=[SMEM, block, block],
        out_specs=[out, out],
        out_shape=[shape, shape],
    )(bit.reshape(1), keep, came)


def across(values, bit):
    size = lax.axis_size("dp")
    return lax.ppermute(values, "dp", [(i, i ^ (1 << bit)) for i in range(size)])


def bit_of(bit):
    return (lax.axis_index("dp") >> bit) & 1


def stacked(values, came, mine, axis):
    return jnp.where(mine == 0, jnp.stack([values, came], axis), jnp.stack([came, values], axis))


def sum_everywhere(keep, came):
    bits = lax.axis_size("dp").bit_length() - 1
    rows = keep.shape[1] // 4
    keep, came = (v.reshape(4, 2, 2, rows, D) for v in (keep, came))
    keep_x, give_x = fold(
        bit_of(0), keep[:2].reshape(4, 2, rows, D), came[:2].reshape(4, 2, rows, D)
    )
    keep_y, give_y = fold(
        bit_of(1), keep[2:].reshape(2, 2, 2 * rows, D), came[2:].reshape(2, 2, 2 * rows, D)
    )
    came_x, came_y = across(give_x, 0), across(give_y, 1)
    keep_x, give_x = fold(
        bit_of(1), keep_x.reshape(2, 2, rows, D), came_x.reshape(2, 2, rows, D)
    )
    keep_y, give_y = fold(
        bit_of(0), keep_y.reshape(2, 2, rows, D), came_y.reshape(2, 2, rows, D)
    )
    came_x, came_y = across(give_x, 1), across(give_y, 0)
    keep = jnp.concatenate([keep_x, keep_y], axis=0).reshape(2, 2, rows, D)
    came = jnp.concatenate([came_x, came_y], axis=0).reshape(2, 2, rows, D)
    keep, give = fold(bit_of(2), keep, came)
    came = across(give, 2)
    keep, give = fold(bit_of(3), keep.reshape(1, 2, rows, D), came.reshape(1, 2, rows, D))
    came = across(give, 3)
    total = (keep.astype(F32) + came.astype(F32)).astype(BF16)
    for bit in range(4, bits):
        total = (total.astype(F32) + across(total, bit).astype(F32)).astype(BF16)
    total = stacked(total, across(total, 3), bit_of(3), 1)
    total = stacked(total, across(total, 2), bit_of(2), 2).reshape(4, rows, D)
    total_x, total_y = total[:2], total[2:]
    total_x = stacked(total_x, across(total_x, 1), bit_of(1), 1)
    total_y = stacked(total_y, across(total_y, 0), bit_of(0), 1)
    total_x = stacked(total_x, across(total_x, 0), bit_of(0), 2)
    total_y = stacked(total_y, across(total_y, 1), bit_of(1), 1)
    return [v.reshape(4 * rows, D).astype(F32) for v in (*total_x, *total_y)]


def sum_small(values):
    bits = lax.axis_size("dp").bit_length() - 1
    values = values + swap(values)
    for bit in range(bits):
        values = values + across(values, bit)
    return values


def halve(values, order):
    size = lax.axis_size("dp")
    bits = size.bit_length() - 1
    index = lax.axis_index("dp")
    rows = values.shape[0] // size
    values = values.reshape((2,) * bits + (rows, values.shape[1]))
    left = list(range(bits - 1, -1, -1))
    for step, bit in enumerate(order):
        axis = left.index(bit)
        left.pop(axis)
        mine = (index >> bit) & 1
        keep = lax.dynamic_index_in_dim(values, mine, axis, keepdims=False)
        give = lax.dynamic_index_in_dim(values, 1 - mine, axis, keepdims=False)
        came = lax.ppermute(give, "dp", [(i, i ^ (1 << bit)) for i in range(size)])
        total = keep.astype(F32) + came.astype(F32)
        values = total if step == bits - 1 else total.astype(BF16)
    return values


def swap(values):
    return lax.ppermute(values, "mp", [(0, 1), (1, 0)])


def body(
    tokens,
    cotangent,
    lengths,
    keep_mask,
    ln_attn,
    w_query,
    w_key,
    w_value,
    w_attn_out,
    rel_table,
    w_delete,
    ln_ffn,
    w_gate,
    w_up,
    w_ffn_out,
):
    dev_count = lax.axis_size("dp")
    bits = dev_count.bit_length() - 1
    part = lax.axis_index("mp")
    inner = 2 * w_query.shape[1]
    heads = inner // HDIM
    half = tokens.shape[1]
    first = part == 0
    part_ref = part.reshape(1).astype(jnp.int32)

    def in_parts(own, peer, axis):
        return jnp.where(
            first, jnp.concatenate([own, peer], axis), jnp.concatenate([peer, own], axis)
        )

    def home(values):
        mine = lax.dynamic_slice_in_dim(values, part * half, half, 0)
        other = lax.dynamic_slice_in_dim(values, (1 - part) * half, half, 0)
        return spread(part_ref, slot, mine, swap(other)).T

    own_weights = (w_query.T, w_key.T, w_value.T, w_attn_out)
    slot, count, stack = places(part_ref, lengths, keep_mask.reshape(1, ROWS_DEV), own_weights)
    came_stack = swap(stack)
    own_tokens, peer_tokens = compact(part_ref, slot, tokens.T)
    came_tokens = swap(peer_tokens)
    own_cot, peer_cot, w_qkv, w_out = compact_join(
        part_ref, slot, cotangent.T, stack, came_stack
    )
    came_cot_own, came_cot_peer = swap(peer_cot), swap(own_cot)
    table = in_parts(rel_table, swap(rel_table), 1)
    strip = bias_strip(table, heads)
    columns = jnp.stack([ln_attn, ln_ffn, w_delete.astype(F32)], axis=1)

    state, normed_one, qkv, gate_rows, del_logit, scale_one = input_part(
        part_ref, own_tokens, came_tokens, columns, w_qkv, count
    )
    prob, attended, wide, cot_own, cot_peer = attend(
        part_ref, qkv, gate_rows, strip, own_cot, peer_cot, came_cot_own, came_cot_peer, heads
    )
    mid, normed_two, scale_two = middle_part(w_out, attended, state, columns)
    w_down_t = w_ffn_out.T
    share = w_gate.shape[1] // dev_count
    if bits == 4 and share % 16 == 0:
        cut = (share // 2 + 15) // 16 * 16
        one = feed(0, cut, w_gate, w_up, w_down_t, normed_two, cot_own, cot_peer, ())
        two = feed(1, cut, w_gate, w_up, w_down_t, normed_two, cot_own, cot_peer, one[4:8])
        keep_x, give_x, keep_y, give_y = two[4:8]
        up_x = (keep_x, across(give_x, 0))
        up_y = (keep_y, across(give_y, 1))
        grad_mid, grad_attn, grad_attended, sum_ffn = after_feed(
            (one[0], two[0], one[1], two[1]), mid, cot_own, columns, scale_two, w_out
        )
        grad_q, grad_k, grad_v, sums, near = attend_back(
            (), qkv, prob, grad_attended, wide, heads
        )
        up_x, up_y, grad_q = lax.optimization_barrier((up_x, up_y, grad_q))
        keep_x, give_x = fold(bit_of(1), *up_x)
        keep_y, give_y = fold(bit_of(0), *up_y)
        up_x = (keep_x, across(give_x, 1))
        up_y = (keep_y, across(give_y, 0))
        keep, give = head_grads(part_ref, grad_q, grad_k, grad_v, normed_one, attended, grad_attn)
        totals, grad_up, small, state_own, state_came, mixed_own, mixed_came = tail(
            keep, give, up_x, up_y, sum_ffn, near.reshape(heads * BUCKETS, TILE),
            (scale_one, del_logit, sums, columns),
            (
                grad_q, grad_k, grad_v, normed_one, state, grad_mid, one[2], two[2], one[3], two[3],
                mid, w_qkv,
            ),
        )
        mixed = spread(part_ref, slot, mixed_own, mixed_came).T
        total_q, total_v, total_k, total_out = totals.reshape(4, inner // 2, D).astype(F32)
        grad_tokens = spread(part_ref, slot, state_own, state_came).T
        grad_ln_ffn, grad_ln_attn, grad_w_delete = small[0], small[1], small[2]
        grad_table = small[3, : heads * BUCKETS].reshape(heads, BUCKETS).T
        grad_down, grad_gate = jnp.where(bit_of(3) == 0, one[8], two[8])
    else:
        normed_two_peer = swap(normed_two)
        hid_own, gg_own, gu_own = ffn(w_gate, w_up, w_down_t, normed_two, cot_own)
        hid_peer, gg_peer, gu_peer = ffn(w_gate, w_up, w_down_t, normed_two_peer, cot_peer)
        order = tuple(range(bits))
        grad_down = halve(weight_grad(hid_own, hid_peer, cot_own, cot_peer), order)
        grad_gate = halve(weight_grad(gg_own, gg_peer, normed_two, normed_two_peer), order)
        grad_up = halve(weight_grad(gu_own, gu_peer, normed_two, normed_two_peer), order)
        back_peer = project((), (w_gate, w_up), (gg_peer, gu_peer), BF16)
        grad_mid, grad_attn, grad_attended, sum_ffn = middle_back(
            w_gate, w_up, gg_own, gu_own, swap(back_peer), mid, cot_own, columns, scale_two, w_out
        )
        grad_q, grad_k, grad_v, sums, near = attend_back(
            (), qkv, prob, grad_attended, wide, heads
        )
        keep, give = head_grads(part_ref, grad_q, grad_k, grad_v, normed_one, attended, grad_attn)
        total_q, total_v, total_k, total_out = sum_everywhere(keep, swap(give))
        grad_state, sum_attn, sum_delete = input_back(
            (), grad_q, grad_k, grad_v, w_qkv, normed_one, state, grad_mid, scale_one, del_logit,
            sums, columns,
        )
        grad_tokens = home(grad_state)
        grad_table = jnp.sum(near, axis=2).T
        small = jnp.concatenate(
            [jnp.sum(v, axis=1) for v in (sum_ffn, sum_attn, sum_delete)]
            + [grad_table.reshape(-1)]
        )
        small = sum_small(small)
        grad_ln_ffn, grad_ln_attn = small[:D], small[D : 2 * D]
        grad_w_delete = small[2 * D : 3 * D]
        grad_table = small[3 * D :].reshape(BUCKETS, heads)
        mixed_peer = project((), (w_down_t,), (hid_peer,), BF16)
        mixed = home(mixed_part(w_down_t, hid_own, swap(mixed_peer), mid))

    def own_half(values):
        return lax.dynamic_slice_in_dim(values, part * half, half, 0)

    return (
        mixed,
        grad_tokens,
        own_half(grad_ln_attn),
        total_q.T,
        total_k.T,
        total_v.T,
        total_out,
        lax.dynamic_slice_in_dim(grad_table, part * (heads // 2), heads // 2, 1),
        grad_w_delete,
        own_half(grad_ln_ffn),
        grad_gate.T,
        grad_up.T,
        grad_down,
    )


def solution(mesh):
    return jax.shard_map(
        body,
        mesh=mesh,
        in_specs=(
            P("dp", "mp"),
            P("dp", "mp"),
            P("dp"),
            P("dp"),
            P(),
            P(None, "mp"),
            P(None, "mp"),
            P(None, "mp"),
            P("mp", None),
            P(None, "mp"),
            P(),
            P(),
            P(None, "mp"),
            P(None, "mp"),
            P("mp", None),
        ),
        out_specs=(
            P("dp", "mp"),
            P("dp", "mp"),
            P("mp"),
            P(None, "mp"),
            P(None, "mp"),
            P(None, "mp"),
            P("mp", None),
            P(None, "mp"),
            P(),
            P("mp"),
            P(None, ("mp", "dp")),
            P(None, ("mp", "dp")),
            P(("mp", "dp"), None),
        ),
        check_vma=False,
    )
```
